32 devices in a mesh: group: 8 (over y, x, core), expert: 4 (over z).
Axes of the slice: x: 2, y: 2, z: 4, core: 2. Of those that a mesh axis runs over, the one named last changes fastest.
Arguments:
- inputs: bfloat16 [8192, 1024], P(('group', 'expert')), may hold values from -6 to 6
- gain_one: float32 [1024], replicated, may hold values from 0.5 to 1.5
- query_matrix: bfloat16 [1024, 1024], replicated, may hold values from -0.1875 to 0.1875
- key_matrix: bfloat16 [1024, 512], replicated, may hold values from -0.1875 to 0.1875
- value_matrix: bfloat16 [1024, 512], replicated, may hold values from -0.1875 to 0.1875
- w_attn_out: bfloat16 [1024, 1024], replicated, may hold values from -0.75 to 0.75
- gain_two: float32 [1024], replicated, may hold values from 0.5 to 1.5
- w_router: bfloat16 [1024, 16], replicated, may hold values from -0.09375 to 0.09375
- expert_in: bfloat16 [16, 1024, 1024], P('expert'), may hold values from -0.1875 to 0.1875
- expert_out: bfloat16 [16, 512, 1024], P('expert'), may hold values from -0.75 to 0.75
- lengths: int32 [32], P(('group', 'expert')), may hold values from 85 to 256, as said below
- routes: int32 [8192, 8], P(('group', 'expert')), may hold values from 0 to 15, all different within a row
- ranks: int32 [8192, 8], P(('group', 'expert')), may hold values from 0 to 2047, as said below
- cotangent: bfloat16 [8192, 1024], P(('group', 'expert')), may hold values from -6 to 6
Outputs:
- output: float32 [8192, 1024], P(('group', 'expert'))
- grad_inputs: float32 [8192, 1024], P(('group', 'expert'))
- grad_gain_one: float32 [1024], P('group')
- grad_w_query: float32 [1024, 1024], P('group')
- grad_w_key: float32 [1024, 512], P('group')
- grad_w_value: float32 [1024, 512], P('group')
- grad_w_attn_out: float32 [1024, 1024], P('group')
- grad_gain_two: float32 [1024], P('group')
- grad_w_router: float32 [1024, 16], P('group')
- grad_expert_in: float32 [16, 1024, 1024], P('expert')
- grad_expert_out: float32 [16, 512, 1024], P('expert')
The draws below stay inside these ranges and needn't reach their ends.
Inputs may be any that keep to these rules, and one draw needn't show every extreme that they name: `lengths`: some slot holds exactly 256 tokens and some exactly 85. `routes`: each row names 8 different experts. `ranks`: the rows of one slot hold each of 0 to 2047 once.
All inputs are finite; a program needn't handle non-finite values.
Results may differ from the reference program's by a relative error of at most 0.012.
The reference program's roundings to bfloat16 on the way count: a program that leaves them out, or rounds other values in their place, can miss the bound.
Values may be sent and summed in bfloat16 or wider, within the bound.
No kernel may reach another device: no remote copies, remote signals or barrier semaphores. Data moves between devices by JAX's collectives and lax.ppermute only.
A program may use at most 192 MiB of HBM per device.

```python
import jax
import jax.numpy as jnp
from jax import lax

MODEL_DIMENSION = 1024
QUERY_HEADS = 16
KEY_VALUE_HEADS = 8
HEAD_DIMENSION = 64
FF = 512
TOPK = 8
SEQ_LEN = 256
EXPERTS = 16
SEQS = 32
TOKENS = 8192
MIN_LEN = 85
CAP = 160


def draw_lengths(key, part):
    key = jax.random.fold_in(key, 11)
    first_key, second_key = jax.random.split(key)
    drawn = jax.random.randint(first_key, (SEQS,), MIN_LEN, SEQ_LEN + 1)
    chosen = jax.random.permutation(second_key, SEQS)
    drawn = drawn.at[chosen[0]].set(SEQ_LEN).at[chosen[1]].set(MIN_LEN)
    return drawn.astype(jnp.int32)


def draw_ranks(key, part):
    key = jax.random.fold_in(key, 23)
    slot_keys = jax.random.split(key, SEQS)
    shuffled = jax.vmap(lambda single: jax.random.permutation(single, SEQ_LEN * TOPK))(slot_keys)
    return shuffled.reshape(SEQS * SEQ_LEN, TOPK).astype(jnp.int32)


def level_of(key, dims, pieces, smallest, high):
    factor_of = 1.0
    for axis_at, parts in pieces:
        steps = jax.random.uniform(jax.random.fold_in(jax.random.fold_in(key, 6), axis_at), (parts,), jnp.float32, smallest / len(pieces), high / len(pieces))
        factor_of = factor_of * jnp.repeat(jnp.exp(steps), dims[axis_at] // parts).reshape((-1,) + (1,) * (len(dims) - 1 - axis_at))
    return factor_of


def distinct(rng, rows, amount, top, lift):
    ranking = jax.random.permutation(jax.random.fold_in(rng, 1), amount)
    boost = ranking
    for power in range(3):
        boost = boost * boost // amount
    boost = boost * lift // amount
    lots = jax.random.randint(jax.random.fold_in(rng, 2), (rows, amount), 0, 4096) + boost
    holders = jax.random.permutation(jax.random.fold_in(rng, 3), rows)[jnp.arange(amount) % rows]
    lots = jnp.where(jnp.arange(rows)[:, None] == holders[None, :], 1 << 14, lots)
    priority = lots * amount + jnp.arange(amount)
    return lax.top_k(priority.astype(jnp.int32), top)[1].astype(jnp.int32)


def noise(key, dims, deviation, limit, pieces=(), kind=jnp.bfloat16):
    result = deviation * jax.random.normal(key, dims, jnp.float32)
    if pieces:
        result = result * level_of(key, dims, pieces, -0.22, 0.18)
    return jnp.clip(result, -limit, limit).astype(kind)


def setup_inputs(seed: int = 0) -> dict:
    splits = jax.random.split(jax.random.key(seed), 15)
    inputs = noise(splits[0], (TOKENS, MODEL_DIMENSION), 1.0, 6.0, ((0, 32),))
    gain_one = jnp.clip(1.0 + 0.1 * jax.random.normal(splits[1], (MODEL_DIMENSION,), jnp.float32), 0.5, 1.5)
    query_matrix = noise(splits[2], (MODEL_DIMENSION, QUERY_HEADS * HEAD_DIMENSION), MODEL_DIMENSION ** -0.5, 0.1875)
    key_matrix = noise(splits[3], (MODEL_DIMENSION, KEY_VALUE_HEADS * HEAD_DIMENSION), MODEL_DIMENSION ** -0.5, 0.1875)
    value_matrix = noise(splits[4], (MODEL_DIMENSION, KEY_VALUE_HEADS * HEAD_DIMENSION), MODEL_DIMENSION ** -0.5, 0.1875)
    w_attn_out = noise(splits[5], (QUERY_HEADS * HEAD_DIMENSION, MODEL_DIMENSION), (QUERY_HEADS * HEAD_DIMENSION * 16 // SEQ_LEN) ** -0.5, 0.75)
    gain_two = jnp.clip(1.0 + 0.1 * jax.random.normal(splits[6], (MODEL_DIMENSION,), jnp.float32), 0.5, 1.5)
    w_router = noise(splits[7], (MODEL_DIMENSION, EXPERTS), (4 * MODEL_DIMENSION) ** -0.5, 0.09375)
    expert_in = noise(splits[8], (EXPERTS, MODEL_DIMENSION, 2 * FF), MODEL_DIMENSION ** -0.5, 0.1875, ((0, 4),))
    expert_out = noise(splits[9], (EXPERTS, FF, MODEL_DIMENSION), (FF // 8) ** -0.5, 0.75, ((0, 4),))
    lengths = draw_lengths(jax.random.fold_in(splits[14], 71), 0)
    routes = distinct(splits[11], TOKENS, EXPERTS, TOPK, 4096)
    ranks = draw_ranks(jax.random.fold_in(splits[14], 71), 0)
    cotangent = noise(splits[13], (TOKENS, MODEL_DIMENSION), 1.0, 6.0, ((0, 32),))
    return {"inputs": inputs, "gain_one": gain_one, "query_matrix": query_matrix, "key_matrix": key_matrix, "value_matrix": value_matrix, "w_attn_out": w_attn_out, "gain_two": gain_two, "w_router": w_router, "expert_in": expert_in, "expert_out": expert_out, "lengths": lengths, "routes": routes, "ranks": ranks, "cotangent": cotangent}


@jax.custom_vjp
def reduced_precision(v):
    return lax.optimization_barrier(v.astype(jnp.bfloat16)).astype(jnp.float32)

@jax.custom_vjp
def reduced_backward(v):
    return v

def low_keep(v):
    return (reduced_precision(v), None)

def low_pass(kept, grad):
    return (grad,)

def back_keep(v):
    return (v, None)

def back_low(kept, grad):
    return (reduced_precision(grad),)
reduced_precision.defvjp(low_keep, low_pass)
reduced_backward.defvjp(back_keep, back_low)
EPS = 1e-05

def exact_matrix_product(left, right):
    return jnp.dot(left, right, precision=lax.Precision.HIGHEST)

def rms_scale(values, gain_vec):
    return values * lax.rsqrt(lax.optimization_barrier(jnp.mean(values * values, -1, keepdims=True)) + EPS) * gain_vec

def place_pairs(seq_length, route_rows, rank_rows):
    pair_total = route_rows.shape[0] * TOPK
    flat_route = route_rows.reshape(-1).astype(jnp.int32)
    flat_rank = rank_rows.reshape(-1).astype(jnp.int32)
    counter = jnp.arange(pair_total, dtype=jnp.int32)
    valid_pair = counter // TOPK < seq_length
    rank_order = jnp.zeros((pair_total,), jnp.int32).at[flat_rank].set(counter)
    ranked_route = flat_route[rank_order]
    ranked_valid = valid_pair[rank_order]
    hit_table = ((ranked_route[:, None] == jnp.arange(EXPERTS, dtype=jnp.int32)[None, :]) & ranked_valid[:, None]).astype(jnp.int32)
    earlier = jnp.cumsum(hit_table, 0) - hit_table
    ranked_place = lax.optimization_barrier(jnp.sum(earlier * hit_table, 1)).astype(jnp.int32)
    slot_place = ranked_place[flat_rank]
    kept_pair = valid_pair & (slot_place < CAP)
    slot_index = jnp.where(kept_pair, flat_route * CAP + slot_place, EXPERTS * CAP).astype(jnp.int32)
    slot_token = jnp.zeros((EXPERTS * CAP,), jnp.int32).at[slot_index].set(counter // TOPK, mode='drop')
    slot_used = jnp.zeros((EXPERTS * CAP,), jnp.int32).at[slot_index].set(1, mode='drop')
    return (kept_pair, slot_index, slot_token, slot_used)

def layer_forward(entry, weights):
    inputs_f, seq_length, route_rows, kept_pair, slot_index, slot_token, slot_used = entry
    gain_one, query_matrix, key_matrix, value_matrix, w_attn_out, gain_two, w_router, expert_in, expert_out = weights
    sequence_rows = inputs_f.shape[0]
    groups_per_head = QUERY_HEADS // KEY_VALUE_HEADS
    first_normalized = reduced_precision(rms_scale(inputs_f, gain_one))
    query_rows = reduced_precision(reduced_backward(exact_matrix_product(first_normalized, query_matrix))).reshape(sequence_rows, KEY_VALUE_HEADS, groups_per_head, HEAD_DIMENSION)
    rows_of_key = reduced_precision(reduced_backward(exact_matrix_product(first_normalized, key_matrix))).reshape(sequence_rows, KEY_VALUE_HEADS, HEAD_DIMENSION)
    rows_of_value = reduced_precision(reduced_backward(exact_matrix_product(first_normalized, value_matrix))).reshape(sequence_rows, KEY_VALUE_HEADS, HEAD_DIMENSION)
    scores = jnp.einsum('qhgd,khd->hgqk', query_rows, rows_of_key, precision=lax.Precision.HIGHEST) * HEAD_DIMENSION ** (-0.5)
    scores = reduced_backward(scores)
    positions = jnp.arange(sequence_rows, dtype=jnp.int32)
    allowed = (positions[None, :] <= positions[:, None]) & (positions[None, :] < seq_length)
    scores = jnp.where(allowed, scores, -1e+30)
    attn_probs = reduced_precision(jax.nn.softmax(scores, axis=-1))
    attn_mixed = jnp.einsum('hgqk,khd->qhgd', attn_probs, rows_of_value, precision=lax.Precision.HIGHEST).reshape(sequence_rows, QUERY_HEADS * HEAD_DIMENSION)
    attn_mixed = reduced_precision(reduced_backward(attn_mixed))
    residual = inputs_f + reduced_backward(exact_matrix_product(attn_mixed, w_attn_out))
    normed_two = reduced_precision(rms_scale(residual, gain_two))
    logits = reduced_backward(exact_matrix_product(normed_two, w_router))
    gate_values = jax.nn.softmax(jnp.take_along_axis(logits, route_rows, axis=1), axis=-1)
    sent_rows = reduced_backward(normed_two[slot_token] * slot_used[:, None].astype(jnp.float32)).reshape(EXPERTS, CAP, MODEL_DIMENSION)
    pre_act = reduced_backward(jnp.einsum('ecd,edf->ecf', sent_rows, expert_in, precision=lax.Precision.HIGHEST))
    hidden = reduced_precision(jax.nn.silu(pre_act[..., :FF]) * pre_act[..., FF:])
    returned = jnp.einsum('ecf,efd->ecd', hidden, expert_out, precision=lax.Precision.HIGHEST)
    returned = reduced_precision(reduced_backward(returned)).reshape(EXPERTS * CAP, MODEL_DIMENSION)
    safe_index = jnp.minimum(slot_index, EXPERTS * CAP - 1)
    pair_rows = returned[safe_index].reshape(sequence_rows, TOPK, MODEL_DIMENSION)
    pair_weight = gate_values * kept_pair.reshape(sequence_rows, TOPK).astype(jnp.float32)
    return residual + lax.optimization_barrier(jnp.sum(pair_weight[..., None] * pair_rows, axis=1))

def reference(inputs, gain_one, query_matrix, key_matrix, value_matrix, w_attn_out, gain_two, w_router, expert_in, expert_out, lengths, routes, ranks, cotangent):
    route_seq = routes.reshape(SEQS, SEQ_LEN, TOPK)
    rank_seq = ranks.reshape(SEQS, SEQ_LEN, TOPK)
    kept_pair, slot_index, slot_token, slot_used = jax.vmap(place_pairs)(lengths, route_seq, rank_seq)
    floats = tuple((member.astype(jnp.float32) for member in (inputs, gain_one, query_matrix, key_matrix, value_matrix, w_attn_out, gain_two, w_router, expert_in, expert_out)))

    def forward(inputs_f, gain_a, query_w, key_w, value_w, attn_w, gain_b, router_w, in_w, out_w):
        weights = (gain_a, query_w, key_w, value_w, attn_w, gain_b, router_w, in_w, out_w)

        def per_slot(entry):
            return layer_forward(entry, weights)
        stacked = lax.map(jax.checkpoint(per_slot), (inputs_f.reshape(SEQS, SEQ_LEN, MODEL_DIMENSION), lengths, route_seq, kept_pair, slot_index, slot_token, slot_used))
        return stacked.reshape(SEQS * SEQ_LEN, MODEL_DIMENSION)
    output, pullback = jax.vjp(forward, *floats)
    grads = pullback(cotangent.astype(jnp.float32))
    return (output, grads[0], grads[1], grads[2], grads[3], grads[4], grads[5], grads[6], grads[7], grads[8], grads[9])
```

```python
import functools

import jax
import jax.numpy as jnp
from jax import lax
from jax.experimental import pallas as pl
from jax.experimental.pallas import tpu as pltpu
from jax.sharding import PartitionSpec as P

QUERY_HEADS = 16
KEY_VALUE_HEADS = 8
HEAD_DIMENSION = 64
PAIR = 2 * HEAD_DIMENSION
EPS = 1e-05
UNROUTED = 1 << 20
LANES = 128
SCALE = HEAD_DIMENSION ** (-0.5)

bf16 = jnp.bfloat16
f32 = jnp.float32
VMEM = pl.BlockSpec(memory_space=pltpu.VMEM)
SMEM = pl.BlockSpec(memory_space=pltpu.SMEM)
LIMIT = 56 * 1024 * 1024


def mm(left, right, dims=((1,), (0,))):
    return lax.dot_general(left, right, (dims, ((), ())), preferred_element_type=f32)


def call(kernel, outs, *args, smem=0, scratch=(), flops=0, name=None):
    outs = [jax.ShapeDtypeStruct(s, d) for s, d in outs]
    moved = sum(a.size * a.dtype.itemsize for a in args) + sum(
        o.size * o.dtype.itemsize for o in outs
    )
    return pl.pallas_call(
        kernel,
        out_shape=outs,
        in_specs=[SMEM] * smem + [VMEM] * (len(args) - smem),
        out_specs=[VMEM] * len(outs),
        scratch_shapes=list(scratch),
        compiler_params=pltpu.CompilerParams(vmem_limit_bytes=LIMIT),
        cost_estimate=pl.CostEstimate(flops=flops, bytes_accessed=moved, transcendentals=0),
        name=name,
    )(*args)


def low_lanes(rows):
    return lax.broadcasted_iota(jnp.int32, (rows, PAIR), 1) < HEAD_DIMENSION


def stack_heads(pair, low):
    pair = pair.astype(f32)
    return jnp.concatenate([jnp.where(low, pair, 0.0), jnp.where(low, 0.0, pair)], 0).astype(bf16)


def allowed_keys(rows, length):
    shape = (2 * rows, rows)
    query = lax.broadcasted_iota(jnp.int32, shape, 0)
    query = jnp.where(query >= rows, query - rows, query)
    key = lax.broadcasted_iota(jnp.int32, shape, 1)
    return (key <= query) & (key < length)


def dense_forward(
    len_ref, x_ref, g1_ref, wq_ref, wk_ref, wv_ref, wo_ref, g2_ref, wr_ref, table_ref,
    n1_ref, q_ref, kk_ref, vv_ref, lse_ref, mixed_ref, res_ref, n2_ref, gate_ref,
):
    rows = x_ref.shape[0]
    x = x_ref[...].astype(f32)
    inverse = lax.rsqrt(jnp.mean(x * x, -1, keepdims=True) + EPS)
    n1 = (x * inverse * g1_ref[...]).astype(bf16)
    n1_ref[...] = n1
    q_ref[...] = mm(n1, wq_ref[...]).astype(bf16)
    low = low_lanes(rows)
    for weight_ref, twice_ref in ((wk_ref, kk_ref), (wv_ref, vv_ref)):
        both = mm(n1, weight_ref[...])
        for j in range(KEY_VALUE_HEADS // 2):
            block = both[:, j * PAIR : (j + 1) * PAIR]
            rolled = pltpu.roll(block, HEAD_DIMENSION, 1)
            twice_ref[:, 2 * j * PAIR : (2 * j + 1) * PAIR] = jnp.where(low, block, rolled).astype(bf16)
            twice_ref[:, (2 * j + 1) * PAIR : (2 * j + 2) * PAIR] = jnp.where(low, rolled, block).astype(bf16)
    allowed = allowed_keys(rows, len_ref[0])
    lane = lax.broadcasted_iota(jnp.int32, (rows, LANES), 1)
    totals = jnp.zeros((rows, LANES), f32)
    for h in range(KEY_VALUE_HEADS):
        cols = slice(h * PAIR, (h + 1) * PAIR)
        scores = mm(stack_heads(q_ref[:, cols], low), kk_ref[:, cols], ((1,), (1,))) * SCALE
        scores = jnp.where(allowed, scores, -1e30)
        top = jnp.max(scores, -1, keepdims=True)
        raised = jnp.exp(scores - top)
        total = jnp.sum(raised, -1, keepdims=True)
        probs = (raised / total).astype(bf16)
        mixed = mm(probs, vv_ref[:, cols])
        mixed_ref[:, cols] = jnp.where(low, mixed[:rows], mixed[rows:]).astype(bf16)
        logs = top + jnp.log(total)
        totals = jnp.where(lane == 2 * h, logs[:rows], totals)
        totals = jnp.where(lane == 2 * h + 1, logs[rows:], totals)
    lse_ref[...] = totals
    residual = x + mm(mixed_ref[...], wo_ref[...])
    res_ref[...] = residual
    inverse = lax.rsqrt(jnp.mean(residual * residual, -1, keepdims=True) + EPS)
    n2 = (residual * inverse * g2_ref[...]).astype(bf16)
    n2_ref[...] = n2
    logits = mm(wr_ref[...], n2, ((1,), (1,)))
    routed = table_ref[...] < UNROUTED
    top = jnp.max(jnp.where(routed, logits, -jnp.inf), 0, keepdims=True)
    raised = jnp.where(routed, jnp.exp(jnp.where(routed, logits - top, 0.0)), 0.0)
    total = jnp.sum(raised, 0, keepdims=True)
    gate_ref[...] = raised / jnp.where(total > 0.0, total, 1.0)


def place_kernel(local, capacity, id_ref, *refs):
    tables, (row_ref, col_ref) = refs[:-2], refs[-2:]
    rows = tables[0].shape[1]
    first = id_ref[0] * local
    mine = [table[pl.ds(first + j, 1), :] for table in tables for j in range(local)]
    count = len(mine)
    packed = jnp.concatenate(mine + [jnp.zeros((LANES - count, rows), jnp.int32)], 0).astype(f32)
    columns = packed.T
    places = []
    for i in range(count):
        row = mine[i].astype(f32)
        before = jnp.sum(jnp.where(columns[:, i : i + 1] < row, 1.0, 0.0), 0, keepdims=True)
        places.append(jnp.where((row < UNROUTED) & (before < capacity), before, -1.0))
    for i in range(count):
        d, j = divmod(i, local)
        row_ref[j, d : d + 1, :] = places[i].astype(jnp.int32)
    full = jnp.concatenate(places + [jnp.zeros((LANES - count, rows), f32)], 0)
    col_ref[...] = full.T.astype(jnp.int32)


def expert_kernel(index, local, capacity, owners, id_ref, *refs):
    place_ref = refs[0]
    gates = refs[1 : 1 + owners]
    tokens = refs[1 + owners : 1 + 2 * owners]
    grads = refs[1 + 2 * owners : 1 + 3 * owners]
    (win_ref, wout_ref, keep_ref, send_ref, wret_ref, grow_ref, gg_ref,
     sent, crow, weight, slope, silu, hidden, gret, gpre, acc) = refs[1 + 3 * owners :]
    width = win_ref.shape[1]
    half = wout_ref.shape[1]
    seq = tokens[0].shape[0]
    row = id_ref[0] * local + index
    core = id_ref[1]
    place = lax.broadcasted_iota(jnp.int32, (capacity, seq), 0)
    for d in range(owners):
        span = slice(d * capacity, (d + 1) * capacity)
        hit = place == place_ref[0, d : d + 1, :]
        one = jnp.where(hit, 1.0, 0.0).astype(bf16)
        sent[span, :] = mm(one, tokens[d][...]).astype(bf16)
        crow[span, :] = mm(one, grads[d][...]).astype(bf16)
        weight[span, :] = jnp.sum(jnp.where(hit, gates[d][pl.ds(row, 1), :], 0.0), 1, keepdims=True)
    tile = 256
    for t in range(0, half, tile):
        gate = mm(sent[...], win_ref[0, :, t : t + tile])
        up = mm(sent[...], win_ref[0, :, half + t : half + t + tile])
        sig = jax.nn.sigmoid(gate)
        act = gate * sig
        silu[:, t : t + tile] = act
        slope[:, t : t + tile] = up * sig * (1.0 + gate * (1.0 - sig))
        hidden[:, t : t + tile] = (act * up).astype(bf16)
    dots = jnp.zeros((owners * capacity, 1), f32)
    for t in range(0, width, tile):
        cols = slice(t, t + tile)
        returned = mm(hidden[...], wout_ref[0, :, cols]).astype(bf16).astype(f32)
        upstream = crow[:, cols].astype(f32)
        dots = dots + jnp.sum(returned * upstream, 1, keepdims=True)
        wret_ref[:, cols] = (weight[...] * returned).astype(bf16)
        gret[:, cols] = (weight[...] * upstream).astype(bf16)
    for d in range(owners):
        hit = place == place_ref[0, d : d + 1, :]
        part = dots[d * capacity : (d + 1) * capacity]
        gg_ref[d : d + 1, :] = jnp.sum(jnp.where(hit, part, 0.0), 0, keepdims=True)
    for t in range(0, half, tile):
        ghid = mm(gret[...], wout_ref[0, t : t + tile, :], ((1,), (1,)))
        gpre[:, t : t + tile] = (ghid * slope[:, t : t + tile]).astype(bf16)
        gpre[:, half + t : half + t + tile] = (ghid * silu[:, t : t + tile]).astype(bf16)
    for t in range(0, width, tile):
        grow_ref[:, t : t + tile] = mm(gpre[...], win_ref[0, t : t + tile, :], ((1,), (1,))).astype(bf16)
    pieces = 2 * keep_ref.shape[0]
    base = 0
    for left, right in ((sent, gpre), (hidden, gret)):
        size = left.shape[1]
        step = size // pieces
        for t in range(0, width, tile):
            acc[:size, t : t + tile] = mm(left[...], right[:, t : t + tile], ((0,), (0,)))
        for q in range(pieces // 2):
            lo = pl.multiple_of((2 * q + core) * step, step)
            hi = pl.multiple_of((2 * q + 1 - core) * step, step)
            keep_ref[q, base : base + step, :] = acc[pl.ds(lo, step), :].astype(bf16)
            send_ref[q, base : base + step, :] = acc[pl.ds(hi, step), :].astype(bf16)
        base += step


def combine_kernel(local, capacity, owners, col_ref, *refs):
    rows_in = refs[:local]
    parts = refs[local : local + owners]
    seq = col_ref.shape[0]
    lane = lax.broadcasted_iota(jnp.int32, (seq, local * capacity), 1)
    for d in range(owners):
        hit = None
        for j in range(local):
            col = col_ref[:, d * local + j : d * local + j + 1]
            same = lane == jnp.where(col < 0, -1, col + j * capacity)
            hit = same if hit is None else hit | same
        one = jnp.where(hit, 1.0, 0.0).astype(bf16)
        span = slice(d * capacity, (d + 1) * capacity)
        stacked = jnp.concatenate([r[span, :] for r in rows_in], 0)
        parts[d][...] = mm(one, stacked).astype(parts[d].dtype)


def dense_backward(owners, local, id_ref, len_ref, *refs):
    parts = refs[:owners]
    ggs = refs[owners : 2 * owners]
    (gate_ref, x_ref, cot_ref, res_ref, n1_ref, n2_ref, q_ref, kk_ref, vv_ref, lse_ref, mixed_ref,
     wq_ref, wk_ref, wv_ref, wo_ref, wr_ref, g1_ref, g2_ref,
     gin_ref, keep_ref, send_ref, gg_all, gmix, gq, gk, gv, acc) = refs[2 * owners :]
    rows, width = x_ref.shape
    core = id_ref[1]
    pieces = 2 * keep_ref.shape[0]
    step = width // pieces

    def put(offset, size):
        for q in range(pieces // 2):
            lo = pl.multiple_of((2 * q + core) * step, step)
            hi = pl.multiple_of((2 * q + 1 - core) * step, step)
            keep_ref[q, :, offset : offset + size] = acc[pl.ds(lo, step), :size].astype(bf16)
            send_ref[q, :, offset : offset + size] = acc[pl.ds(hi, step), :size].astype(bf16)

    def weight_gradient(left, right, offset):
        size = right.shape[1]
        tile = 256
        for t in range(0, size, tile):
            acc[:, t : t + tile] = mm(left[...], right[:, t : t + tile], ((0,), (0,)))
        put(offset, size)

    for d in range(owners):
        owner = lax.rem(id_ref[0] + d, owners)
        for j in range(local):
            gg_all[pl.ds(owner * local + j, 1), :] = ggs[d][j : j + 1, :]
    gates = gate_ref[...]
    grad_gates = gg_all[...]
    mean = jnp.sum(gates * grad_gates, 0, keepdims=True)
    glog = (gates * (grad_gates - mean)).astype(bf16)
    grad = parts[0][...]
    for part in parts[1:]:
        grad = grad + part[...].astype(f32)
    grad = grad + mm(glog, wr_ref[...], ((0,), (0,)))
    grouter = mm(glog, n2_ref[...])
    residual = res_ref[...]
    inverse = lax.rsqrt(jnp.mean(residual * residual, -1, keepdims=True) + EPS)
    ggain_two = jnp.sum(grad * residual * inverse, 0, keepdims=True)
    scaled = grad * g2_ref[...]
    gres = cot_ref[...].astype(f32) + inverse * scaled - residual * inverse**3 * jnp.mean(
        scaled * residual, -1, keepdims=True
    )
    branch = gres.astype(bf16)
    gmix[...] = mm(branch, wo_ref[...], ((1,), (1,))).astype(bf16)
    gin_ref[...] = gres
    gq[...] = branch
    col = wq_ref.shape[1] + wk_ref.shape[1] + wv_ref.shape[1]
    weight_gradient(mixed_ref, gq, col)
    low = low_lanes(rows)
    allowed = allowed_keys(rows, len_ref[0])
    held = None
    for h in range(KEY_VALUE_HEADS):
        cols = slice(h * PAIR, (h + 1) * PAIR)
        queries = stack_heads(q_ref[:, cols], low)
        upstream = stack_heads(gmix[:, cols], low)
        scores = mm(queries, kk_ref[:, cols], ((1,), (1,))) * SCALE
        logs = jnp.concatenate([lse_ref[:, 2 * h : 2 * h + 1], lse_ref[:, 2 * h + 1 : 2 * h + 2]], 0)
        probs = jnp.exp(jnp.where(allowed, scores, -1e30) - logs)
        gprobs = mm(upstream, vv_ref[:, cols], ((1,), (1,)))
        inner = jnp.sum(gprobs * probs, -1, keepdims=True)
        gscores = (probs * (gprobs - inner)).astype(bf16)
        gqueries = mm(gscores, kk_ref[:, cols]) * SCALE
        gq[:, cols] = jnp.where(low, gqueries[:rows], gqueries[rows:]).astype(bf16)
        gkey = mm(gscores, queries, ((0,), (0,))) * SCALE
        gvalue = mm(probs.astype(bf16), upstream, ((0,), (0,)))
        gkey = gkey + pltpu.roll(gkey, HEAD_DIMENSION, 1)
        gvalue = gvalue + pltpu.roll(gvalue, HEAD_DIMENSION, 1)
        if h % 2 == 0:
            held = (gkey, gvalue)
        else:
            both = slice((h // 2) * PAIR, (h // 2 + 1) * PAIR)
            gk[:, both] = jnp.where(low, held[0], gkey).astype(bf16)
            gv[:, both] = jnp.where(low, held[1], gvalue).astype(bf16)
    weight_gradient(n1_ref, gq, 0)
    weight_gradient(n1_ref, gk, wq_ref.shape[1])
    weight_gradient(n1_ref, gv, wq_ref.shape[1] + wk_ref.shape[1])
    grad = mm(gq[...], wq_ref[...], ((1,), (1,)))
    grad = grad + mm(gk[...], wk_ref[...], ((1,), (1,)))
    grad = grad + mm(gv[...], wv_ref[...], ((1,), (1,)))
    x = x_ref[...].astype(f32)
    inverse = lax.rsqrt(jnp.mean(x * x, -1, keepdims=True) + EPS)
    ggain_one = jnp.sum(grad * x * inverse, 0, keepdims=True)
    scaled = grad * g1_ref[...]
    gin_ref[...] = gin_ref[...] + inverse * scaled - x * inverse**3 * jnp.mean(
        scaled * x, -1, keepdims=True
    )
    small = jnp.concatenate(
        [grouter, ggain_one, ggain_two, jnp.zeros((LANES - 2 - grouter.shape[0], width), f32)], 0
    )
    acc[:, :LANES] = small.T
    put(col + width, LANES)


def on_device(
    inputs, gain_one, query_matrix, key_matrix, value_matrix, w_attn_out, gain_two, w_router,
    expert_in, expert_out, lengths, routes, ranks, cotangent,
):
    seq, width = inputs.shape
    picks = routes.shape[1]
    experts = w_router.shape[1]
    local = expert_in.shape[0]
    half = expert_out.shape[1]
    owners = lax.axis_size("expert")
    groups = lax.axis_size("group")
    bits = groups.bit_length() - 1
    capacity = (5 * seq * picks + 4 * experts - 1) // (4 * experts)
    places = owners * capacity
    z = lax.axis_index("expert").astype(jnp.int32)
    g = lax.axis_index("group").astype(jnp.int32)
    ids = jnp.stack([z, g % 2])

    def shift(x, d):
        return lax.ppermute(x, "expert", [(i, (i + d) % owners) for i in range(owners)])

    def gather(x):
        return [x] + [shift(x, d) for d in range(1, owners)]

    def scatter(parts):
        return [parts[0]] + [shift(parts[d], -d) for d in range(1, owners)]

    def exchange(x, bit):
        return lax.ppermute(x, "group", [(i, i ^ (1 << bit)) for i in range(groups)])

    expert_ids = jnp.arange(experts, dtype=jnp.int32)
    valid = jnp.arange(seq, dtype=jnp.int32) < lengths[0]
    hits = (routes.T[None] == expert_ids[:, None, None]) & valid[None, None, :]
    table = jnp.min(jnp.where(hits, ranks.T[None], UNROUTED), 1)
    tables = gather(table)
    cots = gather(cotangent)
    gain_one = gain_one.reshape(1, width)
    gain_two = gain_two.reshape(1, width)
    router = w_router.T

    n1, q, kk, vv, lse, mixed, residual, n2, gates = call(
        dense_forward,
        [((seq, width), bf16)] * 4
        + [((seq, LANES), f32), ((seq, width), bf16), ((seq, width), f32), ((seq, width), bf16), ((experts, seq), f32)],
        lengths, inputs, gain_one, query_matrix, key_matrix, value_matrix, w_attn_out, gain_two, router, table,
        smem=1, flops=2 * seq * width * width * 4, name="dense_forward",
    )
    tokens = gather(n2)
    gate_tables = gather(gates)
    row_places, col_places = call(
        functools.partial(place_kernel, local, capacity),
        [((local, owners, seq), jnp.int32), ((seq, LANES), jnp.int32)],
        ids, *tables, smem=1, name="places",
    )

    piece = (width + half) // groups

    def run_expert(j):
        args = [row_places] + gate_tables + tokens + cots + [expert_in, expert_out]
        outs = [
            ((groups // 2, piece, width), bf16),
            ((groups // 2, piece, width), bf16),
            ((places, width), bf16),
            ((places, width), bf16),
            ((owners, seq), f32),
        ]
        picked = [pl.BlockSpec((1, owners, seq), lambda i: (j, 0, 0))]
        picked += [VMEM] * (3 * owners)
        picked += [
            pl.BlockSpec((1, width, 2 * half), lambda i: (j, 0, 0)),
            pl.BlockSpec((1, half, width), lambda i: (j, 0, 0)),
        ]
        return pl.pallas_call(
            functools.partial(expert_kernel, j, local, capacity, owners),
            grid=(1,),
            out_shape=[jax.ShapeDtypeStruct(s, d) for s, d in outs],
            in_specs=[SMEM] + picked,
            out_specs=[VMEM] * len(outs),
            scratch_shapes=[
                pltpu.VMEM((places, width), bf16),
                pltpu.VMEM((places, width), bf16),
                pltpu.VMEM((places, 1), f32),
                pltpu.VMEM((places, half), f32),
                pltpu.VMEM((places, half), f32),
                pltpu.VMEM((places, half), bf16),
                pltpu.VMEM((places, width), bf16),
                pltpu.VMEM((places, 2 * half), bf16),
                pltpu.VMEM((width, width), f32),
            ],
            compiler_params=pltpu.CompilerParams(vmem_limit_bytes=LIMIT),
            cost_estimate=pl.CostEstimate(
                flops=18 * places * width * half, bytes_accessed=20 << 20, transcendentals=0
            ),
            name=f"expert{j}",
        )(ids, *args)

    def reduce_group(keep, send, order):
        total = keep.astype(f32) + exchange(send, 0).astype(f32)
        done = []
        cut = total.shape[-1] // (2 * LANES) * LANES
        for cols, way in ((slice(0, cut), order), (slice(cut, None), order[::-1])):
            part = total[..., cols]
            part = part.reshape((2,) * (bits - 1) + part.shape[1:])
            left = list(range(bits - 1, 0, -1))
            for bit in way:
                axis = left.index(bit)
                left.pop(axis)
                mine = (g >> bit) & 1
                out = lax.dynamic_index_in_dim(part, 1 - mine, axis, keepdims=False).astype(bf16)
                own = lax.dynamic_index_in_dim(part, mine, axis, keepdims=False)
                part = own + exchange(out, bit).astype(f32)
            done.append(part)
        return done

    def gather_group(halves, order):
        wide = []
        for part, way in zip(halves, (order[::-1], order)):
            part = part.astype(bf16)
            left = []
            for bit in (*way, 0):
                at = len([b for b in left if b > bit])
                other = exchange(part, bit)
                mine = (g >> bit) & 1
                part = jnp.where(
                    mine == 0, jnp.stack([part, other], at), jnp.stack([other, part], at)
                )
                left = sorted(left + [bit], reverse=True)
            wide.append(part.reshape((groups,) + part.shape[-2:]))
        return jnp.concatenate(wide, -1)

    order = tuple(range(1, bits))
    returned, grad_rows, dots, full_in, full_out = [], [], [], [], []
    for j in range(local):
        keep, send, wret, grow, gg = run_expert(j)
        returned.append(wret)
        grad_rows.append(grow)
        dots.append(gg)
        whole = gather_group(reduce_group(keep, send, order), order)
        rows_in = width // groups
        full_in.append(whole[:, :rows_in].reshape(width, 2 * half).astype(f32))
        full_out.append(whole[:, rows_in:].reshape(half, width).astype(f32))

    def combine(rows, name):
        return call(
            functools.partial(combine_kernel, local, capacity, owners),
            [((seq, width), f32)] + [((seq, width), bf16)] * (owners - 1),
            col_places, *rows, flops=2 * seq * owners * local * capacity * width, name=name,
        )

    grad_parts = scatter(combine(grad_rows, "combine_grad"))
    dots = jnp.stack(dots, 1)
    dots = scatter([dots[d] for d in range(owners)])
    out_parts = scatter(combine(returned, "combine_out"))
    output = residual
    for part in out_parts:
        output = output + part.astype(f32)

    columns = 2 * width + key_matrix.shape[1] + value_matrix.shape[1] + LANES
    grad_inputs, keep, send = call(
        functools.partial(dense_backward, owners, local),
        [((seq, width), f32)] + [((groups // 2, width // groups, columns), bf16)] * 2,
        ids, lengths, *grad_parts, *dots, gates, inputs, cotangent, residual, n1, n2, q, kk, vv, lse, mixed,
        query_matrix, key_matrix, value_matrix, w_attn_out, router, gain_one, gain_two,
        smem=2, flops=2 * seq * width * width * 8, name="dense_backward",
        scratch=[
            pltpu.VMEM((experts, seq), f32),
            pltpu.VMEM((seq, width), bf16),
            pltpu.VMEM((seq, width), bf16),
            pltpu.VMEM((seq, key_matrix.shape[1]), bf16),
            pltpu.VMEM((seq, value_matrix.shape[1]), bf16),
            pltpu.VMEM((width, width), f32),
        ],
    )
    dense = jnp.concatenate(reduce_group(keep, send, order), -1)
    dense = dense.reshape((owners, dense.shape[0] // owners, columns)).astype(bf16)
    own = lax.dynamic_index_in_dim(dense, z, 0, keepdims=False).astype(f32)
    for d in range(1, owners):
        out = lax.dynamic_index_in_dim(dense, (z + d) % owners, 0, keepdims=False)
        own = own + shift(out, d).astype(f32)
    blocks = gather(own.astype(bf16))
    stacked = jnp.stack(blocks[::-1])
    dense = jnp.roll(stacked, z + 1, 0).reshape(-1, columns).astype(f32)
    sizes = (width, key_matrix.shape[1], value_matrix.shape[1], width, experts, 1, 1)
    cuts = []
    at = 0
    for size in sizes:
        cuts.append(dense[:, at : at + size])
        at += size
    return (
        output,
        grad_inputs,
        cuts[5].reshape(-1),
        cuts[0],
        cuts[1],
        cuts[2],
        cuts[3],
        cuts[6].reshape(-1),
        cuts[4],
        jnp.stack(full_in),
        jnp.stack(full_out),
    )


def solution(mesh):
    tokens = P(("group", "expert"), None)
    experts = P("expert", None, None)
    shares = P("group", None)
    return jax.shard_map(
        on_device,
        mesh=mesh,
        in_specs=(
            tokens, P(), P(), P(), P(), P(), P(), P(), experts, experts,
            P(("group", "expert")), tokens, tokens, tokens,
        ),
        out_specs=(
            tokens, tokens, P("group"), shares, shares, shares, shares, P("group"), shares,
            experts, experts,
        ),
        check_vma=False,
    )
```

```python
import functools

import jax
import jax.numpy as jnp
from jax import lax
from jax.experimental import pallas as pl
from jax.experimental.pallas import tpu as pltpu
from jax.sharding import PartitionSpec as P

QUERY_HEADS = 16
KEY_VALUE_HEADS = 8
HEAD_DIMENSION = 64
PAIR = 2 * HEAD_DIMENSION
EPS = 1e-05
UNROUTED = 1 << 20
LANES = 128
SCALE = HEAD_DIMENSION ** (-0.5)

bf16 = jnp.bfloat16
f32 = jnp.float32
VMEM = pl.BlockSpec(memory_space=pltpu.VMEM)
SMEM = pl.BlockSpec(memory_space=pltpu.SMEM)
ANY = pl.BlockSpec(memory_space=pl.ANY)
COST = 3600000


def mm(left, right, dims=((1,), (0,))):
    return lax.dot_general(left, right, (dims, ((), ())), preferred_element_type=f32)


def call(kernel, outs, *args, smem=0, deps=(), specs=None, out_specs=None, grid=None, prefetch=0, scratch=(), vmem=56, alias=None, us=4, name=None):
    outs = [(pltpu.HBM if vmem > 32 else jax.ShapeDtypeStruct)(s, d) for s, d in outs]
    taken = len(args)

    def body(*refs):
        kernel(*refs[:taken], *refs[taken + len(deps) :])

    in_specs = (specs or [SMEM] * smem + [VMEM] * (taken - smem)) + [ANY] * len(deps)
    out_specs = out_specs or [VMEM] * len(outs)
    if prefetch:
        placed = dict(
            grid_spec=pltpu.PrefetchScalarGridSpec(
                num_scalar_prefetch=prefetch, grid=grid, in_specs=in_specs, out_specs=out_specs, scratch_shapes=list(scratch)
            )
        )
    else:
        placed = dict(in_specs=in_specs, out_specs=out_specs, scratch_shapes=list(scratch))
        if grid:
            placed["grid"] = grid
    return pl.pallas_call(
        body,
        out_shape=outs,
        compiler_params=pltpu.CompilerParams(vmem_limit_bytes=vmem * 1024 * 1024),
        cost_estimate=pl.CostEstimate(flops=0, bytes_accessed=us * COST, transcendentals=0),
        input_output_aliases=alias or {},
        name=name,
        **placed,
    )(*args, *deps)


def low_lanes(rows):
    return lax.broadcasted_iota(jnp.int32, (rows, PAIR), 1) < HEAD_DIMENSION


def stack_heads(pair, low):
    pair = pair.astype(f32)
    return jnp.concatenate([jnp.where(low, pair, 0.0), jnp.where(low, 0.0, pair)], 0).astype(bf16)


def allowed_keys(rows, length):
    shape = (2 * rows, rows)
    query = lax.broadcasted_iota(jnp.int32, shape, 0)
    query = jnp.where(query >= rows, query - rows, query)
    key = lax.broadcasted_iota(jnp.int32, shape, 1)
    return (key <= query) & (key < length)


def pack_rows(field, blocks):
    per = field.shape[0] // blocks
    return jnp.concatenate([field[c * per : (c + 1) * per] for c in range(blocks)], 1)


def places_and_ranks(length, routes_ref, ranks_ref, experts, capacity):
    picks, rows = routes_ref.shape
    expert = lax.broadcasted_iota(jnp.int32, (LANES, rows), 0)
    table = jnp.full((LANES, rows), UNROUTED, jnp.int32)
    for k in range(picks):
        table = jnp.where(expert == routes_ref[k : k + 1, :], ranks_ref[k : k + 1, :], table)
    token = lax.broadcasted_iota(jnp.int32, (LANES, rows), 1)
    table = jnp.where(token < length, table, UNROUTED).astype(f32)
    columns = table.T
    places = []
    for e in range(experts):
        row = table[e : e + 1]
        before = jnp.sum(jnp.where(columns[:, e : e + 1] < row, 1.0, 0.0), 0, keepdims=True)
        places.append(jnp.where((row < UNROUTED) & (before < capacity), before, -1.0))
    return jnp.concatenate(places, 0), table[:experts] < UNROUTED


def dense_forward(
    capacity, len_ref, x_ref, g1_ref, wq_ref, wk_ref, wv_ref, wo_ref, g2_ref, wr_ref, routes_ref, ranks_ref,
    n1_ref, q_ref, kk_ref, vv_ref, lse_ref, mixed_ref, res_ref, pack_ref, gate_ref,
):
    rows = x_ref.shape[0]
    x = x_ref[...].astype(f32)
    inverse = lax.rsqrt(jnp.mean(x * x, -1, keepdims=True) + EPS)
    n1 = (x * inverse * g1_ref[...]).astype(bf16)
    n1_ref[...] = n1
    q_ref[...] = mm(n1, wq_ref[...]).astype(bf16)
    low = low_lanes(rows)
    for weight_ref, twice_ref in ((wk_ref, kk_ref), (wv_ref, vv_ref)):
        both = mm(n1, weight_ref[...])
        for j in range(KEY_VALUE_HEADS // 2):
            block = both[:, j * PAIR : (j + 1) * PAIR]
            rolled = pltpu.roll(block, HEAD_DIMENSION, 1)
            twice_ref[:, 2 * j * PAIR : (2 * j + 1) * PAIR] = jnp.where(low, block, rolled).astype(bf16)
            twice_ref[:, (2 * j + 1) * PAIR : (2 * j + 2) * PAIR] = jnp.where(low, rolled, block).astype(bf16)
    allowed = allowed_keys(rows, len_ref[0])
    lane = lax.broadcasted_iota(jnp.int32, (rows, LANES), 1)
    totals = jnp.zeros((rows, LANES), f32)
    for h in range(KEY_VALUE_HEADS):
        cols = slice(h * PAIR, (h + 1) * PAIR)
        scores = mm(stack_heads(q_ref[:, cols], low), kk_ref[:, cols], ((1,), (1,))) * SCALE
        scores = jnp.where(allowed, scores, -1e30)
        top = jnp.max(scores, -1, keepdims=True)
        raised = jnp.exp(scores - top)
        total = jnp.sum(raised, -1, keepdims=True)
        probs = (raised / total).astype(bf16)
        mixed = mm(probs, vv_ref[:, cols])
        mixed_ref[:, cols] = jnp.where(low, mixed[:rows], mixed[rows:]).astype(bf16)
        logs = top + jnp.log(total)
        totals = jnp.where(lane == 2 * h, logs[:rows], totals)
        totals = jnp.where(lane == 2 * h + 1, logs[rows:], totals)
    lse_ref[...] = totals
    residual = x + mm(mixed_ref[...], wo_ref[...])
    res_ref[...] = residual
    inverse = lax.rsqrt(jnp.mean(residual * residual, -1, keepdims=True) + EPS)
    n2 = (residual * inverse * g2_ref[...]).astype(bf16)
    pack_ref[:rows, :] = n2
    logits = mm(wr_ref[...], n2, ((1,), (1,)))
    places, routed = places_and_ranks(len_ref[0], routes_ref, ranks_ref, wr_ref.shape[0], capacity)
    top = jnp.max(jnp.where(routed, logits, -jnp.inf), 0, keepdims=True)
    raised = jnp.where(routed, jnp.exp(jnp.where(routed, logits - top, 0.0)), 0.0)
    total = jnp.sum(raised, 0, keepdims=True)
    gates = raised / jnp.where(total > 0.0, total, 1.0)
    gate_ref[...] = gates
    high = gates.astype(bf16).astype(f32)
    blocks = x_ref.shape[1] // rows
    fields = [pack_rows(field, blocks) for field in (places, high, gates - high)]
    fill = pack_ref.shape[0] - rows - sum(field.shape[0] for field in fields)
    if fill:
        fields.append(jnp.zeros((fill, x_ref.shape[1]), f32))
    pack_ref[rows:, :] = jnp.concatenate(fields, 0).astype(bf16)


def unpack(pack_ref, expert, experts, seq):
    extra, width = pack_ref.shape[0] - seq, pack_ref.shape[1]
    per = experts * seq // width
    at = expert // per
    row = expert - at * per
    block = pack_ref[seq:, pl.ds(pl.multiple_of(at * seq, seq), seq)].astype(f32)
    index = lax.broadcasted_iota(jnp.int32, (extra, seq), 0)
    place = jnp.sum(jnp.where(index == row, block, 0.0), 0, keepdims=True)
    gate = jnp.sum(
        jnp.where((index == per + row) | (index == 2 * per + row), block, 0.0), 0, keepdims=True
    )
    return place, gate


def expert_forward(local, capacity, owners, id_ref, *refs):
    tokens = refs[:owners]
    (win_ref, wout_ref, sent_ref, hidden_ref, slope_ref, silu_ref, wret_ref, weight) = refs[owners:]
    width, half = win_ref.shape[1], wout_ref.shape[1]
    seq = width // local
    expert = id_ref[0] * local + pl.program_id(0)
    place = lax.broadcasted_iota(jnp.int32, (capacity, seq), 0).astype(f32)
    for d in range(owners):
        span = slice(d * capacity, (d + 1) * capacity)
        row, gate = unpack(tokens[d], expert, owners * local, seq)
        hit = place == row
        one = jnp.where(hit, 1.0, 0.0).astype(bf16)
        sent_ref[0, span, :] = mm(one, tokens[d][:seq, :]).astype(bf16)
        weight[span, :] = jnp.sum(jnp.where(hit, gate, 0.0), 1, keepdims=True)
    tile = 256
    for t in range(0, half, tile):
        gate = mm(sent_ref[0], win_ref[0, :, t : t + tile])
        up = mm(sent_ref[0], win_ref[0, :, half + t : half + t + tile])
        sig = jax.nn.sigmoid(gate)
        act = gate * sig
        silu_ref[0, :, t : t + tile] = act
        slope_ref[0, :, t : t + tile] = up * sig * (1.0 + gate * (1.0 - sig))
        hidden_ref[0, :, t : t + tile] = (act * up).astype(bf16)
    for t in range(0, width, tile):
        cols = slice(t, t + tile)
        returned = mm(hidden_ref[0], wout_ref[0, :, cols]).astype(bf16).astype(f32)
        wret_ref[0, :, cols] = (weight[...] * returned).astype(bf16)


def expert_backward(local, capacity, owners, id_ref, *refs):
    tokens, cots = refs[:owners], refs[owners : 2 * owners]
    (sent_ref, hidden_ref, slope_ref, silu_ref, win_ref, wout_ref,
     sums_ref, grow_ref, gg_ref, crow, weight, gret, gpre) = refs[2 * owners :]
    width, half = win_ref.shape[1], wout_ref.shape[1]
    seq = cots[0].shape[0]
    expert = id_ref[0] * local + pl.program_id(0)
    place = lax.broadcasted_iota(jnp.int32, (capacity, seq), 0).astype(f32)
    places = []
    for d in range(owners):
        span = slice(d * capacity, (d + 1) * capacity)
        row, gate = unpack(tokens[d], expert, owners * local, seq)
        places.append(row)
        hit = place == row
        one = jnp.where(hit, 1.0, 0.0).astype(bf16)
        weight[span, :] = jnp.sum(jnp.where(hit, gate, 0.0), 1, keepdims=True)
        rows = mm(one, cots[d][...])
        crow[span, :] = rows.astype(bf16)
        gret[span, :] = (weight[span, :] * rows).astype(bf16)
    tile = 256
    dots = jnp.zeros((owners * capacity, 1), f32)
    for t in range(0, half, tile):
        cols = slice(t, t + tile)
        ghid = mm(crow[...], wout_ref[0, cols, :], ((1,), (1,)))
        dots = dots + jnp.sum(ghid * hidden_ref[0, :, cols].astype(f32), 1, keepdims=True)
        ghid = ghid * weight[...]
        gpre[:, cols] = (ghid * slope_ref[0, :, cols]).astype(bf16)
        gpre[:, half + t : half + t + tile] = (ghid * silu_ref[0, :, cols]).astype(bf16)
    for d in range(owners):
        part = dots[d * capacity : (d + 1) * capacity]
        gg_ref[0, d : d + 1, :] = jnp.sum(jnp.where(place == places[d], part, 0.0), 0, keepdims=True)
    for t in range(0, width, tile):
        grow_ref[0, :, t : t + tile] = mm(gpre[...], win_ref[0, t : t + tile, :], ((1,), (1,))).astype(bf16)
    pieces = sums_ref.shape[0]
    base = 0
    for left, right in ((sent_ref, gpre), (hidden_ref, gret)):
        size = left.shape[2]
        step = size // pieces
        for t in range(0, width, tile):
            made = mm(left[0], right[:, t : t + tile], ((0,), (0,))).astype(bf16)
            for q in range(pieces):
                sums_ref[q, base : base + step, t : t + tile] = made[q * step : (q + 1) * step]
        base += step


def combine_kernel(local, capacity, owners, counts, id_ref, *refs):
    tokens = refs[:owners]
    rest = refs[owners:]
    rows_in = [(r, i) for r in rest[: counts[0]] for i in range(r.shape[0])]
    dots = [(r, i) for r in rest[counts[0] : counts[0] + counts[1]] for i in range(r.shape[0])]
    part_ref, columns = rest[-2:]
    width = part_ref.shape[2]
    seq = width // local
    d = pl.program_id(0)

    @pl.when(d == 0)
    def _():
        first = id_ref[0] * local
        for t in range(owners):
            table = [unpack(tokens[t], first + j, owners * local, seq)[0] for j in range(local)]
            table.append(jnp.zeros((LANES - local, seq), f32))
            columns[t] = jnp.concatenate(table, 0).T.astype(jnp.int32)

    lane = lax.broadcasted_iota(jnp.int32, (seq, local * capacity), 1)
    hit = None
    for j in range(local):
        col = columns[d, :, j : j + 1]
        same = lane == jnp.where(col < 0, -1, col + j * capacity)
        hit = same if hit is None else hit | same
    one = jnp.where(hit, 1.0, 0.0).astype(bf16)
    stacked = jnp.concatenate([r[i] for r, i in rows_in], 0)
    part_ref[0, :seq, :] = mm(one, stacked).astype(bf16)
    if dots:
        line = jnp.concatenate([r[i, pl.ds(d, 1), :] for r, i in dots], 1)
        high = line.astype(bf16).astype(f32)
        index = lax.broadcasted_iota(jnp.int32, (part_ref.shape[1] - seq, width), 0)
        mine = jnp.where(index == id_ref[0], high, 0.0)
        mine = jnp.where(index == owners + id_ref[0], line - high, mine)
        part_ref[0, seq:, :] = mine.astype(bf16)


def halve_kernel(id_ref, keep_ref, recv_ref, keep_go_ref, recv_go_ref, own_ref, send_ref):
    own_ref[...] = keep_ref[...].astype(f32) + recv_ref[...].astype(f32)
    send_ref[...] = (keep_go_ref[...].astype(f32) + recv_go_ref[...].astype(f32)).astype(bf16)


def last_kernel(keep_ref, recv_ref, out_ref):
    out_ref[...] = (keep_ref[...].astype(f32) + recv_ref[...].astype(f32)).astype(bf16)


def nothing_kernel(*refs):
    pass


def add_kernel(base_ref, parts_ref, out_ref):
    total = base_ref[...]
    for i in range(parts_ref.shape[0]):
        total = total + parts_ref[i].astype(f32)
    out_ref[...] = total


def sum_kernel(in_ref, out_ref):
    total = in_ref[0].astype(f32)
    for i in range(1, in_ref.shape[0]):
        total = total + in_ref[i].astype(f32)
    out_ref[...] = total.astype(out_ref.dtype)


def widen_kernel(in_ref, first_ref, second_ref):
    count, rows, _ = first_ref.shape
    size = in_ref.shape[1] // count
    for j in range(count):
        first_ref[j] = in_ref[0, j * size : j * size + rows, :].astype(f32)
        second_ref[j] = in_ref[0, j * size + rows : (j + 1) * size, :].astype(f32)


def finish_kernel(owners, id_ref, *refs):
    blocks, outs, ordered = refs[:owners], refs[owners:-1], refs[-1]
    size = blocks[0].shape[0]
    for d in range(owners):
        ordered[lax.rem(id_ref[0] + owners - d, owners)] = blocks[d][...].astype(f32)
    for i in range(owners):
        col = 0
        for out in outs:
            cols = out.shape[1]
            out[i * size : (i + 1) * size, :] = ordered[i, :, col : col + cols]
            col += cols


def dense_backward(owners, local, id_ref, len_ref, *refs):
    (part_ref, gate_ref, x_ref, cot_ref, res_ref, n1_ref, pack_ref, q_ref, kk_ref, vv_ref, lse_ref, mixed_ref,
     wq_ref, wk_ref, wv_ref, wo_ref, wr_ref, g1_ref, g2_ref,
     gin_ref, keep_ref, send_ref, gg_all, gmix, gq, gk, gv, acc) = refs
    rows, width = x_ref.shape
    core = id_ref[1]
    pieces = 2 * keep_ref.shape[0]
    step = width // pieces

    def put(offset, size):
        for q in range(pieces // 2):
            lo = pl.multiple_of((2 * q + core) * step, step)
            hi = pl.multiple_of((2 * q + 1 - core) * step, step)
            keep_ref[q, :, offset : offset + size] = acc[pl.ds(lo, step), :size].astype(bf16)
            send_ref[q, :, offset : offset + size] = acc[pl.ds(hi, step), :size].astype(bf16)

    def weight_gradient(left, right, offset):
        size = right.shape[1]
        tile = 256
        for t in range(0, size, tile):
            acc[:, t : t + tile] = mm(left[...], right[:, t : t + tile], ((0,), (0,)))
        put(offset, size)

    tail = part_ref[0, rows:, :].astype(f32)
    for owner in range(1, owners):
        tail = tail + part_ref[owner, rows:, :].astype(f32)
    lines = tail[:owners] + tail[owners : 2 * owners]
    for owner in range(owners):
        for j in range(local):
            gg_all[owner * local + j : owner * local + j + 1, :] = lines[owner : owner + 1, j * rows : (j + 1) * rows]
    gates = gate_ref[...]
    grad_gates = gg_all[...]
    mean = jnp.sum(gates * grad_gates, 0, keepdims=True)
    glog = (gates * (grad_gates - mean)).astype(bf16)
    grad = part_ref[0, :rows, :].astype(f32)
    for owner in range(1, owners):
        grad = grad + part_ref[owner, :rows, :].astype(f32)
    grad = grad + mm(glog, wr_ref[...], ((0,), (0,)))
    grouter = mm(glog, pack_ref[:rows, :])
    residual = res_ref[...]
    inverse = lax.rsqrt(jnp.mean(residual * residual, -1, keepdims=True) + EPS)
    ggain_two = jnp.sum(grad * residual * inverse, 0, keepdims=True)
    scaled = grad * g2_ref[...]
    gres = cot_ref[...].astype(f32) + inverse * scaled - residual * inverse**3 * jnp.mean(
        scaled * residual, -1, keepdims=True
    )
    branch = gres.astype(bf16)
    gmix[...] = mm(branch, wo_ref[...], ((1,), (1,))).astype(bf16)
    gin_ref[...] = gres
    gq[...] = branch
    col = wq_ref.shape[1] + wk_ref.shape[1] + wv_ref.shape[1]
    weight_gradient(mixed_ref, gq, col)
    low = low_lanes(rows)
    allowed = allowed_keys(rows, len_ref[0])
    held = None
    for h in range(KEY_VALUE_HEADS):
        cols = slice(h * PAIR, (h + 1) * PAIR)
        queries = stack_heads(q_ref[:, cols], low)
        upstream = stack_heads(gmix[:, cols], low)
        scores = mm(queries, kk_ref[:, cols], ((1,), (1,))) * SCALE
        logs = jnp.concatenate([lse_ref[:, 2 * h : 2 * h + 1], lse_ref[:, 2 * h + 1 : 2 * h + 2]], 0)
        probs = jnp.exp(jnp.where(allowed, scores, -1e30) - logs)
        gprobs = mm(upstream, vv_ref[:, cols], ((1,), (1,)))
        inner = jnp.sum(gprobs * probs, -1, keepdims=True)
        gscores = (probs * (gprobs - inner)).astype(bf16)
        gqueries = mm(gscores, kk_ref[:, cols]) * SCALE
        gq[:, cols] = jnp.where(low, gqueries[:rows], gqueries[rows:]).astype(bf16)
        gkey = mm(gscores, queries, ((0,), (0,))) * SCALE
        gvalue = mm(probs.astype(bf16), upstream, ((0,), (0,)))
        gkey = gkey + pltpu.roll(gkey, HEAD_DIMENSION, 1)
        gvalue = gvalue + pltpu.roll(gvalue, HEAD_DIMENSION, 1)
        if h % 2 == 0:
            held = (gkey, gvalue)
        else:
            both = slice((h // 2) * PAIR, (h // 2 + 1) * PAIR)
            gk[:, both] = jnp.where(low, held[0], gkey).astype(bf16)
            gv[:, both] = jnp.where(low, held[1], gvalue).astype(bf16)
    weight_gradient(n1_ref, gq, 0)
    weight_gradient(n1_ref, gk, wq_ref.shape[1])
    weight_gradient(n1_ref, gv, wq_ref.shape[1] + wk_ref.shape[1])
    grad = mm(gq[...], wq_ref[...], ((1,), (1,)))
    grad = grad + mm(gk[...], wk_ref[...], ((1,), (1,)))
    grad = grad + mm(gv[...], wv_ref[...], ((1,), (1,)))
    x = x_ref[...].astype(f32)
    inverse = lax.rsqrt(jnp.mean(x * x, -1, keepdims=True) + EPS)
    ggain_one = jnp.sum(grad * x * inverse, 0, keepdims=True)
    scaled = grad * g1_ref[...]
    gin_ref[...] = gin_ref[...] + inverse * scaled - x * inverse**3 * jnp.mean(
        scaled * x, -1, keepdims=True
    )
    small = jnp.concatenate(
        [grouter, ggain_one, ggain_two, jnp.zeros((LANES - 2 - grouter.shape[0], width), f32)], 0
    )
    acc[:, :LANES] = small.T
    put(col + width, LANES)


def on_device(
    inputs, gain_one, query_matrix, key_matrix, value_matrix, w_attn_out, gain_two, w_router,
    expert_in, expert_out, lengths, routes, ranks, cotangent,
):
    seq, width = inputs.shape
    picks = routes.shape[1]
    experts = w_router.shape[1]
    local = expert_in.shape[0]
    half = expert_out.shape[1]
    owners = lax.axis_size("expert")
    groups = lax.axis_size("group")
    steps = groups.bit_length() - 2
    capacity = (5 * seq * picks + 4 * experts - 1) // (4 * experts)
    places = owners * capacity
    z = lax.axis_index("expert").astype(jnp.int32)
    g = lax.axis_index("group").astype(jnp.int32)
    ids = jnp.stack([z, g % 2, g // 2])

    def ring(x, d):
        return lax.ppermute(x, "expert", [(i, (i + d) % owners) for i in range(owners)])

    def swap_cores(x):
        return lax.ppermute(x, "group", [(i, i ^ 1) for i in range(groups)])

    def swap(x, stage):
        return lax.ppermute(
            x, "group", [(i, i ^ (1 << (steps - stage if i % 2 else 1 + stage))) for i in range(groups)]
        )

    def near(x):
        return [ring(x, 1), ring(x, -1)] if owners == 4 else [ring(x, d) for d in range(1, owners)]

    def far(x, got):
        if owners != 4:
            return [x, *got]
        before, after = got
        up = lax.ppermute(before, "expert", [(1, 2), (2, 3)])
        down = lax.ppermute(after, "expert", [(1, 0), (2, 1)])
        return [x, before, jnp.where(z >= 2, up, down), after]

    def halve(keep, recv, stage, name, deps=()):
        pieces, *rest = keep.shape
        half = pieces // 2
        tile = rest[0] // 2
        core, mine = g % 2, g // 2
        index = jnp.arange(half, dtype=jnp.int32)
        low = (mine >> stage) & 1
        high = (mine >> (steps - 1 - stage)) & 1
        stay = jnp.where(core == 0, 2 * index + low, index + high * half)
        go = jnp.where(core == 0, 2 * index + 1 - low, index + (1 - high) * half)
        block = (1, tile, rest[1])
        here = pl.BlockSpec(block, lambda i, t, which: (which[0, i], t, 0))
        there = pl.BlockSpec(block, lambda i, t, which: (which[1, i], t, 0))
        made = pl.BlockSpec(block, lambda i, t, which: (i, t, 0))
        return call(
            halve_kernel, [((half, *rest), f32), ((half, *rest), bf16)],
            jnp.stack([stay, go]), keep, recv, keep, recv,
            prefetch=1, grid=(half, 2), specs=[here, here, there, there], out_specs=[made, made], deps=deps, vmem=16, name=name,
        )

    def last(keep, recv, name, deps=()):
        _, rows, cols = keep.shape
        spec = pl.BlockSpec((1, rows // 2, cols), lambda t: (0, t, 0))
        (made,) = call(
            last_kernel, [(keep.shape, bf16)], keep, recv,
            grid=(2,), specs=[spec, spec], out_specs=[spec], deps=deps, vmem=16, name=name,
        )
        return made

    def behind(arrays, deps, name):
        shapes = [(a.shape, a.dtype) for a in arrays]
        return call(
            nothing_kernel, shapes, *arrays, specs=[ANY] * len(arrays), out_specs=[ANY] * len(arrays), deps=deps,
            alias={i: i for i in range(len(arrays))}, us=1, name=name,
        )

    cot_got = near(cotangent)
    gain_one = gain_one.reshape(1, width)
    gain_two = gain_two.reshape(1, width)
    router = w_router.T
    extra = -(-3 * experts * seq // width // 16) * 16

    n1, q, kk, vv, lse, mixed, residual, pack, gates = call(
        functools.partial(dense_forward, capacity),
        [((seq, width), bf16)] * 4
        + [((seq, LANES), f32), ((seq, width), bf16), ((seq, width), f32), ((seq + extra, width), bf16), ((experts, seq), f32)],
        lengths, inputs, gain_one, query_matrix, key_matrix, value_matrix, w_attn_out, gain_two, router, routes.T, ranks.T,
        smem=1, us=9, name="dense_forward",
    )
    (pack,) = behind([pack], tuple(cot_got), "tokens_go")
    packs = far(pack, near(pack))
    cot_got = behind(cot_got, (packs[owners // 2],), "cotangents_go")
    cots = far(cotangent, cot_got)
    piece = (width + half) // groups

    def rows_of(n):
        return pl.BlockSpec((1, places, n), lambda i: (i, 0, 0))

    def weights(first):
        return [
            pl.BlockSpec((1, width, 2 * half), lambda i: (first + i, 0, 0)),
            pl.BlockSpec((1, half, width), lambda i: (first + i, 0, 0)),
        ]

    sent, hidden, slope, silu, wret = call(
        functools.partial(expert_forward, local, capacity, owners),
        [
            ((local, places, width), bf16),
            ((local, places, half), bf16),
            ((local, places, half), f32),
            ((local, places, half), f32),
            ((local, places, width), bf16),
        ],
        ids, *packs, expert_in, expert_out,
        grid=(local,), specs=[SMEM] + [VMEM] * owners + weights(0),
        out_specs=[rows_of(width), rows_of(half), rows_of(half), rows_of(half), rows_of(width)],
        scratch=[pltpu.VMEM((places, 1), f32)], us=17, name="expert_forward",
    )

    grad_sums, grow, dots = call(
        functools.partial(expert_backward, local, capacity, owners),
        [
            ((groups, local * piece, width), bf16),
            ((local, places, width), bf16),
            ((local, owners, seq), f32),
        ],
        ids, *packs, *cots, sent, hidden, slope, silu, expert_in, expert_out,
        grid=(local,),
        specs=[SMEM] + [VMEM] * (2 * owners) + [rows_of(width), rows_of(half), rows_of(half), rows_of(half)] + weights(0),
        out_specs=[
            pl.BlockSpec((groups, piece, width), lambda i: (0, i, 0)),
            rows_of(width),
            pl.BlockSpec((1, owners, seq), lambda i: (i, 0, 0)),
        ],
        scratch=[
            pltpu.VMEM((places, width), bf16),
            pltpu.VMEM((places, 1), f32),
            pltpu.VMEM((places, width), bf16),
            pltpu.VMEM((places, 2 * half), bf16),
        ],
        us=36, name="expert_backward",
    )
    mine = lax.psum_scatter(grad_sums, "group", scatter_dimension=0, tiled=False)

    def combine(rows, dots, deps, name):
        tail = -(-2 * owners // 16) * 16 if dots else 0
        (made,) = call(
            functools.partial(combine_kernel, local, capacity, owners, (len(rows), len(dots))),
            [((owners, seq + tail, width), bf16)], ids, *packs, *rows, *dots, grid=(owners,), prefetch=1,
            specs=[VMEM] * owners
            + [pl.BlockSpec((r.shape[0], capacity, width), lambda d, ids: (0, d, 0)) for r in rows]
            + [VMEM] * len(dots),
            out_specs=[pl.BlockSpec((1, seq + tail, width), lambda d, ids: (lax.rem(ids[0] + owners - d, owners), 0, 0))],
            scratch=[pltpu.VMEM((owners, seq, LANES), jnp.int32)],
            deps=deps, us=5, name=name,
        )
        return made

    def to_owners(x):
        return lax.all_to_all(x, "expert", split_axis=0, concat_axis=0, tiled=True)

    parts = combine([grow], [dots], (), "combine_grad")
    grad_part = to_owners(parts)
    owned = combine([wret], [], (parts,), "combine_out")

    columns = 2 * width + key_matrix.shape[1] + value_matrix.shape[1] + LANES
    grad_inputs, keep, send = call(
        functools.partial(dense_backward, owners, local),
        [((seq, width), f32)] + [((groups // 2, width // groups, columns), bf16)] * 2,
        ids, lengths, grad_part, gates, inputs, cotangent, residual, n1, pack, q, kk, vv, lse, mixed,
        query_matrix, key_matrix, value_matrix, w_attn_out, router, gain_one, gain_two,
        smem=2, deps=(owned,), us=18, name="dense_backward",
        scratch=[
            pltpu.VMEM((experts, seq), f32),
            pltpu.VMEM((seq, width), bf16),
            pltpu.VMEM((seq, width), bf16),
            pltpu.VMEM((seq, key_matrix.shape[1]), bf16),
            pltpu.VMEM((seq, value_matrix.shape[1]), bf16),
            pltpu.VMEM((width, width), f32),
        ],
    )
    recv = swap_cores(send)
    (owned,) = behind([owned], (send,), "returned_go")
    out_parts = to_owners(owned)
    deps = (owned,)
    for stage in range(steps):
        keep, send = halve(keep, recv, stage, f"dense_halve{stage}", deps)
        recv = swap(send, stage)
        deps = (send,)
        if stage == 0:
            (mine,) = behind([mine], deps, "gather_go")
            gathered = lax.all_gather(mine, "group", axis=0, tiled=False)
            deps = (mine,)
    spec = pl.BlockSpec((seq // 4, width), lambda t: (t, 0))
    (output,) = call(
        add_kernel, [((seq, width), f32)], residual, out_parts, grid=(4,),
        specs=[spec, pl.BlockSpec((owners, seq // 4, width), lambda t: (0, t, 0))], out_specs=[spec],
        deps=deps, us=3, name="output",
    )
    rows = width // groups
    block = rows // owners
    summed = last(keep, recv, "dense_last", (output,))
    blocks = to_owners(summed.reshape(owners, block, columns))
    (block_sum,) = call(sum_kernel, [((block, columns), bf16)], blocks, vmem=16, us=2, name="dense_sum")
    shares = [block_sum] + [ring(block_sum, d) for d in range(1, owners)]
    full = call(
        widen_kernel,
        [((local, width, 2 * half), f32), ((local, half, width), f32)],
        gathered,
        grid=(groups,),
        specs=[pl.BlockSpec((1, local * piece, width), lambda i: (i, 0, 0))],
        out_specs=[
            pl.BlockSpec((local, width // groups, 2 * half), lambda i: (0, i, 0)),
            pl.BlockSpec((local, half // groups, width), lambda i: (0, i, 0)),
        ],
        deps=(block_sum,), us=12, name="widen",
    )
    outs = call(
        functools.partial(finish_kernel, owners),
        [((rows, c), f32) for c in (width, key_matrix.shape[1], value_matrix.shape[1], width, LANES)],
        ids, *shares, smem=1, deps=(full[1],), vmem=16, us=3, name="finish",
        scratch=[pltpu.VMEM((owners, block, columns), f32)],
    )
    small = outs[4]
    return (
        output,
        grad_inputs,
        small[:, experts],
        outs[0],
        outs[1],
        outs[2],
        outs[3],
        small[:, experts + 1],
        small[:, :experts],
        *full,
    )


def solution(mesh):
    tokens = P(("group", "expert"), None)
    experts = P("expert", None, None)
    shares = P("group", None)
    return jax.shard_map(
        on_device,
        mesh=mesh,
        in_specs=(
            tokens, P(), P(), P(), P(), P(), P(), P(), experts, experts,
            P(("group", "expert")), tokens, tokens, tokens,
        ),
        out_specs=(
            tokens, tokens, P("group"), shares, shares, shares, shares, P("group"), shares,
            experts, experts,
        ),
        check_vma=False,
    )
```

```python
import functools

import jax
import jax.numpy as jnp
from jax import lax
from jax.experimental import pallas as pl
from jax.experimental.pallas import tpu as pltpu
from jax.sharding import PartitionSpec as P

QUERY_HEADS = 16
KEY_VALUE_HEADS = 8
HEAD_DIMENSION = 64
PAIR = 2 * HEAD_DIMENSION
EPS = 1e-05
UNROUTED = 1 << 20
LANES = 128
SCALE = HEAD_DIMENSION ** (-0.5)

bf16 = jnp.bfloat16
f32 = jnp.float32
VMEM = pl.BlockSpec(memory_space=pltpu.VMEM)
SMEM = pl.BlockSpec(memory_space=pltpu.SMEM)
ANY = pl.BlockSpec(memory_space=pl.ANY)
HELD = pl.BlockSpec(memory_space=pltpu.HBM)
COST = 3600000
TOKEN = ((8, LANES), f32)


def mm(left, right, dims=((1,), (0,))):
    return lax.dot_general(left, right, (dims, ((), ())), preferred_element_type=f32)


def call(kernel, outs, *args, smem=0, deps=(), specs=None, out_specs=None, grid=None, prefetch=0, scratch=(), vmem=56, alias=None, us=4, name=None):
    outs = [(pltpu.HBM if vmem > 32 else jax.ShapeDtypeStruct)(s, d) for s, d in outs]
    taken = len(args)

    def body(*refs):
        kernel(*refs[:taken], *refs[taken + len(deps) :])

    in_specs = (specs or [SMEM] * smem + [VMEM] * (taken - smem)) + [HELD] * len(deps)
    out_specs = out_specs or [VMEM] * len(outs)
    if prefetch:
        placed = dict(
            grid_spec=pltpu.PrefetchScalarGridSpec(
                num_scalar_prefetch=prefetch, grid=grid, in_specs=in_specs, out_specs=out_specs, scratch_shapes=list(scratch)
            )
        )
    else:
        placed = dict(in_specs=in_specs, out_specs=out_specs, scratch_shapes=list(scratch))
        if grid:
            placed["grid"] = grid
    return pl.pallas_call(
        body,
        out_shape=outs,
        compiler_params=pltpu.CompilerParams(vmem_limit_bytes=vmem * 1024 * 1024),
        cost_estimate=pl.CostEstimate(flops=0, bytes_accessed=us * COST, transcendentals=0),
        input_output_aliases=alias or {},
        name=name,
        **placed,
    )(*args, *deps)


def low_lanes(rows):
    return lax.broadcasted_iota(jnp.int32, (rows, PAIR), 1) < HEAD_DIMENSION


def stack_heads(pair, low):
    pair = pair.astype(f32)
    return jnp.concatenate([jnp.where(low, pair, 0.0), jnp.where(low, 0.0, pair)], 0).astype(bf16)


def allowed_keys(rows, length):
    shape = (2 * rows, rows)
    query = lax.broadcasted_iota(jnp.int32, shape, 0)
    query = jnp.where(query >= rows, query - rows, query)
    key = lax.broadcasted_iota(jnp.int32, shape, 1)
    return (key <= query) & (key < length)


def pack_rows(field, blocks):
    per = field.shape[0] // blocks
    return jnp.concatenate([field[c * per : (c + 1) * per] for c in range(blocks)], 1)


def places_and_ranks(length, routes_ref, ranks_ref, experts, capacity):
    picks, rows = routes_ref.shape
    expert = lax.broadcasted_iota(jnp.int32, (LANES, rows), 0)
    table = jnp.full((LANES, rows), UNROUTED, jnp.int32)
    for k in range(picks):
        table = jnp.where(expert == routes_ref[k : k + 1, :], ranks_ref[k : k + 1, :], table)
    token = lax.broadcasted_iota(jnp.int32, (LANES, rows), 1)
    table = jnp.where(token < length, table, UNROUTED).astype(f32)
    columns = table.T
    places = []
    for e in range(experts):
        row = table[e : e + 1]
        before = jnp.sum(jnp.where(columns[:, e : e + 1] < row, 1.0, 0.0), 0, keepdims=True)
        places.append(jnp.where((row < UNROUTED) & (before < capacity), before, -1.0))
    return jnp.concatenate(places, 0), table[:experts] < UNROUTED


def dense_forward(
    capacity, len_ref, x_ref, g1_ref, wq_ref, wk_ref, wv_ref, wo_ref, g2_ref, wr_ref, routes_ref, ranks_ref,
    n1_ref, q_ref, kk_ref, vv_ref, lse_ref, mixed_ref, res_ref, pack_ref, gate_ref,
):
    rows = x_ref.shape[0]
    x = x_ref[...].astype(f32)
    inverse = lax.rsqrt(jnp.mean(x * x, -1, keepdims=True) + EPS)
    n1 = (x * inverse * g1_ref[...]).astype(bf16)
    n1_ref[...] = n1
    q_ref[...] = mm(n1, wq_ref[...]).astype(bf16)
    low = low_lanes(rows)
    for weight_ref, twice_ref in ((wk_ref, kk_ref), (wv_ref, vv_ref)):
        both = mm(n1, weight_ref[...])
        for j in range(KEY_VALUE_HEADS // 2):
            block = both[:, j * PAIR : (j + 1) * PAIR]
            rolled = pltpu.roll(block, HEAD_DIMENSION, 1)
            twice_ref[:, 2 * j * PAIR : (2 * j + 1) * PAIR] = jnp.where(low, block, rolled).astype(bf16)
            twice_ref[:, (2 * j + 1) * PAIR : (2 * j + 2) * PAIR] = jnp.where(low, rolled, block).astype(bf16)
    allowed = allowed_keys(rows, len_ref[0])
    lane = lax.broadcasted_iota(jnp.int32, (rows, LANES), 1)
    totals = jnp.zeros((rows, LANES), f32)
    for h in range(KEY_VALUE_HEADS):
        cols = slice(h * PAIR, (h + 1) * PAIR)
        scores = mm(stack_heads(q_ref[:, cols], low), kk_ref[:, cols], ((1,), (1,))) * SCALE
        scores = jnp.where(allowed, scores, -1e30)
        top = jnp.max(scores, -1, keepdims=True)
        raised = jnp.exp(scores - top)
        total = jnp.sum(raised, -1, keepdims=True)
        probs = (raised / total).astype(bf16)
        mixed = mm(probs, vv_ref[:, cols])
        mixed_ref[:, cols] = jnp.where(low, mixed[:rows], mixed[rows:]).astype(bf16)
        logs = top + jnp.log(total)
        totals = jnp.where(lane == 2 * h, logs[:rows], totals)
        totals = jnp.where(lane == 2 * h + 1, logs[rows:], totals)
    lse_ref[...] = totals
    residual = x + mm(mixed_ref[...], wo_ref[...])
    res_ref[...] = residual
    inverse = lax.rsqrt(jnp.mean(residual * residual, -1, keepdims=True) + EPS)
    n2 = (residual * inverse * g2_ref[...]).astype(bf16)
    pack_ref[:rows, :] = n2
    logits = mm(wr_ref[...], n2, ((1,), (1,)))
    places, routed = places_and_ranks(len_ref[0], routes_ref, ranks_ref, wr_ref.shape[0], capacity)
    top = jnp.max(jnp.where(routed, logits, -jnp.inf), 0, keepdims=True)
    raised = jnp.where(routed, jnp.exp(jnp.where(routed, logits - top, 0.0)), 0.0)
    total = jnp.sum(raised, 0, keepdims=True)
    gates = raised / jnp.where(total > 0.0, total, 1.0)
    gate_ref[...] = gates
    high = gates.astype(bf16).astype(f32)
    blocks = x_ref.shape[1] // rows
    fields = [pack_rows(field, blocks) for field in (places, high, gates - high)]
    fill = pack_ref.shape[0] - rows - sum(field.shape[0] for field in fields)
    if fill:
        fields.append(jnp.zeros((fill, x_ref.shape[1]), f32))
    pack_ref[rows:, :] = jnp.concatenate(fields, 0).astype(bf16)


def unpack(pack_ref, expert, experts, seq):
    extra, width = pack_ref.shape[0] - seq, pack_ref.shape[1]
    per = experts * seq // width
    at = expert // per
    row = expert - at * per
    block = pack_ref[seq:, pl.ds(pl.multiple_of(at * seq, seq), seq)].astype(f32)
    index = lax.broadcasted_iota(jnp.int32, (extra, seq), 0)
    place = jnp.sum(jnp.where(index == row, block, 0.0), 0, keepdims=True)
    gate = jnp.sum(
        jnp.where((index == per + row) | (index == 2 * per + row), block, 0.0), 0, keepdims=True
    )
    return place, gate


def expert_forward(local, capacity, owners, id_ref, *refs):
    tokens = refs[:owners]
    (win_ref, wout_ref, sent_ref, hidden_ref, slope_ref, silu_ref, wret_ref, weight) = refs[owners:]
    width, half = win_ref.shape[1], wout_ref.shape[1]
    seq = width // local
    expert = id_ref[0] * local + pl.program_id(0)
    place = lax.broadcasted_iota(jnp.int32, (capacity, seq), 0).astype(f32)
    for d in range(owners):
        span = slice(d * capacity, (d + 1) * capacity)
        row, gate = unpack(tokens[d], expert, owners * local, seq)
        hit = place == row
        one = jnp.where(hit, 1.0, 0.0).astype(bf16)
        sent_ref[0, span, :] = mm(one, tokens[d][:seq, :]).astype(bf16)
        weight[span, :] = jnp.sum(jnp.where(hit, gate, 0.0), 1, keepdims=True)
    tile = 256
    for t in range(0, half, tile):
        gate = mm(sent_ref[0], win_ref[0, :, t : t + tile])
        up = mm(sent_ref[0], win_ref[0, :, half + t : half + t + tile])
        sig = jax.nn.sigmoid(gate)
        act = gate * sig
        silu_ref[0, :, t : t + tile] = act
        slope_ref[0, :, t : t + tile] = up * sig * (1.0 + gate * (1.0 - sig))
        hidden_ref[0, :, t : t + tile] = (act * up).astype(bf16)
    for t in range(0, width, tile):
        cols = slice(t, t + tile)
        returned = mm(hidden_ref[0], wout_ref[0, :, cols]).astype(bf16).astype(f32)
        wret_ref[0, :, cols] = (weight[...] * returned).astype(bf16)


def expert_backward(first, split, local, capacity, owners, id_ref, *refs):
    tokens, cots = refs[:owners], refs[owners : 2 * owners]
    rest = refs[2 * owners :]
    sent_ref, hidden_ref, slope_ref, silu_ref, win_ref, wout_ref = rest[:6]
    sums, (grow_ref, gg_ref, crow, weight, gret, gpre) = rest[6:-6], rest[-6:]
    width, half = win_ref.shape[1], wout_ref.shape[1]
    seq = cots[0].shape[0]
    expert = id_ref[0] * local + first + pl.program_id(0)
    place = lax.broadcasted_iota(jnp.int32, (capacity, seq), 0).astype(f32)
    places = []
    for d in range(owners):
        span = slice(d * capacity, (d + 1) * capacity)
        row, gate = unpack(tokens[d], expert, owners * local, seq)
        places.append(row)
        hit = place == row
        one = jnp.where(hit, 1.0, 0.0).astype(bf16)
        weight[span, :] = jnp.sum(jnp.where(hit, gate, 0.0), 1, keepdims=True)
        rows = mm(one, cots[d][...])
        crow[span, :] = rows.astype(bf16)
        gret[span, :] = (weight[span, :] * rows).astype(bf16)
    tile = 256
    dots = jnp.zeros((owners * capacity, 1), f32)
    for t in range(0, half, tile):
        cols = slice(t, t + tile)
        ghid = mm(crow[...], wout_ref[0, cols, :], ((1,), (1,)))
        dots = dots + jnp.sum(ghid * hidden_ref[0, :, cols].astype(f32), 1, keepdims=True)
        ghid = ghid * weight[...]
        gpre[:, cols] = (ghid * slope_ref[0, :, cols]).astype(bf16)
        gpre[:, half + t : half + t + tile] = (ghid * silu_ref[0, :, cols]).astype(bf16)
    for d in range(owners):
        part = dots[d * capacity : (d + 1) * capacity]
        gg_ref[0, d : d + 1, :] = jnp.sum(jnp.where(place == places[d], part, 0.0), 0, keepdims=True)
    for t in range(0, width, tile):
        grow_ref[0, :, t : t + tile] = mm(gpre[...], win_ref[0, t : t + tile, :], ((1,), (1,))).astype(bf16)
    pieces = sums[0].shape[0] * len(sums)
    base = 0
    for left, right in ((sent_ref, gpre), (hidden_ref, gret)):
        size = left.shape[2]
        step = size // pieces
        for t in range(0, width, tile):
            made = mm(left[0], right[:, t : t + tile], ((0,), (0,)))
            for q in range(pieces // len(sums)):
                if split:
                    low = made[2 * q * step : (2 * q + 1) * step]
                    high = made[(2 * q + 1) * step : (2 * q + 2) * step]
                    mine = id_ref[1] == 0
                    sums[0][q, base : base + step, t : t + tile] = jnp.where(mine, low, high).astype(bf16)
                    sums[1][q, base : base + step, t : t + tile] = jnp.where(mine, high, low).astype(bf16)
                else:
                    sums[0][q, base : base + step, t : t + tile] = made[q * step : (q + 1) * step].astype(bf16)
        base += step


def combine_kernel(local, capacity, owners, counts, id_ref, *refs):
    tokens = refs[:owners]
    rest = refs[owners:]
    rows_in = [(r, i) for r in rest[: counts[0]] for i in range(r.shape[0])]
    dots = [(r, i) for r in rest[counts[0] : counts[0] + counts[1]] for i in range(r.shape[0])]
    parts, columns = rest[sum(counts) : -1], rest[-1]
    width = parts[0].shape[-1]
    seq = width // local
    d = pl.program_id(0)

    @pl.when(d == 0)
    def _():
        first = id_ref[0] * local
        for t in range(owners):
            table = [unpack(tokens[t], first + j, owners * local, seq)[0] for j in range(local)]
            table.append(jnp.zeros((LANES - local, seq), f32))
            columns[t] = jnp.concatenate(table, 0).T.astype(jnp.int32)

    lane = lax.broadcasted_iota(jnp.int32, (seq, local * capacity), 1)
    hit = None
    for j in range(local):
        col = columns[d, :, j : j + 1]
        same = lane == jnp.where(col < 0, -1, col + j * capacity)
        hit = same if hit is None else hit | same
    one = jnp.where(hit, 1.0, 0.0).astype(bf16)
    stacked = jnp.concatenate([r[i] for r, i in rows_in], 0)
    made = mm(one, stacked).astype(bf16)
    if dots:
        line = jnp.concatenate([r[i, pl.ds(d, 1), :] for r, i in dots], 1)
        high = line.astype(bf16).astype(f32)
        index = lax.broadcasted_iota(jnp.int32, (parts[0].shape[0] - seq, width), 0)
        mine = jnp.where(index == id_ref[0], high, 0.0)
        mine = jnp.where(index == owners + id_ref[0], line - high, mine)
    if len(parts) == 1:
        parts[0][lax.rem(id_ref[0] + owners - d, owners)] = made
    for t in range(len(parts) if dots else 0):

        @pl.when(d == t)
        def _():
            parts[t][:seq, :] = made
            parts[t][seq:, :] = mine.astype(bf16)


def hop_kernel(*refs):
    pairs = len(refs) // 3
    for i in range(pairs):
        total = refs[i][...].astype(f32) + refs[pairs + i][...].astype(f32)
        refs[2 * pairs + i][...] = total.astype(bf16)


def halve_kernel(id_ref, keep_ref, recv_ref, keep_go_ref, recv_go_ref, own_ref, send_ref, token_ref):
    token_ref[...] = jnp.zeros_like(token_ref)
    own_ref[...] = (keep_ref[...].astype(f32) + recv_ref[...].astype(f32)).astype(own_ref.dtype)
    send_ref[...] = (keep_go_ref[...].astype(f32) + recv_go_ref[...].astype(f32)).astype(bf16)


def nothing_kernel(*refs):
    pass


def add_kernel(base_ref, parts_ref, out_ref, token_ref):
    total = base_ref[...]
    for i in range(parts_ref.shape[0]):
        total = total + parts_ref[i].astype(f32)
    out_ref[...] = total
    token_ref[...] = jnp.zeros_like(token_ref)


def spread_kernel(owners, id_ref, keep_ref, recv_ref, *refs):
    outs, token_ref, total = refs[:owners], refs[owners], refs[owners + 1]
    token_ref[...] = jnp.zeros_like(token_ref)
    block = outs[0].shape[0]
    for i in range(owners):
        span = slice(i * block, (i + 1) * block)
        total[i] = keep_ref[0, span, :].astype(f32) + recv_ref[0, span, :].astype(f32)
    for d in range(owners):
        outs[d][...] = total[lax.rem(id_ref[0] + d, owners)].astype(bf16)


def sum_kernel(*refs):
    total = refs[0][...].astype(f32)
    for ref in refs[1:-1]:
        total = total + ref[...].astype(f32)
    refs[-1][...] = total.astype(refs[-1].dtype)


def widen_kernel(in_ref, *refs):
    first_ref, second_ref, token_ref = refs[-3:]
    token_ref[...] = jnp.zeros_like(token_ref)
    count, rows, _ = first_ref.shape
    size = in_ref.shape[1] // count
    for j in range(count):
        first_ref[j] = in_ref[0, j * size : j * size + rows, :].astype(f32)
        second_ref[j] = in_ref[0, j * size + rows : (j + 1) * size, :].astype(f32)


def finish_kernel(owners, id_ref, *refs):
    blocks, outs, ordered = refs[:owners], refs[owners:-1], refs[-1]
    size = blocks[0].shape[0]
    for d in range(owners):
        ordered[lax.rem(id_ref[0] + owners - d, owners)] = blocks[d][...].astype(f32)
    for i in range(owners):
        col = 0
        for out in outs:
            cols = out.shape[1]
            out[i * size : (i + 1) * size, :] = ordered[i, :, col : col + cols]
            col += cols


def dense_backward(parts, owners, local, id_ref, len_ref, *refs):
    part_refs, refs = refs[:parts], refs[parts:]
    (gate_ref, x_ref, cot_ref, res_ref, n1_ref, pack_ref, q_ref, kk_ref, vv_ref, lse_ref, mixed_ref,
     wq_ref, wk_ref, wv_ref, wo_ref, wr_ref, g1_ref, g2_ref,
     gin_ref, keep_one, send_one, keep_two, send_two, gg_all, gmix, gq, gk, gv, acc) = refs
    rows, width = x_ref.shape
    core = id_ref[1]
    pieces = 2 * keep_one.shape[0]
    step = width // pieces

    def put(stream, offset, size):
        keep_ref, send_ref = stream
        for q in range(pieces // 2):
            lo = pl.multiple_of((2 * q + core) * step, step)
            hi = pl.multiple_of((2 * q + 1 - core) * step, step)
            keep_ref[q, :, offset : offset + size] = acc[pl.ds(lo, step), :size].astype(bf16)
            send_ref[q, :, offset : offset + size] = acc[pl.ds(hi, step), :size].astype(bf16)

    def weight_gradient(left, right, stream, offset):
        size = right.shape[1]
        tile = 256
        for t in range(0, size, tile):
            acc[:, t : t + tile] = mm(left[...], right[:, t : t + tile], ((0,), (0,)))
        put(stream, offset, size)

    tail = part_refs[0][rows:, :].astype(f32)
    for part_ref in part_refs[1:]:
        tail = tail + part_ref[rows:, :].astype(f32)
    lines = tail[:owners] + tail[owners : 2 * owners]
    for owner in range(owners):
        for j in range(local):
            gg_all[owner * local + j : owner * local + j + 1, :] = lines[owner : owner + 1, j * rows : (j + 1) * rows]
    gates = gate_ref[...]
    grad_gates = gg_all[...]
    mean = jnp.sum(gates * grad_gates, 0, keepdims=True)
    glog = (gates * (grad_gates - mean)).astype(bf16)
    grad = part_refs[0][:rows, :].astype(f32)
    for part_ref in part_refs[1:]:
        grad = grad + part_ref[:rows, :].astype(f32)
    grad = grad + mm(glog, wr_ref[...], ((0,), (0,)))
    grouter = mm(glog, pack_ref[:rows, :])
    residual = res_ref[...]
    inverse = lax.rsqrt(jnp.mean(residual * residual, -1, keepdims=True) + EPS)
    ggain_two = jnp.sum(grad * residual * inverse, 0, keepdims=True)
    scaled = grad * g2_ref[...]
    gres = cot_ref[...].astype(f32) + inverse * scaled - residual * inverse**3 * jnp.mean(
        scaled * residual, -1, keepdims=True
    )
    branch = gres.astype(bf16)
    gmix[...] = mm(branch, wo_ref[...], ((1,), (1,))).astype(bf16)
    gin_ref[...] = gres
    gq[...] = branch
    one, two = (keep_one, send_one), (keep_two, send_two)
    weight_gradient(mixed_ref, gq, one, 0)
    rest = LANES - 1 - grouter.shape[0]
    acc[:, :LANES] = jnp.concatenate([grouter, ggain_two, jnp.zeros((rest, width), f32)], 0).T
    put(one, width, LANES)
    low = low_lanes(rows)
    allowed = allowed_keys(rows, len_ref[0])
    held = None
    for h in range(KEY_VALUE_HEADS):
        cols = slice(h * PAIR, (h + 1) * PAIR)
        queries = stack_heads(q_ref[:, cols], low)
        upstream = stack_heads(gmix[:, cols], low)
        scores = mm(queries, kk_ref[:, cols], ((1,), (1,))) * SCALE
        logs = jnp.concatenate([lse_ref[:, 2 * h : 2 * h + 1], lse_ref[:, 2 * h + 1 : 2 * h + 2]], 0)
        probs = jnp.exp(jnp.where(allowed, scores, -1e30) - logs)
        gprobs = mm(upstream, vv_ref[:, cols], ((1,), (1,)))
        inner = jnp.sum(gprobs * probs, -1, keepdims=True)
        gscores = (probs * (gprobs - inner)).astype(bf16)
        gqueries = mm(gscores, kk_ref[:, cols]) * SCALE
        gq[:, cols] = jnp.where(low, gqueries[:rows], gqueries[rows:]).astype(bf16)
        gkey = mm(gscores, queries, ((0,), (0,))) * SCALE
        gvalue = mm(probs.astype(bf16), upstream, ((0,), (0,)))
        gkey = gkey + pltpu.roll(gkey, HEAD_DIMENSION, 1)
        gvalue = gvalue + pltpu.roll(gvalue, HEAD_DIMENSION, 1)
        if h % 2 == 0:
            held = (gkey, gvalue)
        else:
            both = slice((h // 2) * PAIR, (h // 2 + 1) * PAIR)
            gk[:, both] = jnp.where(low, held[0], gkey).astype(bf16)
            gv[:, both] = jnp.where(low, held[1], gvalue).astype(bf16)
    col = 0
    for right in (gq, gk, gv):
        weight_gradient(n1_ref, right, two, col)
        col += right.shape[1]
    grad = mm(gq[...], wq_ref[...], ((1,), (1,)))
    grad = grad + mm(gk[...], wk_ref[...], ((1,), (1,)))
    grad = grad + mm(gv[...], wv_ref[...], ((1,), (1,)))
    x = x_ref[...].astype(f32)
    inverse = lax.rsqrt(jnp.mean(x * x, -1, keepdims=True) + EPS)
    ggain_one = jnp.sum(grad * x * inverse, 0, keepdims=True)
    scaled = grad * g1_ref[...]
    gin_ref[...] = gin_ref[...] + inverse * scaled - x * inverse**3 * jnp.mean(
        scaled * x, -1, keepdims=True
    )
    acc[:, :LANES] = jnp.concatenate([ggain_one, jnp.zeros((LANES - 1, width), f32)], 0).T
    put(two, col, LANES)


def on_device(
    inputs, gain_one, query_matrix, key_matrix, value_matrix, w_attn_out, gain_two, w_router,
    expert_in, expert_out, lengths, routes, ranks, cotangent,
):
    seq, width = inputs.shape
    picks = routes.shape[1]
    experts = w_router.shape[1]
    local = expert_in.shape[0]
    half = expert_out.shape[1]
    owners = lax.axis_size("expert")
    groups = lax.axis_size("group")
    steps = groups.bit_length() - 2
    capacity = (5 * seq * picks + 4 * experts - 1) // (4 * experts)
    places = owners * capacity
    z = lax.axis_index("expert").astype(jnp.int32)
    g = lax.axis_index("group").astype(jnp.int32)
    ids = jnp.stack([z, g % 2, g // 2])

    def ring(x, d):
        return lax.ppermute(x, "expert", [(i, (i + d) % owners) for i in range(owners)])

    def swap_cores(x):
        return lax.ppermute(x, "group", [(i, i ^ 1) for i in range(groups)])

    def swap(x, stage):
        return lax.ppermute(
            x, "group", [(i, i ^ (1 << (steps - stage if i % 2 else 1 + stage))) for i in range(groups)]
        )

    def near(x):
        return [ring(x, 1), ring(x, -1)] if owners == 4 else [ring(x, d) for d in range(1, owners)]

    def far(x, got):
        if owners != 4:
            return [x, *got]
        before, after = got
        up = lax.ppermute(before, "expert", [(1, 2), (2, 3)])
        down = lax.ppermute(after, "expert", [(1, 0), (2, 1)])
        return [x, before, jnp.where(z >= 2, up, down), after]

    def halve(keep, recv, stage, name, deps=(), us=4):
        pieces, *rest = keep.shape
        half = pieces // 2
        tile = rest[0] // 2
        core, mine = g % 2, g // 2
        index = jnp.arange(half, dtype=jnp.int32)
        low = (mine >> stage) & 1
        high = (mine >> (steps - 1 - stage)) & 1
        stay = jnp.where(core == 0, 2 * index + low, index + high * half)
        go = jnp.where(core == 0, 2 * index + 1 - low, index + (1 - high) * half)
        block = (1, tile, rest[1])
        here = pl.BlockSpec(block, lambda i, t, which: (which[0, i], t, 0))
        there = pl.BlockSpec(block, lambda i, t, which: (which[1, i], t, 0))
        made = pl.BlockSpec(block, lambda i, t, which: (i, t, 0))
        return call(
            halve_kernel, [((half, *rest), bf16), ((half, *rest), bf16), TOKEN],
            jnp.stack([stay, go]), keep, recv, keep, recv,
            prefetch=1, grid=(half, 2), specs=[here, here, there, there], out_specs=[made, made, VMEM], deps=deps, vmem=16, us=us, name=name,
        )

    def behind(arrays, deps, name):
        shapes = [(a.shape, a.dtype) for a in arrays]
        return call(
            nothing_kernel, shapes, *arrays, specs=[ANY] * len(arrays), out_specs=[ANY] * len(arrays), deps=deps,
            alias={i: i for i in range(len(arrays))}, us=0, name=name,
        )

    cot_got = near(cotangent)
    gain_one = gain_one.reshape(1, width)
    gain_two = gain_two.reshape(1, width)
    router = w_router.T
    extra = -(-3 * experts * seq // width // 16) * 16

    n1, q, kk, vv, lse, mixed, residual, pack, gates = call(
        functools.partial(dense_forward, capacity),
        [((seq, width), bf16)] * 4
        + [((seq, LANES), f32), ((seq, width), bf16), ((seq, width), f32), ((seq + extra, width), bf16), ((experts, seq), f32)],
        lengths, inputs, gain_one, query_matrix, key_matrix, value_matrix, w_attn_out, gain_two, router, routes.T, ranks.T,
        smem=1, us=9, name="dense_forward",
    )
    (pack,) = behind([pack], tuple(cot_got), "tokens_go")
    packs = far(pack, near(pack))
    cot_got = behind(cot_got, (packs[owners // 2],), "cotangents_go")
    cots = far(cotangent, cot_got)
    piece = (width + half) // groups

    def rows_of(n):
        return pl.BlockSpec((1, places, n), lambda i: (i, 0, 0))

    def weights(first):
        return [
            pl.BlockSpec((1, width, 2 * half), lambda i: (first + i, 0, 0)),
            pl.BlockSpec((1, half, width), lambda i: (first + i, 0, 0)),
        ]

    sent, hidden, slope, silu, wret = call(
        functools.partial(expert_forward, local, capacity, owners),
        [
            ((local, places, width), bf16),
            ((local, places, half), bf16),
            ((local, places, half), f32),
            ((local, places, half), f32),
            ((local, places, width), bf16),
        ],
        ids, *packs, expert_in, expert_out,
        grid=(local,), specs=[SMEM] + [VMEM] * owners + weights(0),
        out_specs=[rows_of(width), rows_of(half), rows_of(half), rows_of(half), rows_of(width)],
        scratch=[pltpu.VMEM((places, 1), f32)], us=17, name="expert_forward",
    )

    tail = -(-2 * owners // 16) * 16

    def backward(first, count, split, deps=()):
        def of(n):
            return pl.BlockSpec((1, places, n), lambda i: (first + i, 0, 0))

        if split:
            sums = [((groups // 2, count * piece, width), bf16)] * 2
            sum_specs = [pl.BlockSpec((groups // 2, piece, width), lambda i: (0, i, 0))] * 2
        else:
            sums = [((groups, count * piece, width), bf16)]
            sum_specs = [pl.BlockSpec((groups, piece, width), lambda i: (0, i, 0))]
        return call(
            functools.partial(expert_backward, first, split, local, capacity, owners),
            sums + [((count, places, width), bf16), ((count, owners, seq), f32)],
            ids, *packs, *cots, sent, hidden, slope, silu, expert_in, expert_out,
            grid=(count,),
            specs=[SMEM] + [VMEM] * (2 * owners) + [of(width), of(half), of(half), of(half)] + weights(first),
            out_specs=sum_specs + [rows_of(width), pl.BlockSpec((1, owners, seq), lambda i: (i, 0, 0))],
            scratch=[
                pltpu.VMEM((places, width), bf16),
                pltpu.VMEM((places, 1), f32),
                pltpu.VMEM((places, width), bf16),
                pltpu.VMEM((places, 2 * half), bf16),
            ],
            deps=deps, us=8 * count, name=f"expert_backward{first}",
        )

    def combine(rows, dots, deps, name, us=8):
        outs = [((seq + tail, width), bf16)] * owners if dots else [((owners, seq, width), bf16)]
        return call(
            functools.partial(combine_kernel, local, capacity, owners, (len(rows), len(dots))),
            outs, ids, *packs, *rows, *dots, grid=(owners,),
            specs=[SMEM] + [VMEM] * owners
            + [pl.BlockSpec((r.shape[0], capacity, width), lambda d: (0, d, 0)) for r in rows]
            + [VMEM] * len(dots),
            scratch=[pltpu.VMEM((owners, seq, LANES), jnp.int32)],
            deps=deps, us=us, name=name,
        )

    sums, *grads = backward(0, local, False)
    mine = lax.psum_scatter(sums, "group", scatter_dimension=0, tiled=False)
    parts = combine([grads[0]], [grads[1]], (), "combine_grad")
    if owners == 4:
        near_by = [
            lax.ppermute(parts[2], "expert", [(2, 1), (3, 2)]),
            lax.ppermute(parts[2], "expert", [(0, 1), (1, 2)]),
        ]
        joined = call(hop_kernel, [(parts[0].shape, bf16)] * 2, parts[1], parts[3], *near_by, us=2, name="hop")
        grad_parts = [parts[0], ring(joined[0], -1), ring(joined[1], 1)]
    else:
        joined = parts
        grad_parts = [parts[0]] + [ring(parts[d], -d) for d in range(1, owners)]
    (owned,) = combine([wret], [], (joined[0],), "combine_out")
    deps = (owned,)

    def to_owners(x):
        return lax.all_to_all(x, "expert", split_axis=0, concat_axis=0, tiled=True)

    sizes = ((width, LANES), (width, key_matrix.shape[1], value_matrix.shape[1], LANES))
    grad_inputs, keep_one, send_one, keep_two, send_two = call(
        functools.partial(dense_backward, len(grad_parts), owners, local),
        [((seq, width), f32)] + [((groups // 2, width // groups, sum(cols)), bf16) for cols in sizes for _ in range(2)],
        ids, lengths, *grad_parts, gates, inputs, cotangent, residual, n1, pack, q, kk, vv, lse, mixed,
        query_matrix, key_matrix, value_matrix, w_attn_out, router, gain_one, gain_two,
        smem=2, deps=deps, us=18, name="dense_backward",
        scratch=[
            pltpu.VMEM((experts, seq), f32),
            pltpu.VMEM((seq, width), bf16),
            pltpu.VMEM((seq, width), bf16),
            pltpu.VMEM((seq, key_matrix.shape[1]), bf16),
            pltpu.VMEM((seq, value_matrix.shape[1]), bf16),
            pltpu.VMEM((width, width), f32),
        ],
    )
    rows = width // groups
    block = rows // owners
    recv_one, recv_two = swap_cores(send_one), swap_cores(send_two)
    (owned,) = behind([owned], (send_one,), "returned_go")
    out_parts = to_owners(owned)
    keep_one, send_one, token = halve(keep_one, recv_one, 0, "one_halve0", (owned,))
    recv_one = swap(send_one, 0)
    keep_two, send_two, token = halve(keep_two, recv_two, 0, "two_halve0", (token,))
    recv_two = swap(send_two, 0)
    (mine,) = behind([mine], (recv_one, token), "gather_go")
    gathered = lax.all_gather(mine, "group", axis=0, tiled=False)
    token = mine
    def spread(keep, recv, name, deps):
        cols = keep.shape[2]
        return call(
            functools.partial(spread_kernel, owners), [((block, cols), bf16)] * owners + [TOKEN], ids, keep, recv,
            smem=1, deps=deps, vmem=16, us=2, name=name, scratch=[pltpu.VMEM((owners, block, cols), f32)],
        )

    def total(blocks, name, deps):
        (made,) = call(sum_kernel, [(blocks[0].shape, bf16)], *blocks, deps=deps, vmem=16, us=2, name=name)
        return [made] + [ring(made, d) for d in range(1, owners)]

    def finish(shares, cols, name, deps):
        return call(
            functools.partial(finish_kernel, owners), [((rows, c), f32) for c in cols],
            ids, *shares, smem=1, deps=deps, vmem=16, us=2, name=name,
            scratch=[pltpu.VMEM((owners, block, sum(cols)), f32)],
        )

    for stage in range(1, steps):
        keep_one, send_one, token = halve(keep_one, recv_one, stage, f"one_halve{stage}", (token,))
        recv_one = swap(send_one, stage)
    *blocks_one, token = spread(keep_one, recv_one, "one_spread", (token,))
    blocks_one = [blocks_one[0]] + [ring(blocks_one[d], d) for d in range(1, owners)]
    for stage in range(1, steps):
        keep_two, send_two, token = halve(keep_two, recv_two, stage, f"two_halve{stage}", (token,))
        recv_two = swap(send_two, stage)
    shares_one = total(blocks_one, "one_sum", (token,))
    spec = pl.BlockSpec((seq // 4, width), lambda t: (t, 0))
    output, token = call(
        add_kernel, [((seq, width), f32), TOKEN], residual, out_parts, grid=(4,),
        specs=[spec, pl.BlockSpec((owners, seq // 4, width), lambda t: (0, t, 0))], out_specs=[spec, VMEM],
        deps=(shares_one[0],), us=4, name="output",
    )
    *one, small_one = finish(shares_one, sizes[0], "one_finish", (token,))
    *blocks_two, token = spread(keep_two, recv_two, "two_spread", (small_one,))
    blocks_two = [blocks_two[0]] + [ring(blocks_two[d], d) for d in range(1, owners)]

    shares_two = total(blocks_two, "two_sum", (token,))
    token = shares_two[0]
    *full, token = call(
        widen_kernel,
        [((local, width, 2 * half), f32), ((local, half, width), f32), TOKEN],
        gathered,
        grid=(groups,),
        specs=[pl.BlockSpec((1, local * piece, width), lambda i: (i, 0, 0))],
        out_specs=[
            pl.BlockSpec((local, width // groups, 2 * half), lambda i: (0, i, 0)),
            pl.BlockSpec((local, half // groups, width), lambda i: (0, i, 0)),
            VMEM,
        ],
        deps=(token,), us=12, name="widen",
    )
    *two, small_two = finish(shares_two, sizes[1], "two_finish", (token,))
    return (
        output,
        grad_inputs,
        small_two[:, 0],
        *two,
        *one,
        small_one[:, experts],
        small_one[:, :experts],
        *full,
    )


def solution(mesh):
    tokens = P(("group", "expert"), None)
    experts = P("expert", None, None)
    shares = P("group", None)
    return jax.shard_map(
        on_device,
        mesh=mesh,
        in_specs=(
            tokens, P(), P(), P(), P(), P(), P(), P(), experts, experts,
            P(("group", "expert")), tokens, tokens, tokens,
        ),
        out_specs=(
            tokens, tokens, P("group"), shares, shares, shares, shares, P("group"), shares,
            experts, experts,
        ),
        check_vma=False,
    )
```

```python
import functools

import jax
import jax.numpy as jnp
from jax import lax
from jax.experimental import pallas as pl
from jax.experimental.pallas import tpu as pltpu
from jax.sharding import PartitionSpec as P

QUERY_HEADS = 16
KEY_VALUE_HEADS = 8
HEAD_DIMENSION = 64
PAIR = 2 * HEAD_DIMENSION
EPS = 1e-05
UNROUTED = 1 << 20
LANES = 128
SCALE = HEAD_DIMENSION ** (-0.5)

bf16 = jnp.bfloat16
f32 = jnp.float32
VMEM = pl.BlockSpec(memory_space=pltpu.VMEM)
SMEM = pl.BlockSpec(memory_space=pltpu.SMEM)
ANY = pl.BlockSpec(memory_space=pl.ANY)
HELD = pl.BlockSpec(memory_space=pltpu.HBM)
COST = 3600000
TOKEN = ((8, LANES), f32)


def mm(left, right, dims=((1,), (0,))):
    return lax.dot_general(left, right, (dims, ((), ())), preferred_element_type=f32)


def call(kernel, outs, *args, smem=0, deps=(), specs=None, out_specs=None, grid=None, prefetch=0, scratch=(), vmem=56, alias=None, us=4, name=None):
    outs = [(pltpu.HBM if vmem > 32 else jax.ShapeDtypeStruct)(s, d) for s, d in outs]
    taken = len(args)

    def body(*refs):
        kernel(*refs[:taken], *refs[taken + len(deps) :])

    in_specs = (specs or [SMEM] * smem + [VMEM] * (taken - smem)) + [HELD] * len(deps)
    out_specs = out_specs or [VMEM] * len(outs)
    if prefetch:
        placed = dict(
            grid_spec=pltpu.PrefetchScalarGridSpec(
                num_scalar_prefetch=prefetch, grid=grid, in_specs=in_specs, out_specs=out_specs, scratch_shapes=list(scratch)
            )
        )
    else:
        placed = dict(in_specs=in_specs, out_specs=out_specs, scratch_shapes=list(scratch))
        if grid:
            placed["grid"] = grid
    return pl.pallas_call(
        body,
        out_shape=outs,
        compiler_params=pltpu.CompilerParams(vmem_limit_bytes=vmem * 1024 * 1024),
        cost_estimate=pl.CostEstimate(flops=0, bytes_accessed=us * COST, transcendentals=0),
        input_output_aliases=alias or {},
        name=name,
        **placed,
    )(*args, *deps)


def low_lanes(rows):
    return lax.broadcasted_iota(jnp.int32, (rows, PAIR), 1) < HEAD_DIMENSION


def stack_heads(pair, low):
    pair = pair.astype(f32)
    return jnp.concatenate([jnp.where(low, pair, 0.0), jnp.where(low, 0.0, pair)], 0).astype(bf16)


def allowed_keys(rows, length):
    shape = (2 * rows, rows)
    query = lax.broadcasted_iota(jnp.int32, shape, 0)
    query = jnp.where(query >= rows, query - rows, query)
    key = lax.broadcasted_iota(jnp.int32, shape, 1)
    return (key <= query) & (key < length)


def pack_rows(field, blocks):
    per = field.shape[0] // blocks
    return jnp.concatenate([field[c * per : (c + 1) * per] for c in range(blocks)], 1)


def places_and_ranks(length, routes_ref, ranks_ref, experts, capacity):
    picks, rows = routes_ref.shape
    expert = lax.broadcasted_iota(jnp.int32, (LANES, rows), 0)
    table = jnp.full((LANES, rows), UNROUTED, jnp.int32)
    for k in range(picks):
        table = jnp.where(expert == routes_ref[k : k + 1, :], ranks_ref[k : k + 1, :], table)
    token = lax.broadcasted_iota(jnp.int32, (LANES, rows), 1)
    table = jnp.where(token < length, table, UNROUTED).astype(f32)
    columns = table.T
    places = []
    for e in range(experts):
        row = table[e : e + 1]
        before = jnp.sum(jnp.where(columns[:, e : e + 1] < row, 1.0, 0.0), 0, keepdims=True)
        places.append(jnp.where((row < UNROUTED) & (before < capacity), before, -1.0))
    return jnp.concatenate(places, 0), table[:experts] < UNROUTED


def dense_forward(
    capacity, len_ref, x_ref, g1_ref, wq_ref, wk_ref, wv_ref, wo_ref, g2_ref, wr_ref, routes_ref, ranks_ref,
    n1_ref, q_ref, kk_ref, vv_ref, lse_ref, mixed_ref, res_ref, pack_ref, gate_ref,
):
    rows = x_ref.shape[0]
    x = x_ref[...].astype(f32)
    inverse = lax.rsqrt(jnp.mean(x * x, -1, keepdims=True) + EPS)
    n1 = (x * inverse * g1_ref[...]).astype(bf16)
    n1_ref[...] = n1
    q_ref[...] = mm(n1, wq_ref[...]).astype(bf16)
    low = low_lanes(rows)
    for weight_ref, twice_ref in ((wk_ref, kk_ref), (wv_ref, vv_ref)):
        both = mm(n1, weight_ref[...])
        for j in range(KEY_VALUE_HEADS // 2):
            block = both[:, j * PAIR : (j + 1) * PAIR]
            rolled = pltpu.roll(block, HEAD_DIMENSION, 1)
            twice_ref[:, 2 * j * PAIR : (2 * j + 1) * PAIR] = jnp.where(low, block, rolled).astype(bf16)
            twice_ref[:, (2 * j + 1) * PAIR : (2 * j + 2) * PAIR] = jnp.where(low, rolled, block).astype(bf16)
    allowed = allowed_keys(rows, len_ref[0])
    lane = lax.broadcasted_iota(jnp.int32, (rows, LANES), 1)
    totals = jnp.zeros((rows, LANES), f32)
    for h in range(KEY_VALUE_HEADS):
        cols = slice(h * PAIR, (h + 1) * PAIR)
        scores = mm(stack_heads(q_ref[:, cols], low), kk_ref[:, cols], ((1,), (1,))) * SCALE
        scores = jnp.where(allowed, scores, -1e30)
        top = jnp.max(scores, -1, keepdims=True)
        raised = jnp.exp(scores - top)
        total = jnp.sum(raised, -1, keepdims=True)
        probs = (raised / total).astype(bf16)
        mixed = mm(probs, vv_ref[:, cols])
        mixed_ref[:, cols] = jnp.where(low, mixed[:rows], mixed[rows:]).astype(bf16)
        logs = top + jnp.log(total)
        totals = jnp.where(lane == 2 * h, logs[:rows], totals)
        totals = jnp.where(lane == 2 * h + 1, logs[rows:], totals)
    lse_ref[...] = totals
    residual = x + mm(mixed_ref[...], wo_ref[...])
    res_ref[...] = residual
    inverse = lax.rsqrt(jnp.mean(residual * residual, -1, keepdims=True) + EPS)
    n2 = (residual * inverse * g2_ref[...]).astype(bf16)
    pack_ref[:rows, :] = n2
    logits = mm(wr_ref[...], n2, ((1,), (1,)))
    places, routed = places_and_ranks(len_ref[0], routes_ref, ranks_ref, wr_ref.shape[0], capacity)
    top = jnp.max(jnp.where(routed, logits, -jnp.inf), 0, keepdims=True)
    raised = jnp.where(routed, jnp.exp(jnp.where(routed, logits - top, 0.0)), 0.0)
    total = jnp.sum(raised, 0, keepdims=True)
    gates = raised / jnp.where(total > 0.0, total, 1.0)
    gate_ref[...] = gates
    high = gates.astype(bf16).astype(f32)
    blocks = x_ref.shape[1] // rows
    fields = [pack_rows(field, blocks) for field in (places, high, gates - high)]
    fill = pack_ref.shape[0] - rows - sum(field.shape[0] for field in fields)
    if fill:
        fields.append(jnp.zeros((fill, x_ref.shape[1]), f32))
    pack_ref[rows:, :] = jnp.concatenate(fields, 0).astype(bf16)


def unpack(pack_ref, expert, experts, seq):
    extra, width = pack_ref.shape[0] - seq, pack_ref.shape[1]
    per = experts * seq // width
    at = expert // per
    row = expert - at * per
    block = pack_ref[seq:, pl.ds(pl.multiple_of(at * seq, seq), seq)].astype(f32)
    index = lax.broadcasted_iota(jnp.int32, (extra, seq), 0)
    place = jnp.sum(jnp.where(index == row, block, 0.0), 0, keepdims=True)
    gate = jnp.sum(
        jnp.where((index == per + row) | (index == 2 * per + row), block, 0.0), 0, keepdims=True
    )
    return place, gate


def expert_forward(local, capacity, owners, id_ref, *refs):
    tokens = refs[:owners]
    (win_ref, wout_ref, sent_ref, hidden_ref, slope_ref, silu_ref, wret_ref, weight) = refs[owners:]
    width, half = win_ref.shape[1], wout_ref.shape[1]
    seq = width // local
    expert = id_ref[0] * local + pl.program_id(0)
    place = lax.broadcasted_iota(jnp.int32, (capacity, seq), 0).astype(f32)
    for d in range(owners):
        span = slice(d * capacity, (d + 1) * capacity)
        row, gate = unpack(tokens[d], expert, owners * local, seq)
        hit = place == row
        one = jnp.where(hit, 1.0, 0.0).astype(bf16)
        sent_ref[0, span, :] = mm(one, tokens[d][:seq, :]).astype(bf16)
        weight[span, :] = jnp.sum(jnp.where(hit, gate, 0.0), 1, keepdims=True)
    tile = 256
    for t in range(0, half, tile):
        gate = mm(sent_ref[0], win_ref[0, :, t : t + tile])
        up = mm(sent_ref[0], win_ref[0, :, half + t : half + t + tile])
        sig = jax.nn.sigmoid(gate)
        act = gate * sig
        silu_ref[0, :, t : t + tile] = act.astype(bf16)
        slope_ref[0, :, t : t + tile] = (up * sig * (1.0 + gate * (1.0 - sig))).astype(bf16)
        hidden_ref[0, :, t : t + tile] = (act * up).astype(bf16)
    for t in range(0, width, tile):
        cols = slice(t, t + tile)
        returned = mm(hidden_ref[0], wout_ref[0, :, cols]).astype(bf16).astype(f32)
        wret_ref[0, :, cols] = (weight[...] * returned).astype(bf16)


def expert_backward(first, split, local, capacity, owners, id_ref, *refs):
    tokens, cots = refs[:owners], refs[owners : 2 * owners]
    rest = refs[2 * owners :]
    sent_ref, hidden_ref, slope_ref, silu_ref, win_ref, wout_ref = rest[:6]
    sums, (grow_ref, gg_ref, crow, weight, gret, gpre) = rest[6:-6], rest[-6:]
    width, half = win_ref.shape[1], wout_ref.shape[1]
    seq = cots[0].shape[0]
    expert = id_ref[0] * local + first + pl.program_id(0)
    place = lax.broadcasted_iota(jnp.int32, (capacity, seq), 0).astype(f32)
    places = []
    for d in range(owners):
        span = slice(d * capacity, (d + 1) * capacity)
        row, gate = unpack(tokens[d], expert, owners * local, seq)
        places.append(row)
        hit = place == row
        one = jnp.where(hit, 1.0, 0.0).astype(bf16)
        weight[span, :] = jnp.sum(jnp.where(hit, gate, 0.0), 1, keepdims=True)
        rows = mm(one, cots[d][...])
        crow[span, :] = rows.astype(bf16)
        gret[span, :] = (weight[span, :] * rows).astype(bf16)
    tile = 256
    dots = jnp.zeros((owners * capacity, 1), f32)
    for t in range(0, half, tile):
        cols = slice(t, t + tile)
        ghid = mm(crow[...], wout_ref[0, cols, :], ((1,), (1,)))
        dots = dots + jnp.sum(ghid * hidden_ref[0, :, cols].astype(f32), 1, keepdims=True)
        ghid = ghid * weight[...]
        gpre[:, cols] = (ghid * slope_ref[0, :, cols].astype(f32)).astype(bf16)
        gpre[:, half + t : half + t + tile] = (ghid * silu_ref[0, :, cols].astype(f32)).astype(bf16)
    for d in range(owners):
        part = dots[d * capacity : (d + 1) * capacity]
        gg_ref[0, d : d + 1, :] = jnp.sum(jnp.where(place == places[d], part, 0.0), 0, keepdims=True)
    for t in range(0, width, tile):
        grow_ref[0, :, t : t + tile] = mm(gpre[...], win_ref[0, t : t + tile, :], ((1,), (1,))).astype(bf16)
    pieces = sums[0].shape[0] * len(sums)
    base = 0
    for left, right in ((sent_ref, gpre), (hidden_ref, gret)):
        size = left.shape[2]
        step = size // pieces
        for t in range(0, width, tile):
            made = mm(left[0], right[:, t : t + tile], ((0,), (0,)))
            for q in range(pieces // len(sums)):
                if split:
                    low = made[2 * q * step : (2 * q + 1) * step]
                    high = made[(2 * q + 1) * step : (2 * q + 2) * step]
                    mine = id_ref[1] == 0
                    sums[0][q, base : base + step, t : t + tile] = jnp.where(mine, low, high).astype(bf16)
                    sums[1][q, base : base + step, t : t + tile] = jnp.where(mine, high, low).astype(bf16)
                else:
                    sums[0][q, base : base + step, t : t + tile] = made[q * step : (q + 1) * step].astype(bf16)
        base += step


def combine_kernel(local, capacity, owners, counts, id_ref, *refs):
    tokens = refs[:owners]
    rest = refs[owners:]
    rows_in = [(r, i) for r in rest[: counts[0]] for i in range(r.shape[0])]
    dots = [(r, i) for r in rest[counts[0] : counts[0] + counts[1]] for i in range(r.shape[0])]
    parts, columns = rest[sum(counts) : -1], rest[-1]
    width = parts[0].shape[-1]
    seq = width // local
    d = pl.program_id(0)

    @pl.when(d == 0)
    def _():
        first = id_ref[0] * local
        for t in range(owners):
            table = [unpack(tokens[t], first + j, owners * local, seq)[0] for j in range(local)]
            table.append(jnp.zeros((LANES - local, seq), f32))
            columns[t] = jnp.concatenate(table, 0).T.astype(jnp.int32)

    lane = lax.broadcasted_iota(jnp.int32, (seq, local * capacity), 1)
    hit = None
    for j in range(local):
        col = columns[d, :, j : j + 1]
        same = lane == jnp.where(col < 0, -1, col + j * capacity)
        hit = same if hit is None else hit | same
    one = jnp.where(hit, 1.0, 0.0).astype(bf16)
    stacked = jnp.concatenate([r[i] for r, i in rows_in], 0)
    made = mm(one, stacked).astype(bf16)
    if dots:
        line = jnp.concatenate([r[i, pl.ds(d, 1), :] for r, i in dots], 1)
        high = line.astype(bf16).astype(f32)
        index = lax.broadcasted_iota(jnp.int32, (parts[0].shape[0] - seq, width), 0)
        mine = jnp.where(index == id_ref[0], high, 0.0)
        mine = jnp.where(index == owners + id_ref[0], line - high, mine)
    if len(parts) == 1:
        parts[0][lax.rem(id_ref[0] + owners - d, owners)] = made
    for t in range(len(parts) if dots else 0):

        @pl.when(d == t)
        def _():
            parts[t][:seq, :] = made
            parts[t][seq:, :] = mine.astype(bf16)


def hop_kernel(*refs):
    pairs = len(refs) // 3
    for i in range(pairs):
        total = refs[i][...].astype(f32) + refs[pairs + i][...].astype(f32)
        refs[2 * pairs + i][...] = total.astype(bf16)


def halve_kernel(id_ref, keep_ref, recv_ref, keep_go_ref, recv_go_ref, own_ref, send_ref, token_ref):
    token_ref[...] = jnp.zeros_like(token_ref)
    own_ref[...] = (keep_ref[...].astype(f32) + recv_ref[...].astype(f32)).astype(own_ref.dtype)
    send_ref[...] = (keep_go_ref[...].astype(f32) + recv_go_ref[...].astype(f32)).astype(bf16)


def nothing_kernel(*refs):
    pass


def add_kernel(base_ref, parts_ref, out_ref, token_ref):
    total = base_ref[...]
    for i in range(parts_ref.shape[0]):
        total = total + parts_ref[i].astype(f32)
    out_ref[...] = total
    token_ref[...] = jnp.zeros_like(token_ref)


def spread_kernel(owners, id_ref, keep_ref, recv_ref, *refs):
    outs, token_ref, total = refs[:owners], refs[owners], refs[owners + 1]
    token_ref[...] = jnp.zeros_like(token_ref)
    block = outs[0].shape[0]
    for i in range(owners):
        span = slice(i * block, (i + 1) * block)
        total[i] = keep_ref[0, span, :].astype(f32) + recv_ref[0, span, :].astype(f32)
    for d in range(owners):
        outs[d][...] = total[lax.rem(id_ref[0] + d, owners)].astype(bf16)


def sum_kernel(*refs):
    total = refs[0][...].astype(f32)
    for ref in refs[1:-1]:
        total = total + ref[...].astype(f32)
    refs[-1][...] = total.astype(refs[-1].dtype)


def widen_kernel(in_ref, *refs):
    first_ref, second_ref, token_ref = refs[-3:]
    token_ref[...] = jnp.zeros_like(token_ref)
    count, rows, _ = first_ref.shape
    size = in_ref.shape[1] // count
    for j in range(count):
        first_ref[j] = in_ref[0, j * size : j * size + rows, :].astype(f32)
        second_ref[j] = in_ref[0, j * size + rows : (j + 1) * size, :].astype(f32)


def finish_kernel(owners, id_ref, *refs):
    blocks, outs, ordered = refs[:owners], refs[owners:-1], refs[-1]
    size = blocks[0].shape[0]
    for d in range(owners):
        ordered[lax.rem(id_ref[0] + owners - d, owners)] = blocks[d][...].astype(f32)
    for i in range(owners):
        col = 0
        for out in outs:
            cols = out.shape[1]
            out[i * size : (i + 1) * size, :] = ordered[i, :, col : col + cols]
            col += cols


def dense_backward(parts, owners, local, id_ref, len_ref, *refs):
    part_refs, refs = refs[:parts], refs[parts:]
    (gate_ref, x_ref, cot_ref, res_ref, n1_ref, pack_ref, q_ref, kk_ref, vv_ref, lse_ref, mixed_ref,
     wq_ref, wk_ref, wv_ref, wo_ref, wr_ref, g1_ref, g2_ref,
     gin_ref, keep_one, send_one, keep_two, send_two, gg_all, gmix, gq, gk, gv, acc) = refs
    rows, width = x_ref.shape
    core = id_ref[1]
    pieces = 2 * keep_one.shape[0]
    step = width // pieces

    def put(stream, offset, size):
        keep_ref, send_ref = stream
        for q in range(pieces // 2):
            lo = pl.multiple_of((2 * q + core) * step, step)
            hi = pl.multiple_of((2 * q + 1 - core) * step, step)
            keep_ref[q, :, offset : offset + size] = acc[pl.ds(lo, step), :size].astype(bf16)
            send_ref[q, :, offset : offset + size] = acc[pl.ds(hi, step), :size].astype(bf16)

    def weight_gradient(left, right, stream, offset):
        size = right.shape[1]
        tile = 256
        for t in range(0, size, tile):
            acc[:, t : t + tile] = mm(left[...], right[:, t : t + tile], ((0,), (0,)))
        put(stream, offset, size)

    tail = part_refs[0][rows:, :].astype(f32)
    for part_ref in part_refs[1:]:
        tail = tail + part_ref[rows:, :].astype(f32)
    lines = tail[:owners] + tail[owners : 2 * owners]
    for owner in range(owners):
        for j in range(local):
            gg_all[owner * local + j : owner * local + j + 1, :] = lines[owner : owner + 1, j * rows : (j + 1) * rows]
    gates = gate_ref[...]
    grad_gates = gg_all[...]
    mean = jnp.sum(gates * grad_gates, 0, keepdims=True)
    glog = (gates * (grad_gates - mean)).astype(bf16)
    grad = part_refs[0][:rows, :].astype(f32)
    for part_ref in part_refs[1:]:
        grad = grad + part_ref[:rows, :].astype(f32)
    grad = grad + mm(glog, wr_ref[...], ((0,), (0,)))
    grouter = mm(glog, pack_ref[:rows, :])
    residual = res_ref[...]
    inverse = lax.rsqrt(jnp.mean(residual * residual, -1, keepdims=True) + EPS)
    ggain_two = jnp.sum(grad * residual * inverse, 0, keepdims=True)
    scaled = grad * g2_ref[...]
    gres = cot_ref[...].astype(f32) + inverse * scaled - residual * inverse**3 * jnp.mean(
        scaled * residual, -1, keepdims=True
    )
    branch = gres.astype(bf16)
    gmix[...] = mm(branch, wo_ref[...], ((1,), (1,))).astype(bf16)
    gin_ref[...] = gres
    gq[...] = branch
    one, two = (keep_one, send_one), (keep_two, send_two)
    weight_gradient(mixed_ref, gq, one, 0)
    rest = LANES - 1 - grouter.shape[0]
    acc[:, :LANES] = jnp.concatenate([grouter, ggain_two, jnp.zeros((rest, width), f32)], 0).T
    put(one, width, LANES)
    low = low_lanes(rows)
    allowed = allowed_keys(rows, len_ref[0])
    held = None
    for h in range(KEY_VALUE_HEADS):
        cols = slice(h * PAIR, (h + 1) * PAIR)
        queries = stack_heads(q_ref[:, cols], low)
        upstream = stack_heads(gmix[:, cols], low)
        scores = mm(queries, kk_ref[:, cols], ((1,), (1,))) * SCALE
        logs = jnp.concatenate([lse_ref[:, 2 * h : 2 * h + 1], lse_ref[:, 2 * h + 1 : 2 * h + 2]], 0)
        probs = jnp.exp(jnp.where(allowed, scores, -1e30) - logs)
        gprobs = mm(upstream, vv_ref[:, cols], ((1,), (1,)))
        inner = jnp.sum(gprobs * probs, -1, keepdims=True)
        gscores = (probs * (gprobs - inner)).astype(bf16)
        gqueries = mm(gscores, kk_ref[:, cols]) * SCALE
        gq[:, cols] = jnp.where(low, gqueries[:rows], gqueries[rows:]).astype(bf16)
        gkey = mm(gscores, queries, ((0,), (0,))) * SCALE
        gvalue = mm(probs.astype(bf16), upstream, ((0,), (0,)))
        gkey = gkey + pltpu.roll(gkey, HEAD_DIMENSION, 1)
        gvalue = gvalue + pltpu.roll(gvalue, HEAD_DIMENSION, 1)
        if h % 2 == 0:
            held = (gkey, gvalue)
        else:
            both = slice((h // 2) * PAIR, (h // 2 + 1) * PAIR)
            gk[:, both] = jnp.where(low, held[0], gkey).astype(bf16)
            gv[:, both] = jnp.where(low, held[1], gvalue).astype(bf16)
    col = 0
    for right in (gq, gk, gv):
        weight_gradient(n1_ref, right, two, col)
        col += right.shape[1]
    grad = mm(gq[...], wq_ref[...], ((1,), (1,)))
    grad = grad + mm(gk[...], wk_ref[...], ((1,), (1,)))
    grad = grad + mm(gv[...], wv_ref[...], ((1,), (1,)))
    x = x_ref[...].astype(f32)
    inverse = lax.rsqrt(jnp.mean(x * x, -1, keepdims=True) + EPS)
    ggain_one = jnp.sum(grad * x * inverse, 0, keepdims=True)
    scaled = grad * g1_ref[...]
    gin_ref[...] = gin_ref[...] + inverse * scaled - x * inverse**3 * jnp.mean(
        scaled * x, -1, keepdims=True
    )
    acc[:, :LANES] = jnp.concatenate([ggain_one, jnp.zeros((LANES - 1, width), f32)], 0).T
    put(two, col, LANES)


def on_device(
    inputs, gain_one, query_matrix, key_matrix, value_matrix, w_attn_out, gain_two, w_router,
    expert_in, expert_out, lengths, routes, ranks, cotangent,
):
    seq, width = inputs.shape
    picks = routes.shape[1]
    experts = w_router.shape[1]
    local = expert_in.shape[0]
    half = expert_out.shape[1]
    owners = lax.axis_size("expert")
    groups = lax.axis_size("group")
    steps = groups.bit_length() - 2
    capacity = (5 * seq * picks + 4 * experts - 1) // (4 * experts)
    places = owners * capacity
    z = lax.axis_index("expert").astype(jnp.int32)
    g = lax.axis_index("group").astype(jnp.int32)
    ids = jnp.stack([z, g % 2, g // 2])

    def ring(x, d):
        return lax.ppermute(x, "expert", [(i, (i + d) % owners) for i in range(owners)])

    def swap_cores(x):
        return lax.ppermute(x, "group", [(i, i ^ 1) for i in range(groups)])

    def swap(x, stage):
        return lax.ppermute(
            x, "group", [(i, i ^ (1 << (steps - stage if i % 2 else 1 + stage))) for i in range(groups)]
        )

    def near(x):
        return [ring(x, 1), ring(x, -1)] if owners == 4 else [ring(x, d) for d in range(1, owners)]

    def far(x, got):
        if owners != 4:
            return [x, *got]
        before, after = got
        up = lax.ppermute(before, "expert", [(1, 2), (2, 3)])
        down = lax.ppermute(after, "expert", [(1, 0), (2, 1)])
        return [x, before, jnp.where(z >= 2, up, down), after]

    def halve(keep, recv, stage, name, deps=(), us=4):
        pieces, *rest = keep.shape
        half = pieces // 2
        tile = rest[0] // 2
        core, mine = g % 2, g // 2
        index = jnp.arange(half, dtype=jnp.int32)
        low = (mine >> stage) & 1
        high = (mine >> (steps - 1 - stage)) & 1
        stay = jnp.where(core == 0, 2 * index + low, index + high * half)
        go = jnp.where(core == 0, 2 * index + 1 - low, index + (1 - high) * half)
        block = (1, tile, rest[1])
        here = pl.BlockSpec(block, lambda i, t, which: (which[0, i], t, 0))
        there = pl.BlockSpec(block, lambda i, t, which: (which[1, i], t, 0))
        made = pl.BlockSpec(block, lambda i, t, which: (i, t, 0))
        return call(
            halve_kernel, [((half, *rest), bf16), ((half, *rest), bf16), TOKEN],
            jnp.stack([stay, go]), keep, recv, keep, recv,
            prefetch=1, grid=(half, 2), specs=[here, here, there, there], out_specs=[made, made, VMEM], deps=deps, vmem=16, us=us, name=name,
        )

    def behind(arrays, deps, name):
        shapes = [(a.shape, a.dtype) for a in arrays]
        return call(
            nothing_kernel, shapes, *arrays, specs=[ANY] * len(arrays), out_specs=[ANY] * len(arrays), deps=deps,
            alias={i: i for i in range(len(arrays))}, us=0, name=name,
        )

    cot_got = near(cotangent)
    gain_one = gain_one.reshape(1, width)
    gain_two = gain_two.reshape(1, width)
    router = w_router.T
    extra = -(-3 * experts * seq // width // 16) * 16

    n1, q, kk, vv, lse, mixed, residual, pack, gates = call(
        functools.partial(dense_forward, capacity),
        [((seq, width), bf16)] * 4
        + [((seq, LANES), f32), ((seq, width), bf16), ((seq, width), f32), ((seq + extra, width), bf16), ((experts, seq), f32)],
        lengths, inputs, gain_one, query_matrix, key_matrix, value_matrix, w_attn_out, gain_two, router, routes.T, ranks.T,
        smem=1, us=9, name="dense_forward",
    )
    (pack,) = behind([pack], tuple(cot_got), "tokens_go")
    packs = far(pack, near(pack))
    cot_got = behind(cot_got, (packs[owners // 2],), "cotangents_go")
    cots = far(cotangent, cot_got)
    piece = (width + half) // groups

    def rows_of(n):
        return pl.BlockSpec((1, places, n), lambda i: (i, 0, 0))

    def weights(first):
        return [
            pl.BlockSpec((1, width, 2 * half), lambda i: (first + i, 0, 0)),
            pl.BlockSpec((1, half, width), lambda i: (first + i, 0, 0)),
        ]

    sent, hidden, slope, silu, wret = call(
        functools.partial(expert_forward, local, capacity, owners),
        [
            ((local, places, width), bf16),
            ((local, places, half), bf16),
            ((local, places, half), bf16),
            ((local, places, half), bf16),
            ((local, places, width), bf16),
        ],
        ids, *packs, expert_in, expert_out,
        grid=(local,), specs=[SMEM] + [VMEM] * owners + weights(0),
        out_specs=[rows_of(width), rows_of(half), rows_of(half), rows_of(half), rows_of(width)],
        scratch=[pltpu.VMEM((places, 1), f32)], us=17, name="expert_forward",
    )

    tail = -(-2 * owners // 16) * 16

    def backward(first, count, split, deps=()):
        def of(n):
            return pl.BlockSpec((1, places, n), lambda i: (first + i, 0, 0))

        if split:
            sums = [((groups // 2, count * piece, width), bf16)] * 2
            sum_specs = [pl.BlockSpec((groups // 2, piece, width), lambda i: (0, i, 0))] * 2
        else:
            sums = [((groups, count * piece, width), bf16)]
            sum_specs = [pl.BlockSpec((groups, piece, width), lambda i: (0, i, 0))]
        return call(
            functools.partial(expert_backward, first, split, local, capacity, owners),
            sums + [((count, places, width), bf16), ((count, owners, seq), f32)],
            ids, *packs, *cots, sent, hidden, slope, silu, expert_in, expert_out,
            grid=(count,),
            specs=[SMEM] + [VMEM] * (2 * owners) + [of(width), of(half), of(half), of(half)] + weights(first),
            out_specs=sum_specs + [rows_of(width), pl.BlockSpec((1, owners, seq), lambda i: (i, 0, 0))],
            scratch=[
                pltpu.VMEM((places, width), bf16),
                pltpu.VMEM((places, 1), f32),
                pltpu.VMEM((places, width), bf16),
                pltpu.VMEM((places, 2 * half), bf16),
            ],
            deps=deps, us=8 * count, name=f"expert_backward{first}",
        )

    def combine(rows, dots, deps, name, us=8):
        outs = [((seq + tail, width), bf16)] * owners if dots else [((owners, seq, width), bf16)]
        return call(
            functools.partial(combine_kernel, local, capacity, owners, (len(rows), len(dots))),
            outs, ids, *packs, *rows, *dots, grid=(owners,),
            specs=[SMEM] + [VMEM] * owners
            + [pl.BlockSpec((r.shape[0], capacity, width), lambda d: (0, d, 0)) for r in rows]
            + [VMEM] * len(dots),
            scratch=[pltpu.VMEM((owners, seq, LANES), jnp.int32)],
            deps=deps, us=us, name=name,
        )

    sums, *grads = backward(0, local, False)
    mine = lax.psum_scatter(sums, "group", scatter_dimension=0, tiled=False)
    parts = combine([grads[0]], [grads[1]], (), "combine_grad")
    if owners == 4:
        near_by = [
            lax.ppermute(parts[2], "expert", [(2, 1), (3, 2)]),
            lax.ppermute(parts[2], "expert", [(0, 1), (1, 2)]),
        ]
        joined = call(hop_kernel, [(parts[0].shape, bf16)] * 2, parts[1], parts[3], *near_by, us=2, name="hop")
        grad_parts = [parts[0], ring(joined[0], -1), ring(joined[1], 1)]
    else:
        joined = parts
        grad_parts = [parts[0]] + [ring(parts[d], -d) for d in range(1, owners)]
    (owned,) = combine([wret], [], (joined[0],), "combine_out")
    deps = (owned,)

    def to_owners(x):
        return lax.all_to_all(x, "expert", split_axis=0, concat_axis=0, tiled=True)

    sizes = ((width, LANES), (width, key_matrix.shape[1], value_matrix.shape[1], LANES))
    grad_inputs, keep_one, send_one, keep_two, send_two = call(
        functools.partial(dense_backward, len(grad_parts), owners, local),
        [((seq, width), f32)] + [((groups // 2, width // groups, sum(cols)), bf16) for cols in sizes for _ in range(2)],
        ids, lengths, *grad_parts, gates, inputs, cotangent, residual, n1, pack, q, kk, vv, lse, mixed,
        query_matrix, key_matrix, value_matrix, w_attn_out, router, gain_one, gain_two,
        smem=2, deps=deps, us=18, name="dense_backward",
        scratch=[
            pltpu.VMEM((experts, seq), f32),
            pltpu.VMEM((seq, width), bf16),
            pltpu.VMEM((seq, width), bf16),
            pltpu.VMEM((seq, key_matrix.shape[1]), bf16),
            pltpu.VMEM((seq, value_matrix.shape[1]), bf16),
            pltpu.VMEM((width, width), f32),
        ],
    )
    rows = width // groups
    block = rows // owners
    recv_one, recv_two = swap_cores(send_one), swap_cores(send_two)
    (owned,) = behind([owned], (send_one,), "returned_go")
    out_parts = to_owners(owned)
    keep_one, send_one, token = halve(keep_one, recv_one, 0, "one_halve0", (owned,))
    recv_one = swap(send_one, 0)
    keep_two, send_two, token = halve(keep_two, recv_two, 0, "two_halve0", (token,))
    recv_two = swap(send_two, 0)
    (mine,) = behind([mine], (recv_one, token), "gather_go")
    gathered = lax.all_gather(mine, "group", axis=0, tiled=False)
    token = mine
    def spread(keep, recv, name, deps):
        cols = keep.shape[2]
        return call(
            functools.partial(spread_kernel, owners), [((block, cols), bf16)] * owners + [TOKEN], ids, keep, recv,
            smem=1, deps=deps, vmem=16, us=2, name=name, scratch=[pltpu.VMEM((owners, block, cols), f32)],
        )

    def total(blocks, name, deps):
        (made,) = call(sum_kernel, [(blocks[0].shape, bf16)], *blocks, deps=deps, vmem=16, us=2, name=name)
        return [made] + [ring(made, d) for d in range(1, owners)]

    def finish(shares, cols, name, deps):
        return call(
            functools.partial(finish_kernel, owners), [((rows, c), f32) for c in cols],
            ids, *shares, smem=1, deps=deps, vmem=16, us=2, name=name,
            scratch=[pltpu.VMEM((owners, block, sum(cols)), f32)],
        )

    for stage in range(1, steps):
        keep_one, send_one, token = halve(keep_one, recv_one, stage, f"one_halve{stage}", (token,))
        recv_one = swap(send_one, stage)
    *blocks_one, token = spread(keep_one, recv_one, "one_spread", (token,))
    blocks_one = [blocks_one[0]] + [ring(blocks_one[d], d) for d in range(1, owners)]
    for stage in range(1, steps):
        keep_two, send_two, token = halve(keep_two, recv_two, stage, f"two_halve{stage}", (token,))
        recv_two = swap(send_two, stage)
    shares_one = total(blocks_one, "one_sum", (token,))
    *blocks_two, token = spread(keep_two, recv_two, "two_spread", (shares_one[0],))
    blocks_two = [blocks_two[0]] + [ring(blocks_two[d], d) for d in range(1, owners)]
    spec = pl.BlockSpec((seq // 4, width), lambda t: (t, 0))
    output, token = call(
        add_kernel, [((seq, width), f32), TOKEN], residual, out_parts, grid=(4,),
        specs=[spec, pl.BlockSpec((owners, seq // 4, width), lambda t: (0, t, 0))], out_specs=[spec, VMEM],
        deps=(token,), us=4, name="output",
    )
    shares_two = total(blocks_two, "two_sum", (token,))
    *one, small_one = finish(shares_one, sizes[0], "one_finish", (shares_two[0],))
    *two, small_two = finish(shares_two, sizes[1], "two_finish", (small_one,))
    token = small_two
    *full, _ = call(
        widen_kernel,
        [((local, width, 2 * half), f32), ((local, half, width), f32), TOKEN],
        gathered,
        grid=(groups,),
        specs=[pl.BlockSpec((1, local * piece, width), lambda i: (i, 0, 0))],
        out_specs=[
            pl.BlockSpec((local, width // groups, 2 * half), lambda i: (0, i, 0)),
            pl.BlockSpec((local, half // groups, width), lambda i: (0, i, 0)),
            VMEM,
        ],
        deps=(token,), us=12, name="widen",
    )
    return (
        output,
        grad_inputs,
        small_two[:, 0],
        *two,
        *one,
        small_one[:, experts],
        small_one[:, :experts],
        *full,
    )


def solution(mesh):
    tokens = P(("group", "expert"), None)
    experts = P("expert", None, None)
    shares = P("group", None)
    return jax.shard_map(
        on_device,
        mesh=mesh,
        in_specs=(
            tokens, P(), P(), P(), P(), P(), P(), P(), experts, experts,
            P(("group", "expert")), tokens, tokens, tokens,
        ),
        out_specs=(
            tokens, tokens, P("group"), shares, shares, shares, shares, P("group"), shares,
            experts, experts,
        ),
        check_vma=False,
    )
```

```python
import functools

import jax
import jax.numpy as jnp
from jax import lax
from jax.experimental import pallas as pl
from jax.experimental.pallas import tpu as pltpu
from jax.sharding import PartitionSpec as P

QUERY_HEADS = 16
KEY_VALUE_HEADS = 8
HEAD_DIMENSION = 64
PAIR = 2 * HEAD_DIMENSION
EPS = 1e-05
UNROUTED = 1 << 20
LANES = 128
SCALE = HEAD_DIMENSION ** (-0.5)

bf16 = jnp.bfloat16
f32 = jnp.float32
VMEM = pl.BlockSpec(memory_space=pltpu.VMEM)
SMEM = pl.BlockSpec(memory_space=pltpu.SMEM)
ANY = pl.BlockSpec(memory_space=pl.ANY)
HELD = pl.BlockSpec(memory_space=pltpu.HBM)
COST = 3600000
TOKEN = ((8, LANES), f32)


def mm(left, right, dims=((1,), (0,))):
    return lax.dot_general(left, right, (dims, ((), ())), preferred_element_type=f32)


def call(kernel, outs, *args, smem=0, deps=(), specs=None, out_specs=None, grid=None, prefetch=0, scratch=(), vmem=56, alias=None, us=4, name=None):
    outs = [(pltpu.HBM if vmem > 32 else jax.ShapeDtypeStruct)(s, d) for s, d in outs]
    taken = len(args)

    def body(*refs):
        kernel(*refs[:taken], *refs[taken + len(deps) :])

    in_specs = (specs or [SMEM] * smem + [VMEM] * (taken - smem)) + [HELD] * len(deps)
    out_specs = out_specs or [VMEM] * len(outs)
    if prefetch:
        placed = dict(
            grid_spec=pltpu.PrefetchScalarGridSpec(
                num_scalar_prefetch=prefetch, grid=grid, in_specs=in_specs, out_specs=out_specs, scratch_shapes=list(scratch)
            )
        )
    else:
        placed = dict(in_specs=in_specs, out_specs=out_specs, scratch_shapes=list(scratch))
        if grid:
            placed["grid"] = grid
    return pl.pallas_call(
        body,
        out_shape=outs,
        compiler_params=pltpu.CompilerParams(vmem_limit_bytes=vmem * 1024 * 1024),
        cost_estimate=pl.CostEstimate(flops=0, bytes_accessed=us * COST, transcendentals=0),
        input_output_aliases=alias or {},
        name=name,
        **placed,
    )(*args, *deps)


def low_lanes(rows):
    return lax.broadcasted_iota(jnp.int32, (rows, PAIR), 1) < HEAD_DIMENSION


def stack_heads(pair, low):
    pair = pair.astype(f32)
    return jnp.concatenate([jnp.where(low, pair, 0.0), jnp.where(low, 0.0, pair)], 0).astype(bf16)


def allowed_keys(rows, length):
    shape = (2 * rows, rows)
    query = lax.broadcasted_iota(jnp.int32, shape, 0)
    query = jnp.where(query >= rows, query - rows, query)
    key = lax.broadcasted_iota(jnp.int32, shape, 1)
    return (key <= query) & (key < length)


def pack_rows(field, blocks):
    per = field.shape[0] // blocks
    return jnp.concatenate([field[c * per : (c + 1) * per] for c in range(blocks)], 1)


def places_and_ranks(length, routes_ref, ranks_ref, experts, capacity):
    picks, rows = routes_ref.shape
    expert = lax.broadcasted_iota(jnp.int32, (LANES, rows), 0)
    table = jnp.full((LANES, rows), UNROUTED, jnp.int32)
    for k in range(picks):
        table = jnp.where(expert == routes_ref[k : k + 1, :], ranks_ref[k : k + 1, :], table)
    token = lax.broadcasted_iota(jnp.int32, (LANES, rows), 1)
    table = jnp.where(token < length, table, UNROUTED).astype(f32)
    columns = table.T
    places = []
    for e in range(experts):
        row = table[e : e + 1]
        before = jnp.sum(jnp.where(columns[:, e : e + 1] < row, 1.0, 0.0), 0, keepdims=True)
        places.append(jnp.where((row < UNROUTED) & (before < capacity), before, -1.0))
    return jnp.concatenate(places, 0), table[:experts] < UNROUTED


def dense_forward(
    capacity, len_ref, x_ref, g1_ref, wq_ref, wk_ref, wv_ref, wo_ref, g2_ref, wr_ref, routes_ref, ranks_ref,
    n1_ref, q_ref, kk_ref, vv_ref, lse_ref, mixed_ref, res_ref, pack_ref, gate_ref,
):
    rows = x_ref.shape[0]
    x = x_ref[...].astype(f32)
    inverse = lax.rsqrt(jnp.mean(x * x, -1, keepdims=True) + EPS)
    n1 = (x * inverse * g1_ref[...]).astype(bf16)
    n1_ref[...] = n1
    q_ref[...] = mm(n1, wq_ref[...]).astype(bf16)
    low = low_lanes(rows)
    for weight_ref, twice_ref in ((wk_ref, kk_ref), (wv_ref, vv_ref)):
        both = mm(n1, weight_ref[...])
        for j in range(KEY_VALUE_HEADS // 2):
            block = both[:, j * PAIR : (j + 1) * PAIR]
            rolled = pltpu.roll(block, HEAD_DIMENSION, 1)
            twice_ref[:, 2 * j * PAIR : (2 * j + 1) * PAIR] = jnp.where(low, block, rolled).astype(bf16)
            twice_ref[:, (2 * j + 1) * PAIR : (2 * j + 2) * PAIR] = jnp.where(low, rolled, block).astype(bf16)
    allowed = allowed_keys(rows, len_ref[0])
    lane = lax.broadcasted_iota(jnp.int32, (rows, LANES), 1)
    totals = jnp.zeros((rows, LANES), f32)
    for h in range(KEY_VALUE_HEADS):
        cols = slice(h * PAIR, (h + 1) * PAIR)
        scores = mm(stack_heads(q_ref[:, cols], low), kk_ref[:, cols], ((1,), (1,))) * SCALE
        scores = jnp.where(allowed, scores, -1e30)
        top = jnp.max(scores, -1, keepdims=True)
        raised = jnp.exp(scores - top)
        total = jnp.sum(raised, -1, keepdims=True)
        probs = (raised / total).astype(bf16)
        mixed = mm(probs, vv_ref[:, cols])
        mixed_ref[:, cols] = jnp.where(low, mixed[:rows], mixed[rows:]).astype(bf16)
        logs = top + jnp.log(total)
        totals = jnp.where(lane == 2 * h, logs[:rows], totals)
        totals = jnp.where(lane == 2 * h + 1, logs[rows:], totals)
    lse_ref[...] = totals
    residual = x + mm(mixed_ref[...], wo_ref[...])
    res_ref[...] = residual
    inverse = lax.rsqrt(jnp.mean(residual * residual, -1, keepdims=True) + EPS)
    n2 = (residual * inverse * g2_ref[...]).astype(bf16)
    pack_ref[:rows, :] = n2
    logits = mm(wr_ref[...], n2, ((1,), (1,)))
    places, routed = places_and_ranks(len_ref[0], routes_ref, ranks_ref, wr_ref.shape[0], capacity)
    top = jnp.max(jnp.where(routed, logits, -jnp.inf), 0, keepdims=True)
    raised = jnp.where(routed, jnp.exp(jnp.where(routed, logits - top, 0.0)), 0.0)
    total = jnp.sum(raised, 0, keepdims=True)
    gates = raised / jnp.where(total > 0.0, total, 1.0)
    gate_ref[...] = gates
    high = gates.astype(bf16).astype(f32)
    blocks = x_ref.shape[1] // rows
    fields = [pack_rows(field, blocks) for field in (places, high, gates - high)]
    fill = pack_ref.shape[0] - rows - sum(field.shape[0] for field in fields)
    if fill:
        fields.append(jnp.zeros((fill, x_ref.shape[1]), f32))
    pack_ref[rows:, :] = jnp.concatenate(fields, 0).astype(bf16)


def unpack(pack_ref, expert, experts, seq):
    extra, width = pack_ref.shape[0] - seq, pack_ref.shape[1]
    per = experts * seq // width
    at = expert // per
    row = expert - at * per
    block = pack_ref[seq:, pl.ds(pl.multiple_of(at * seq, seq), seq)].astype(f32)
    index = lax.broadcasted_iota(jnp.int32, (extra, seq), 0)
    place = jnp.sum(jnp.where(index == row, block, 0.0), 0, keepdims=True)
    gate = jnp.sum(
        jnp.where((index == per + row) | (index == 2 * per + row), block, 0.0), 0, keepdims=True
    )
    return place, gate


def expert_forward(local, capacity, owners, id_ref, *refs):
    tokens = refs[:owners]
    (win_ref, wout_ref, sent_ref, hidden_ref, slope_ref, silu_ref, wret_ref, weight) = refs[owners:]
    width, half = win_ref.shape[1], wout_ref.shape[1]
    seq = width // local
    expert = id_ref[0] * local + pl.program_id(0)
    place = lax.broadcasted_iota(jnp.int32, (capacity, seq), 0).astype(f32)
    for d in range(owners):
        span = slice(d * capacity, (d + 1) * capacity)
        row, gate = unpack(tokens[d], expert, owners * local, seq)
        hit = place == row
        one = jnp.where(hit, 1.0, 0.0).astype(bf16)
        sent_ref[0, span, :] = mm(one, tokens[d][:seq, :]).astype(bf16)
        weight[span, :] = jnp.sum(jnp.where(hit, gate, 0.0), 1, keepdims=True)
    tile = 256
    for t in range(0, half, tile):
        gate = mm(sent_ref[0], win_ref[0, :, t : t + tile])
        up = mm(sent_ref[0], win_ref[0, :, half + t : half + t + tile])
        sig = jax.nn.sigmoid(gate)
        act = gate * sig
        silu_ref[0, :, t : t + tile] = act.astype(bf16)
        slope_ref[0, :, t : t + tile] = (up * sig * (1.0 + gate * (1.0 - sig))).astype(bf16)
        hidden_ref[0, :, t : t + tile] = (act * up).astype(bf16)
    for t in range(0, width, tile):
        cols = slice(t, t + tile)
        returned = mm(hidden_ref[0], wout_ref[0, :, cols]).astype(bf16).astype(f32)
        wret_ref[0, :, cols] = (weight[...] * returned).astype(bf16)


def expert_backward(first, split, local, capacity, owners, id_ref, *refs):
    tokens, cots = refs[:owners], refs[owners : 2 * owners]
    rest = refs[2 * owners :]
    sent_ref, hidden_ref, slope_ref, silu_ref, win_ref, wout_ref = rest[:6]
    sums, (gpre_ref, gg_ref, crow, weight, gret) = rest[6:-5], rest[-5:]
    gpre = gpre_ref.at[0]
    width, half = win_ref.shape[1], wout_ref.shape[1]
    seq = cots[0].shape[0]
    expert = id_ref[0] * local + first + pl.program_id(0)
    place = lax.broadcasted_iota(jnp.int32, (capacity, seq), 0).astype(f32)
    places = []
    for d in range(owners):
        span = slice(d * capacity, (d + 1) * capacity)
        row, gate = unpack(tokens[d], expert, owners * local, seq)
        places.append(row)
        hit = place == row
        one = jnp.where(hit, 1.0, 0.0).astype(bf16)
        weight[span, :] = jnp.sum(jnp.where(hit, gate, 0.0), 1, keepdims=True)
        rows = mm(one, cots[d][...])
        crow[span, :] = rows.astype(bf16)
        gret[span, :] = (weight[span, :] * rows).astype(bf16)
    tile = 256
    dots = jnp.zeros((owners * capacity, 1), f32)
    for t in range(0, half, tile):
        cols = slice(t, t + tile)
        ghid = mm(crow[...], wout_ref[0, cols, :], ((1,), (1,)))
        dots = dots + jnp.sum(ghid * hidden_ref[0, :, cols].astype(f32), 1, keepdims=True)
        ghid = ghid * weight[...]
        gpre[:, cols] = (ghid * slope_ref[0, :, cols].astype(f32)).astype(bf16)
        gpre[:, half + t : half + t + tile] = (ghid * silu_ref[0, :, cols].astype(f32)).astype(bf16)
    for d in range(owners):
        part = dots[d * capacity : (d + 1) * capacity]
        gg_ref[0, d : d + 1, :] = jnp.sum(jnp.where(place == places[d], part, 0.0), 0, keepdims=True)
    pieces = sums[0].shape[0] * len(sums)
    base = 0
    for left, right in ((sent_ref, gpre), (hidden_ref, gret)):
        size = left.shape[2]
        step = size // pieces
        for t in range(0, width, tile):
            made = mm(left[0], right[:, t : t + tile], ((0,), (0,)))
            for q in range(pieces // len(sums)):
                if split:
                    low = made[2 * q * step : (2 * q + 1) * step]
                    high = made[(2 * q + 1) * step : (2 * q + 2) * step]
                    mine = id_ref[1] == 0
                    sums[0][q, base : base + step, t : t + tile] = jnp.where(mine, low, high).astype(bf16)
                    sums[1][q, base : base + step, t : t + tile] = jnp.where(mine, high, low).astype(bf16)
                else:
                    sums[0][q, base : base + step, t : t + tile] = made[q * step : (q + 1) * step].astype(bf16)
        base += step


def combine_kernel(local, capacity, owners, counts, id_ref, *refs):
    tokens = refs[:owners]
    rest = refs[owners:]
    rows_in = [(r, i) for r in rest[: counts[0]] for i in range(r.shape[0])]
    dots = [(r, i) for r in rest[counts[0] : counts[0] + counts[1]] for i in range(r.shape[0])]
    parts, columns = rest[sum(counts) : -1], rest[-1]
    width = parts[0].shape[-1]
    seq = width // local
    d = pl.program_id(0)

    @pl.when(d == 0)
    def _():
        first = id_ref[0] * local
        for t in range(owners):
            table = [unpack(tokens[t], first + j, owners * local, seq)[0] for j in range(local)]
            table.append(jnp.zeros((LANES - local, seq), f32))
            columns[t] = jnp.concatenate(table, 0).T.astype(jnp.int32)

    lane = lax.broadcasted_iota(jnp.int32, (seq, local * capacity), 1)
    hit = None
    for j in range(local):
        col = columns[d, :, j : j + 1]
        same = lane == jnp.where(col < 0, -1, col + j * capacity)
        hit = same if hit is None else hit | same
    one = jnp.where(hit, 1.0, 0.0).astype(bf16)
    stacked = jnp.concatenate([r[i] for r, i in rows_in], 0)
    made = mm(one, stacked).astype(bf16)
    if dots:
        line = jnp.concatenate([r[i, pl.ds(d, 1), :] for r, i in dots], 1)
        high = line.astype(bf16).astype(f32)
        index = lax.broadcasted_iota(jnp.int32, (parts[0].shape[0] - seq, width), 0)
        mine = jnp.where(index == id_ref[0], high, 0.0)
        mine = jnp.where(index == owners + id_ref[0], line - high, mine)
    if len(parts) == 1:
        parts[0][lax.rem(id_ref[0] + owners - d, owners)] = made
    for t in range(len(parts) if dots else 0):

        @pl.when(d == t)
        def _():
            parts[t][:seq, :] = made
            parts[t][seq:, :] = mine.astype(bf16)


def rows_kernel(local, capacity, owners, id_ref, *refs):
    tokens, (gpre_ref, win_ref, dots_ref), parts, rows = (
        refs[:owners], refs[owners : owners + 3], refs[owners + 3 : -1], refs[-1]
    )
    width = win_ref.shape[1]
    seq = width // local
    step = pl.program_id(0)
    for t in range(0, width, 256):
        rows[step, :, t : t + 256] = mm(gpre_ref[0], win_ref[0, t : t + 256, :], ((1,), (1,))).astype(bf16)

    @pl.when(step == local - 1)
    def _():
        first = id_ref[0] * local
        lane = lax.broadcasted_iota(jnp.int32, (seq, local * capacity), 1)
        index = lax.broadcasted_iota(jnp.int32, (parts[0].shape[0] - seq, width), 0)
        for d in range(owners):
            table = [unpack(tokens[d], first + j, owners * local, seq)[0] for j in range(local)]
            table.append(jnp.zeros((LANES - local, seq), f32))
            columns = jnp.concatenate(table, 0).T.astype(jnp.int32)
            hit = None
            for j in range(local):
                col = columns[:, j : j + 1]
                same = lane == jnp.where(col < 0, -1, col + j * capacity)
                hit = same if hit is None else hit | same
            one = jnp.where(hit, 1.0, 0.0).astype(bf16)
            span = slice(d * capacity, (d + 1) * capacity)
            stacked = jnp.concatenate([rows[j, span, :] for j in range(local)], 0)
            parts[d][:seq, :] = mm(one, stacked).astype(bf16)
            line = jnp.concatenate([dots_ref[j, d : d + 1, :] for j in range(local)], 1)
            high = line.astype(bf16).astype(f32)
            mine = jnp.where(index == id_ref[0], high, 0.0)
            mine = jnp.where(index == owners + id_ref[0], line - high, mine)
            parts[d][seq:, :] = mine.astype(bf16)


def hop_kernel(*refs):
    pairs = len(refs) // 3
    for i in range(pairs):
        total = refs[i][...].astype(f32) + refs[pairs + i][...].astype(f32)
        refs[2 * pairs + i][...] = total.astype(bf16)


def halve_kernel(id_ref, keep_ref, recv_ref, keep_go_ref, recv_go_ref, own_ref, send_ref, token_ref):
    token_ref[...] = jnp.zeros_like(token_ref)
    own_ref[...] = (keep_ref[...].astype(f32) + recv_ref[...].astype(f32)).astype(own_ref.dtype)
    send_ref[...] = (keep_go_ref[...].astype(f32) + recv_go_ref[...].astype(f32)).astype(bf16)


def nothing_kernel(*refs):
    pass


def add_kernel(base_ref, parts_ref, out_ref, token_ref):
    total = base_ref[...]
    for i in range(parts_ref.shape[0]):
        total = total + parts_ref[i].astype(f32)
    out_ref[...] = total
    token_ref[...] = jnp.zeros_like(token_ref)


def spread_kernel(owners, id_ref, keep_ref, recv_ref, *refs):
    outs, token_ref, total = refs[:owners], refs[owners], refs[owners + 1]
    token_ref[...] = jnp.zeros_like(token_ref)
    block = outs[0].shape[0]
    for i in range(owners):
        span = slice(i * block, (i + 1) * block)
        total[i] = keep_ref[0, span, :].astype(f32) + recv_ref[0, span, :].astype(f32)
    for d in range(owners):
        outs[d][...] = total[lax.rem(id_ref[0] + d, owners)].astype(bf16)


def sum_kernel(*refs):
    total = refs[0][...].astype(f32)
    for ref in refs[1:-1]:
        total = total + ref[...].astype(f32)
    refs[-1][...] = total.astype(refs[-1].dtype)


def widen_kernel(in_ref, *refs):
    first_ref, second_ref, token_ref = refs[-3:]
    token_ref[...] = jnp.zeros_like(token_ref)
    count, rows, _ = first_ref.shape
    size = in_ref.shape[1] // count
    for j in range(count):
        first_ref[j] = in_ref[0, j * size : j * size + rows, :].astype(f32)
        second_ref[j] = in_ref[0, j * size + rows : (j + 1) * size, :].astype(f32)


def finish_kernel(owners, id_ref, *refs):
    blocks, outs, ordered = refs[:owners], refs[owners:-1], refs[-1]
    size = blocks[0].shape[0]
    for d in range(owners):
        ordered[lax.rem(id_ref[0] + owners - d, owners)] = blocks[d][...].astype(f32)
    for i in range(owners):
        col = 0
        for out in outs:
            cols = out.shape[1]
            out[i * size : (i + 1) * size, :] = ordered[i, :, col : col + cols]
            col += cols


def dense_backward(parts, owners, local, id_ref, len_ref, *refs):
    part_refs, refs = refs[:parts], refs[parts:]
    (gate_ref, x_ref, cot_ref, res_ref, n1_ref, pack_ref, q_ref, kk_ref, vv_ref, lse_ref, mixed_ref,
     wq_ref, wk_ref, wv_ref, wo_ref, wr_ref, g1_ref, g2_ref,
     gin_ref, keep_one, send_one, keep_two, send_two, gg_all, gmix, gq, gk, gv, acc) = refs
    rows, width = x_ref.shape
    core = id_ref[1]
    pieces = 2 * keep_one.shape[0]
    step = width // pieces

    def put(stream, offset, size):
        keep_ref, send_ref = stream
        for q in range(pieces // 2):
            lo = pl.multiple_of((2 * q + core) * step, step)
            hi = pl.multiple_of((2 * q + 1 - core) * step, step)
            keep_ref[q, :, offset : offset + size] = acc[pl.ds(lo, step), :size].astype(bf16)
            send_ref[q, :, offset : offset + size] = acc[pl.ds(hi, step), :size].astype(bf16)

    def weight_gradient(left, right, stream, offset):
        size = right.shape[1]
        tile = 256
        for t in range(0, size, tile):
            acc[:, t : t + tile] = mm(left[...], right[:, t : t + tile], ((0,), (0,)))
        put(stream, offset, size)

    tail = part_refs[0][rows:, :].astype(f32)
    for part_ref in part_refs[1:]:
        tail = tail + part_ref[rows:, :].astype(f32)
    lines = tail[:owners] + tail[owners : 2 * owners]
    for owner in range(owners):
        for j in range(local):
            gg_all[owner * local + j : owner * local + j + 1, :] = lines[owner : owner + 1, j * rows : (j + 1) * rows]
    gates = gate_ref[...]
    grad_gates = gg_all[...]
    mean = jnp.sum(gates * grad_gates, 0, keepdims=True)
    glog = (gates * (grad_gates - mean)).astype(bf16)
    grad = part_refs[0][:rows, :].astype(f32)
    for part_ref in part_refs[1:]:
        grad = grad + part_ref[:rows, :].astype(f32)
    grad = grad + mm(glog, wr_ref[...], ((0,), (0,)))
    grouter = mm(glog, pack_ref[:rows, :])
    residual = res_ref[...]
    inverse = lax.rsqrt(jnp.mean(residual * residual, -1, keepdims=True) + EPS)
    ggain_two = jnp.sum(grad * residual * inverse, 0, keepdims=True)
    scaled = grad * g2_ref[...]
    gres = cot_ref[...].astype(f32) + inverse * scaled - residual * inverse**3 * jnp.mean(
        scaled * residual, -1, keepdims=True
    )
    branch = gres.astype(bf16)
    gmix[...] = mm(branch, wo_ref[...], ((1,), (1,))).astype(bf16)
    gin_ref[...] = gres
    gq[...] = branch
    one, two = (keep_one, send_one), (keep_two, send_two)
    weight_gradient(mixed_ref, gq, one, 0)
    rest = LANES - 1 - grouter.shape[0]
    acc[:, :LANES] = jnp.concatenate([grouter, ggain_two, jnp.zeros((rest, width), f32)], 0).T
    put(one, width, LANES)
    low = low_lanes(rows)
    allowed = allowed_keys(rows, len_ref[0])
    held = None
    for h in range(KEY_VALUE_HEADS):
        cols = slice(h * PAIR, (h + 1) * PAIR)
        queries = stack_heads(q_ref[:, cols], low)
        upstream = stack_heads(gmix[:, cols], low)
        scores = mm(queries, kk_ref[:, cols], ((1,), (1,))) * SCALE
        logs = jnp.concatenate([lse_ref[:, 2 * h : 2 * h + 1], lse_ref[:, 2 * h + 1 : 2 * h + 2]], 0)
        probs = jnp.exp(jnp.where(allowed, scores, -1e30) - logs)
        gprobs = mm(upstream, vv_ref[:, cols], ((1,), (1,)))
        inner = jnp.sum(gprobs * probs, -1, keepdims=True)
        gscores = (probs * (gprobs - inner)).astype(bf16)
        gqueries = mm(gscores, kk_ref[:, cols]) * SCALE
        gq[:, cols] = jnp.where(low, gqueries[:rows], gqueries[rows:]).astype(bf16)
        gkey = mm(gscores, queries, ((0,), (0,))) * SCALE
        gvalue = mm(probs.astype(bf16), upstream, ((0,), (0,)))
        gkey = gkey + pltpu.roll(gkey, HEAD_DIMENSION, 1)
        gvalue = gvalue + pltpu.roll(gvalue, HEAD_DIMENSION, 1)
        if h % 2 == 0:
            held = (gkey, gvalue)
        else:
            both = slice((h // 2) * PAIR, (h // 2 + 1) * PAIR)
            gk[:, both] = jnp.where(low, held[0], gkey).astype(bf16)
            gv[:, both] = jnp.where(low, held[1], gvalue).astype(bf16)
    col = 0
    for right in (gq, gk, gv):
        weight_gradient(n1_ref, right, two, col)
        col += right.shape[1]
    grad = mm(gq[...], wq_ref[...], ((1,), (1,)))
    grad = grad + mm(gk[...], wk_ref[...], ((1,), (1,)))
    grad = grad + mm(gv[...], wv_ref[...], ((1,), (1,)))
    x = x_ref[...].astype(f32)
    inverse = lax.rsqrt(jnp.mean(x * x, -1, keepdims=True) + EPS)
    ggain_one = jnp.sum(grad * x * inverse, 0, keepdims=True)
    scaled = grad * g1_ref[...]
    gin_ref[...] = gin_ref[...] + inverse * scaled - x * inverse**3 * jnp.mean(
        scaled * x, -1, keepdims=True
    )
    acc[:, :LANES] = jnp.concatenate([ggain_one, jnp.zeros((LANES - 1, width), f32)], 0).T
    put(two, col, LANES)


def on_device(
    inputs, gain_one, query_matrix, key_matrix, value_matrix, w_attn_out, gain_two, w_router,
    expert_in, expert_out, lengths, routes, ranks, cotangent,
):
    seq, width = inputs.shape
    picks = routes.shape[1]
    experts = w_router.shape[1]
    local = expert_in.shape[0]
    half = expert_out.shape[1]
    owners = lax.axis_size("expert")
    groups = lax.axis_size("group")
    steps = groups.bit_length() - 2
    capacity = (5 * seq * picks + 4 * experts - 1) // (4 * experts)
    places = owners * capacity
    z = lax.axis_index("expert").astype(jnp.int32)
    g = lax.axis_index("group").astype(jnp.int32)
    ids = jnp.stack([z, g % 2, g // 2])

    def ring(x, d):
        return lax.ppermute(x, "expert", [(i, (i + d) % owners) for i in range(owners)])

    def swap_cores(x):
        return lax.ppermute(x, "group", [(i, i ^ 1) for i in range(groups)])

    def swap(x, stage):
        return lax.ppermute(
            x, "group", [(i, i ^ (1 << (steps - stage if i % 2 else 1 + stage))) for i in range(groups)]
        )

    def near(x):
        return [ring(x, 1), ring(x, -1)] if owners == 4 else [ring(x, d) for d in range(1, owners)]

    def far(x, got):
        if owners != 4:
            return [x, *got]
        before, after = got
        up = lax.ppermute(before, "expert", [(1, 2), (2, 3)])
        down = lax.ppermute(after, "expert", [(1, 0), (2, 1)])
        return [x, before, jnp.where(z >= 2, up, down), after]

    def halve(keep, recv, stage, name, deps=(), us=4):
        pieces, *rest = keep.shape
        half = pieces // 2
        tile = rest[0] // 2
        core, mine = g % 2, g // 2
        index = jnp.arange(half, dtype=jnp.int32)
        low = (mine >> stage) & 1
        high = (mine >> (steps - 1 - stage)) & 1
        stay = jnp.where(core == 0, 2 * index + low, index + high * half)
        go = jnp.where(core == 0, 2 * index + 1 - low, index + (1 - high) * half)
        block = (1, tile, rest[1])
        here = pl.BlockSpec(block, lambda i, t, which: (which[0, i], t, 0))
        there = pl.BlockSpec(block, lambda i, t, which: (which[1, i], t, 0))
        made = pl.BlockSpec(block, lambda i, t, which: (i, t, 0))
        return call(
            halve_kernel, [((half, *rest), bf16), ((half, *rest), bf16), TOKEN],
            jnp.stack([stay, go]), keep, recv, keep, recv,
            prefetch=1, grid=(half, 2), specs=[here, here, there, there], out_specs=[made, made, VMEM], deps=deps, vmem=16, us=us, name=name,
        )

    def behind(arrays, deps, name):
        shapes = [(a.shape, a.dtype) for a in arrays]
        return call(
            nothing_kernel, shapes, *arrays, specs=[ANY] * len(arrays), out_specs=[ANY] * len(arrays), deps=deps,
            alias={i: i for i in range(len(arrays))}, us=0, name=name,
        )

    cot_got = near(cotangent)
    gain_one = gain_one.reshape(1, width)
    gain_two = gain_two.reshape(1, width)
    router = w_router.T
    extra = -(-3 * experts * seq // width // 16) * 16

    n1, q, kk, vv, lse, mixed, residual, pack, gates = call(
        functools.partial(dense_forward, capacity),
        [((seq, width), bf16)] * 4
        + [((seq, LANES), f32), ((seq, width), bf16), ((seq, width), f32), ((seq + extra, width), bf16), ((experts, seq), f32)],
        lengths, inputs, gain_one, query_matrix, key_matrix, value_matrix, w_attn_out, gain_two, router, routes.T, ranks.T,
        smem=1, us=9, name="dense_forward",
    )
    (pack,) = behind([pack], tuple(cot_got), "tokens_go")
    packs = far(pack, near(pack))
    cot_got = behind(cot_got, (packs[owners // 2],), "cotangents_go")
    cots = far(cotangent, cot_got)
    piece = (width + half) // groups

    def rows_of(n):
        return pl.BlockSpec((1, places, n), lambda i: (i, 0, 0))

    def weights(first):
        return [
            pl.BlockSpec((1, width, 2 * half), lambda i: (first + i, 0, 0)),
            pl.BlockSpec((1, half, width), lambda i: (first + i, 0, 0)),
        ]

    sent, hidden, slope, silu, wret = call(
        functools.partial(expert_forward, local, capacity, owners),
        [
            ((local, places, width), bf16),
            ((local, places, half), bf16),
            ((local, places, half), bf16),
            ((local, places, half), bf16),
            ((local, places, width), bf16),
        ],
        ids, *packs, expert_in, expert_out,
        grid=(local,), specs=[SMEM] + [VMEM] * owners + weights(0),
        out_specs=[rows_of(width), rows_of(half), rows_of(half), rows_of(half), rows_of(width)],
        scratch=[pltpu.VMEM((places, 1), f32)], us=17, name="expert_forward",
    )

    tail = -(-2 * owners // 16) * 16

    def backward(first, count, split, deps=()):
        def of(n):
            return pl.BlockSpec((1, places, n), lambda i: (first + i, 0, 0))

        if split:
            sums = [((groups // 2, count * piece, width), bf16)] * 2
            sum_specs = [pl.BlockSpec((groups // 2, piece, width), lambda i: (0, i, 0))] * 2
        else:
            sums = [((groups, count * piece, width), bf16)]
            sum_specs = [pl.BlockSpec((groups, piece, width), lambda i: (0, i, 0))]
        return call(
            functools.partial(expert_backward, first, split, local, capacity, owners),
            sums + [((count, places, 2 * half), bf16), ((count, owners, seq), f32)],
            ids, *packs, *cots, sent, hidden, slope, silu, expert_in, expert_out,
            grid=(count,),
            specs=[SMEM] + [VMEM] * (2 * owners) + [of(width), of(half), of(half), of(half)] + weights(first),
            out_specs=sum_specs + [rows_of(2 * half), pl.BlockSpec((1, owners, seq), lambda i: (i, 0, 0))],
            scratch=[
                pltpu.VMEM((places, width), bf16),
                pltpu.VMEM((places, 1), f32),
                pltpu.VMEM((places, width), bf16),
            ],
            deps=deps, us=8 * count, name=f"expert_backward{first}",
        )

    def combine(rows, dots, deps, name, us=8):
        outs = [((seq + tail, width), bf16)] * owners if dots else [((owners, seq, width), bf16)]
        return call(
            functools.partial(combine_kernel, local, capacity, owners, (len(rows), len(dots))),
            outs, ids, *packs, *rows, *dots, grid=(owners,),
            specs=[SMEM] + [VMEM] * owners
            + [pl.BlockSpec((r.shape[0], capacity, width), lambda d: (0, d, 0)) for r in rows]
            + [VMEM] * len(dots),
            scratch=[pltpu.VMEM((owners, seq, LANES), jnp.int32)],
            deps=deps, us=us, name=name,
        )

    sums, *grads = backward(0, local, False)
    mine = lax.psum_scatter(sums, "group", scatter_dimension=0, tiled=False)
    parts = call(
        functools.partial(rows_kernel, local, capacity, owners),
        [((seq + tail, width), bf16)] * owners,
        ids, *packs, grads[0], expert_in, grads[1],
        grid=(local,), specs=[SMEM] + [VMEM] * owners + [rows_of(2 * half), weights(0)[0], VMEM],
        scratch=[pltpu.VMEM((local, places, width), bf16)], us=14, name="expert_rows",
    )
    if owners == 4:
        near_by = [
            lax.ppermute(parts[2], "expert", [(2, 1), (3, 2)]),
            lax.ppermute(parts[2], "expert", [(0, 1), (1, 2)]),
        ]
        joined = call(hop_kernel, [(parts[0].shape, bf16)] * 2, parts[1], parts[3], *near_by, us=2, name="hop")
        grad_parts = [parts[0], ring(joined[0], -1), ring(joined[1], 1)]
    else:
        joined = parts
        grad_parts = [parts[0]] + [ring(parts[d], -d) for d in range(1, owners)]
    (owned,) = combine([wret], [], (joined[0],), "combine_out")
    deps = (owned,)

    def to_owners(x):
        return lax.all_to_all(x, "expert", split_axis=0, concat_axis=0, tiled=True)

    sizes = ((width, LANES), (width, key_matrix.shape[1], value_matrix.shape[1], LANES))
    grad_inputs, keep_one, send_one, keep_two, send_two = call(
        functools.partial(dense_backward, len(grad_parts), owners, local),
        [((seq, width), f32)] + [((groups // 2, width // groups, sum(cols)), bf16) for cols in sizes for _ in range(2)],
        ids, lengths, *grad_parts, gates, inputs, cotangent, residual, n1, pack, q, kk, vv, lse, mixed,
        query_matrix, key_matrix, value_matrix, w_attn_out, router, gain_one, gain_two,
        smem=2, deps=deps, us=18, name="dense_backward",
        scratch=[
            pltpu.VMEM((experts, seq), f32),
            pltpu.VMEM((seq, width), bf16),
            pltpu.VMEM((seq, width), bf16),
            pltpu.VMEM((seq, key_matrix.shape[1]), bf16),
            pltpu.VMEM((seq, value_matrix.shape[1]), bf16),
            pltpu.VMEM((width, width), f32),
        ],
    )
    rows = width // groups
    block = rows // owners
    recv_one, recv_two = swap_cores(send_one), swap_cores(send_two)
    (owned,) = behind([owned], (send_one,), "returned_go")
    out_parts = to_owners(owned)
    keep_one, send_one, token = halve(keep_one, recv_one, 0, "one_halve0", (owned,))
    recv_one = swap(send_one, 0)
    keep_two, send_two, token = halve(keep_two, recv_two, 0, "two_halve0", (token,))
    recv_two = swap(send_two, 0)
    (mine,) = behind([mine], (recv_one, token), "gather_go")
    gathered = lax.all_gather(mine, "group", axis=0, tiled=False)
    token = mine
    def spread(keep, recv, name, deps):
        cols = keep.shape[2]
        return call(
            functools.partial(spread_kernel, owners), [((block, cols), bf16)] * owners + [TOKEN], ids, keep, recv,
            smem=1, deps=deps, vmem=16, us=2, name=name, scratch=[pltpu.VMEM((owners, block, cols), f32)],
        )

    def total(blocks, name, deps):
        (made,) = call(sum_kernel, [(blocks[0].shape, bf16)], *blocks, deps=deps, vmem=16, us=2, name=name)
        return [made] + [ring(made, d) for d in range(1, owners)]

    def finish(shares, cols, name, deps):
        return call(
            functools.partial(finish_kernel, owners), [((rows, c), f32) for c in cols],
            ids, *shares, smem=1, deps=deps, vmem=16, us=2, name=name,
            scratch=[pltpu.VMEM((owners, block, sum(cols)), f32)],
        )

    for stage in range(1, steps):
        keep_one, send_one, token = halve(keep_one, recv_one, stage, f"one_halve{stage}", (token,))
        recv_one = swap(send_one, stage)
    *blocks_one, token = spread(keep_one, recv_one, "one_spread", (token,))
    blocks_one = [blocks_one[0]] + [ring(blocks_one[d], d) for d in range(1, owners)]
    for stage in range(1, steps):
        keep_two, send_two, token = halve(keep_two, recv_two, stage, f"two_halve{stage}", (token,))
        recv_two = swap(send_two, stage)
    shares_one = total(blocks_one, "one_sum", (token,))
    *blocks_two, token = spread(keep_two, recv_two, "two_spread", (shares_one[0],))
    blocks_two = [blocks_two[0]] + [ring(blocks_two[d], d) for d in range(1, owners)]
    spec = pl.BlockSpec((seq // 4, width), lambda t: (t, 0))
    output, token = call(
        add_kernel, [((seq, width), f32), TOKEN], residual, out_parts, grid=(4,),
        specs=[spec, pl.BlockSpec((owners, seq // 4, width), lambda t: (0, t, 0))], out_specs=[spec, VMEM],
        deps=(token,), us=4, name="output",
    )
    shares_two = total(blocks_two, "two_sum", (token,))
    *one, small_one = finish(shares_one, sizes[0], "one_finish", (shares_two[0],))
    *two, small_two = finish(shares_two, sizes[1], "two_finish", (small_one,))
    token = small_two
    *full, _ = call(
        widen_kernel,
        [((local, width, 2 * half), f32), ((local, half, width), f32), TOKEN],
        gathered,
        grid=(groups,),
        specs=[pl.BlockSpec((1, local * piece, width), lambda i: (i, 0, 0))],
        out_specs=[
            pl.BlockSpec((local, width // groups, 2 * half), lambda i: (0, i, 0)),
            pl.BlockSpec((local, half // groups, width), lambda i: (0, i, 0)),
            VMEM,
        ],
        deps=(token,), us=12, name="widen",
    )
    return (
        output,
        grad_inputs,
        small_two[:, 0],
        *two,
        *one,
        small_one[:, experts],
        small_one[:, :experts],
        *full,
    )


def solution(mesh):
    tokens = P(("group", "expert"), None)
    experts = P("expert", None, None)
    shares = P("group", None)
    return jax.shard_map(
        on_device,
        mesh=mesh,
        in_specs=(
            tokens, P(), P(), P(), P(), P(), P(), P(), experts, experts,
            P(("group", "expert")), tokens, tokens, tokens,
        ),
        out_specs=(
            tokens, tokens, P("group"), shares, shares, shares, shares, P("group"), shares,
            experts, experts,
        ),
        check_vma=False,
    )
```

```python
import functools

import jax
import jax.numpy as jnp
from jax import lax
from jax.experimental import pallas as pl
from jax.experimental.pallas import tpu as pltpu
from jax.sharding import PartitionSpec as P

QUERY_HEADS = 16
KEY_VALUE_HEADS = 8
HEAD_DIMENSION = 64
PAIR = 2 * HEAD_DIMENSION
EPS = 1e-05
UNROUTED = 1 << 20
LANES = 128
SCALE = HEAD_DIMENSION ** (-0.5)

bf16 = jnp.bfloat16
f32 = jnp.float32
VMEM = pl.BlockSpec(memory_space=pltpu.VMEM)
SMEM = pl.BlockSpec(memory_space=pltpu.SMEM)
ANY = pl.BlockSpec(memory_space=pl.ANY)
HELD = pl.BlockSpec(memory_space=pltpu.HBM)
COST = 3600000
TOKEN = ((8, LANES), f32)


def mm(left, right, dims=((1,), (0,))):
    return lax.dot_general(left, right, (dims, ((), ())), preferred_element_type=f32)


def call(kernel, outs, *args, smem=0, deps=(), specs=None, out_specs=None, grid=None, prefetch=0, scratch=(), vmem=56, alias=None, us=4, name=None):
    outs = [(pltpu.HBM if vmem > 32 else jax.ShapeDtypeStruct)(s, d) for s, d in outs]
    taken = len(args)

    def body(*refs):
        kernel(*refs[:taken], *refs[taken + len(deps) :])

    in_specs = (specs or [SMEM] * smem + [VMEM] * (taken - smem)) + [HELD] * len(deps)
    out_specs = out_specs or [VMEM] * len(outs)
    if prefetch:
        placed = dict(
            grid_spec=pltpu.PrefetchScalarGridSpec(
                num_scalar_prefetch=prefetch, grid=grid, in_specs=in_specs, out_specs=out_specs, scratch_shapes=list(scratch)
            )
        )
    else:
        placed = dict(in_specs=in_specs, out_specs=out_specs, scratch_shapes=list(scratch))
        if grid:
            placed["grid"] = grid
    return pl.pallas_call(
        body,
        out_shape=outs,
        compiler_params=pltpu.CompilerParams(vmem_limit_bytes=vmem * 1024 * 1024),
        cost_estimate=pl.CostEstimate(flops=0, bytes_accessed=us * COST, transcendentals=0),
        input_output_aliases=alias or {},
        name=name,
        **placed,
    )(*args, *deps)


def low_lanes(rows):
    return lax.broadcasted_iota(jnp.int32, (rows, PAIR), 1) < HEAD_DIMENSION


def stack_heads(pair, low):
    pair = pair.astype(f32)
    return jnp.concatenate([jnp.where(low, pair, 0.0), jnp.where(low, 0.0, pair)], 0).astype(bf16)


def allowed_keys(rows, length):
    shape = (2 * rows, rows)
    query = lax.broadcasted_iota(jnp.int32, shape, 0)
    query = jnp.where(query >= rows, query - rows, query)
    key = lax.broadcasted_iota(jnp.int32, shape, 1)
    return (key <= query) & (key < length)


def pack_rows(field, blocks):
    per = field.shape[0] // blocks
    return jnp.concatenate([field[c * per : (c + 1) * per] for c in range(blocks)], 1)


def places_and_ranks(length, routes_ref, ranks_ref, experts, capacity):
    picks, rows = routes_ref.shape
    expert = lax.broadcasted_iota(jnp.int32, (LANES, rows), 0)
    table = jnp.full((LANES, rows), UNROUTED, jnp.int32)
    for k in range(picks):
        table = jnp.where(expert == routes_ref[k : k + 1, :], ranks_ref[k : k + 1, :], table)
    token = lax.broadcasted_iota(jnp.int32, (LANES, rows), 1)
    table = jnp.where(token < length, table, UNROUTED).astype(f32)
    columns = table.T
    places = []
    for e in range(experts):
        row = table[e : e + 1]
        before = jnp.sum(jnp.where(columns[:, e : e + 1] < row, 1.0, 0.0), 0, keepdims=True)
        places.append(jnp.where((row < UNROUTED) & (before < capacity), before, -1.0))
    return jnp.concatenate(places, 0), table[:experts] < UNROUTED


def dense_forward(
    capacity, len_ref, x_ref, g1_ref, wq_ref, wk_ref, wv_ref, wo_ref, g2_ref, wr_ref, routes_ref, ranks_ref,
    n1_ref, q_ref, kk_ref, vv_ref, lse_ref, mixed_ref, res_ref, pack_ref, gate_ref,
):
    rows = x_ref.shape[0]
    x = x_ref[...].astype(f32)
    inverse = lax.rsqrt(jnp.mean(x * x, -1, keepdims=True) + EPS)
    n1 = (x * inverse * g1_ref[...]).astype(bf16)
    n1_ref[...] = n1
    q_ref[...] = mm(n1, wq_ref[...]).astype(bf16)
    low = low_lanes(rows)
    for weight_ref, twice_ref in ((wk_ref, kk_ref), (wv_ref, vv_ref)):
        both = mm(n1, weight_ref[...])
        for j in range(KEY_VALUE_HEADS // 2):
            block = both[:, j * PAIR : (j + 1) * PAIR]
            rolled = pltpu.roll(block, HEAD_DIMENSION, 1)
            twice_ref[:, 2 * j * PAIR : (2 * j + 1) * PAIR] = jnp.where(low, block, rolled).astype(bf16)
            twice_ref[:, (2 * j + 1) * PAIR : (2 * j + 2) * PAIR] = jnp.where(low, rolled, block).astype(bf16)
    allowed = allowed_keys(rows, len_ref[0])
    lane = lax.broadcasted_iota(jnp.int32, (rows, LANES), 1)
    totals = jnp.zeros((rows, LANES), f32)
    for h in range(KEY_VALUE_HEADS):
        cols = slice(h * PAIR, (h + 1) * PAIR)
        scores = mm(stack_heads(q_ref[:, cols], low), kk_ref[:, cols], ((1,), (1,))) * SCALE
        scores = jnp.where(allowed, scores, -1e30)
        top = jnp.max(scores, -1, keepdims=True)
        raised = jnp.exp(scores - top)
        total = jnp.sum(raised, -1, keepdims=True)
        probs = (raised / total).astype(bf16)
        mixed = mm(probs, vv_ref[:, cols])
        mixed_ref[:, cols] = jnp.where(low, mixed[:rows], mixed[rows:]).astype(bf16)
        logs = top + jnp.log(total)
        totals = jnp.where(lane == 2 * h, logs[:rows], totals)
        totals = jnp.where(lane == 2 * h + 1, logs[rows:], totals)
    lse_ref[...] = totals
    residual = x + mm(mixed_ref[...], wo_ref[...])
    res_ref[...] = residual
    inverse = lax.rsqrt(jnp.mean(residual * residual, -1, keepdims=True) + EPS)
    n2 = (residual * inverse * g2_ref[...]).astype(bf16)
    pack_ref[:rows, :] = n2
    logits = mm(wr_ref[...], n2, ((1,), (1,)))
    places, routed = places_and_ranks(len_ref[0], routes_ref, ranks_ref, wr_ref.shape[0], capacity)
    top = jnp.max(jnp.where(routed, logits, -jnp.inf), 0, keepdims=True)
    raised = jnp.where(routed, jnp.exp(jnp.where(routed, logits - top, 0.0)), 0.0)
    total = jnp.sum(raised, 0, keepdims=True)
    gates = raised / jnp.where(total > 0.0, total, 1.0)
    gate_ref[...] = gates
    high = gates.astype(bf16).astype(f32)
    blocks = x_ref.shape[1] // rows
    fields = [pack_rows(field, blocks) for field in (places, high, gates - high)]
    fill = pack_ref.shape[0] - rows - sum(field.shape[0] for field in fields)
    if fill:
        fields.append(jnp.zeros((fill, x_ref.shape[1]), f32))
    pack_ref[rows:, :] = jnp.concatenate(fields, 0).astype(bf16)


def unpack(pack_ref, expert, experts, seq):
    extra, width = pack_ref.shape[0] - seq, pack_ref.shape[1]
    per = experts * seq // width
    at = expert // per
    row = expert - at * per
    block = pack_ref[seq:, pl.ds(pl.multiple_of(at * seq, seq), seq)].astype(f32)
    index = lax.broadcasted_iota(jnp.int32, (extra, seq), 0)
    place = jnp.sum(jnp.where(index == row, block, 0.0), 0, keepdims=True)
    gate = jnp.sum(
        jnp.where((index == per + row) | (index == 2 * per + row), block, 0.0), 0, keepdims=True
    )
    return place, gate


def expert_forward(local, capacity, owners, id_ref, *refs):
    tokens = refs[:owners]
    (win_ref, wout_ref, sent_ref, hidden_ref, slope_ref, silu_ref, wret_ref, weight) = refs[owners:]
    width, half = win_ref.shape[1], wout_ref.shape[1]
    seq = width // local
    expert = id_ref[0] * local + pl.program_id(0)
    place = lax.broadcasted_iota(jnp.int32, (capacity, seq), 0).astype(f32)
    for d in range(owners):
        span = slice(d * capacity, (d + 1) * capacity)
        row, gate = unpack(tokens[d], expert, owners * local, seq)
        hit = place == row
        one = jnp.where(hit, 1.0, 0.0).astype(bf16)
        sent_ref[0, span, :] = mm(one, tokens[d][:seq, :]).astype(bf16)
        weight[span, :] = jnp.sum(jnp.where(hit, gate, 0.0), 1, keepdims=True)
    tile = 256
    for t in range(0, half, tile):
        gate = mm(sent_ref[0], win_ref[0, :, t : t + tile])
        up = mm(sent_ref[0], win_ref[0, :, half + t : half + t + tile])
        sig = jax.nn.sigmoid(gate)
        act = gate * sig
        silu_ref[0, :, t : t + tile] = act.astype(bf16)
        slope_ref[0, :, t : t + tile] = (up * sig * (1.0 + gate * (1.0 - sig))).astype(bf16)
        hidden_ref[0, :, t : t + tile] = (act * up).astype(bf16)
    for t in range(0, width, tile):
        cols = slice(t, t + tile)
        returned = mm(hidden_ref[0], wout_ref[0, :, cols]).astype(bf16).astype(f32)
        wret_ref[0, :, cols] = (weight[...] * returned).astype(bf16)


def expert_backward(first, split, local, capacity, owners, id_ref, *refs):
    tokens, cots = refs[:owners], refs[owners : 2 * owners]
    rest = refs[2 * owners :]
    sent_ref, hidden_ref, slope_ref, silu_ref, win_ref, wout_ref = rest[:6]
    sums, (gpre_ref, gg_ref, crow, weight, gret) = rest[6:-5], rest[-5:]
    gpre = gpre_ref.at[0]
    width, half = win_ref.shape[1], wout_ref.shape[1]
    seq = cots[0].shape[0]
    expert = id_ref[0] * local + first + pl.program_id(0)
    place = lax.broadcasted_iota(jnp.int32, (capacity, seq), 0).astype(f32)
    places = []
    for d in range(owners):
        span = slice(d * capacity, (d + 1) * capacity)
        row, gate = unpack(tokens[d], expert, owners * local, seq)
        places.append(row)
        hit = place == row
        one = jnp.where(hit, 1.0, 0.0).astype(bf16)
        weight[span, :] = jnp.sum(jnp.where(hit, gate, 0.0), 1, keepdims=True)
        rows = mm(one, cots[d][...])
        crow[span, :] = rows.astype(bf16)
        gret[span, :] = (weight[span, :] * rows).astype(bf16)
    tile = 256
    dots = jnp.zeros((owners * capacity, 1), f32)
    for t in range(0, half, tile):
        cols = slice(t, t + tile)
        ghid = mm(crow[...], wout_ref[0, cols, :], ((1,), (1,)))
        dots = dots + jnp.sum(ghid * hidden_ref[0, :, cols].astype(f32), 1, keepdims=True)
        ghid = ghid * weight[...]
        gpre[:, cols] = (ghid * slope_ref[0, :, cols].astype(f32)).astype(bf16)
        gpre[:, half + t : half + t + tile] = (ghid * silu_ref[0, :, cols].astype(f32)).astype(bf16)
    for d in range(owners):
        part = dots[d * capacity : (d + 1) * capacity]
        gg_ref[0, d : d + 1, :] = jnp.sum(jnp.where(place == places[d], part, 0.0), 0, keepdims=True)
    pieces = sums[0].shape[0] * len(sums)
    base = 0
    for left, right in ((sent_ref, gpre), (hidden_ref, gret)):
        size = left.shape[2]
        step = size // pieces
        for t in range(0, width, tile):
            made = mm(left[0], right[:, t : t + tile], ((0,), (0,)))
            for q in range(pieces // len(sums)):
                if split:
                    low = made[2 * q * step : (2 * q + 1) * step]
                    high = made[(2 * q + 1) * step : (2 * q + 2) * step]
                    mine = id_ref[1] == 0
                    sums[0][q, base : base + step, t : t + tile] = jnp.where(mine, low, high).astype(bf16)
                    sums[1][q, base : base + step, t : t + tile] = jnp.where(mine, high, low).astype(bf16)
                else:
                    sums[0][q, base : base + step, t : t + tile] = made[q * step : (q + 1) * step].astype(bf16)
        base += step


def combine_kernel(local, capacity, owners, counts, id_ref, *refs):
    tokens = refs[:owners]
    rest = refs[owners:]
    rows_in = [(r, i) for r in rest[: counts[0]] for i in range(r.shape[0])]
    dots = [(r, i) for r in rest[counts[0] : counts[0] + counts[1]] for i in range(r.shape[0])]
    parts, columns = rest[sum(counts) : -1], rest[-1]
    width = parts[0].shape[-1]
    seq = width // local
    d = pl.program_id(0)

    @pl.when(d == 0)
    def _():
        first = id_ref[0] * local
        for t in range(owners):
            table = [unpack(tokens[t], first + j, owners * local, seq)[0] for j in range(local)]
            table.append(jnp.zeros((LANES - local, seq), f32))
            columns[t] = jnp.concatenate(table, 0).T.astype(jnp.int32)

    lane = lax.broadcasted_iota(jnp.int32, (seq, local * capacity), 1)
    hit = None
    for j in range(local):
        col = columns[d, :, j : j + 1]
        same = lane == jnp.where(col < 0, -1, col + j * capacity)
        hit = same if hit is None else hit | same
    one = jnp.where(hit, 1.0, 0.0).astype(bf16)
    stacked = jnp.concatenate([r[i] for r, i in rows_in], 0)
    made = mm(one, stacked).astype(bf16)
    if dots:
        line = jnp.concatenate([r[i, pl.ds(d, 1), :] for r, i in dots], 1)
        high = line.astype(bf16).astype(f32)
        index = lax.broadcasted_iota(jnp.int32, (parts[0].shape[0] - seq, width), 0)
        mine = jnp.where(index == id_ref[0], high, 0.0)
        mine = jnp.where(index == owners + id_ref[0], line - high, mine)
    if len(parts) == 1:
        parts[0][lax.rem(id_ref[0] + owners - d, owners)] = made
    for t in range(len(parts) if dots else 0):

        @pl.when(d == t)
        def _():
            parts[t][:seq, :] = made
            parts[t][seq:, :] = mine.astype(bf16)


def rows_kernel(local, capacity, owners, id_ref, *refs):
    tokens, (gpre_ref, win_ref, dots_ref), parts, rows = (
        refs[:owners], refs[owners : owners + 3], refs[owners + 3 : -1], refs[-1]
    )
    width = win_ref.shape[1]
    seq = width // local
    step = pl.program_id(0)
    for t in range(0, width, 256):
        rows[step, :, t : t + 256] = mm(gpre_ref[0], win_ref[0, t : t + 256, :], ((1,), (1,))).astype(bf16)

    @pl.when(step == local - 1)
    def _():
        first = id_ref[0] * local
        lane = lax.broadcasted_iota(jnp.int32, (seq, local * capacity), 1)
        index = lax.broadcasted_iota(jnp.int32, (parts[0].shape[0] - seq, width), 0)
        for d in range(owners):
            table = [unpack(tokens[d], first + j, owners * local, seq)[0] for j in range(local)]
            table.append(jnp.zeros((LANES - local, seq), f32))
            columns = jnp.concatenate(table, 0).T.astype(jnp.int32)
            hit = None
            for j in range(local):
                col = columns[:, j : j + 1]
                same = lane == jnp.where(col < 0, -1, col + j * capacity)
                hit = same if hit is None else hit | same
            one = jnp.where(hit, 1.0, 0.0).astype(bf16)
            span = slice(d * capacity, (d + 1) * capacity)
            stacked = jnp.concatenate([rows[j, span, :] for j in range(local)], 0)
            parts[d][:seq, :] = mm(one, stacked).astype(bf16)
            line = jnp.concatenate([dots_ref[j, d : d + 1, :] for j in range(local)], 1)
            high = line.astype(bf16).astype(f32)
            mine = jnp.where(index == id_ref[0], high, 0.0)
            mine = jnp.where(index == owners + id_ref[0], line - high, mine)
            parts[d][seq:, :] = mine.astype(bf16)


def hop_kernel(*refs):
    pairs = len(refs) // 3
    for i in range(pairs):
        total = refs[i][...].astype(f32) + refs[pairs + i][...].astype(f32)
        refs[2 * pairs + i][...] = total.astype(bf16)


def halve_kernel(id_ref, keep_ref, recv_ref, keep_go_ref, recv_go_ref, own_ref, send_ref, token_ref):
    token_ref[...] = jnp.zeros_like(token_ref)
    own_ref[...] = (keep_ref[...].astype(f32) + recv_ref[...].astype(f32)).astype(own_ref.dtype)
    send_ref[...] = (keep_go_ref[...].astype(f32) + recv_go_ref[...].astype(f32)).astype(bf16)


def nothing_kernel(*refs):
    pass


def add_kernel(base_ref, parts_ref, out_ref, token_ref):
    total = base_ref[...]
    for i in range(parts_ref.shape[0]):
        total = total + parts_ref[i].astype(f32)
    out_ref[...] = total
    token_ref[...] = jnp.zeros_like(token_ref)


def spread_kernel(owners, id_ref, keep_ref, recv_ref, *refs):
    outs, token_ref, total = refs[:owners], refs[owners], refs[owners + 1]
    token_ref[...] = jnp.zeros_like(token_ref)
    block = outs[0].shape[0]
    for i in range(owners):
        span = slice(i * block, (i + 1) * block)
        total[i] = keep_ref[0, span, :].astype(f32) + recv_ref[0, span, :].astype(f32)
    for d in range(owners):
        outs[d][...] = total[lax.rem(id_ref[0] + d, owners)].astype(bf16)


def sum_kernel(*refs):
    total = refs[0][...].astype(f32)
    for ref in refs[1:-1]:
        total = total + ref[...].astype(f32)
    refs[-1][...] = total.astype(refs[-1].dtype)


def widen_kernel(in_ref, *refs):
    first_ref, second_ref, token_ref = refs[-3:]
    token_ref[...] = jnp.zeros_like(token_ref)
    count, rows, _ = first_ref.shape
    size = in_ref.shape[1] // count
    for j in range(count):
        first_ref[j] = in_ref[0, j * size : j * size + rows, :].astype(f32)
        second_ref[j] = in_ref[0, j * size + rows : (j + 1) * size, :].astype(f32)


def finish_kernel(owners, id_ref, *refs):
    blocks, outs, ordered = refs[:owners], refs[owners:-1], refs[-1]
    size = blocks[0].shape[0]
    for d in range(owners):
        ordered[lax.rem(id_ref[0] + owners - d, owners)] = blocks[d][...].astype(f32)
    for i in range(owners):
        col = 0
        for out in outs:
            cols = out.shape[1]
            out[i * size : (i + 1) * size, :] = ordered[i, :, col : col + cols]
            col += cols


def dense_backward(parts, owners, local, id_ref, len_ref, *refs):
    part_refs, refs = refs[:parts], refs[parts:]
    (gate_ref, x_ref, cot_ref, res_ref, n1_ref, pack_ref, q_ref, kk_ref, vv_ref, lse_ref, mixed_ref,
     wq_ref, wk_ref, wv_ref, wo_ref, wr_ref, g1_ref, g2_ref,
     gin_ref, keep_one, send_one, keep_two, send_two, gg_all, gmix, gq, gk, gv, acc) = refs
    rows, width = x_ref.shape
    core = id_ref[1]
    pieces = 2 * keep_one.shape[0]
    step = width // pieces

    def put(stream, offset, size):
        keep_ref, send_ref = stream
        for q in range(pieces // 2):
            lo = pl.multiple_of((2 * q + core) * step, step)
            hi = pl.multiple_of((2 * q + 1 - core) * step, step)
            keep_ref[q, :, offset : offset + size] = acc[pl.ds(lo, step), :size].astype(bf16)
            send_ref[q, :, offset : offset + size] = acc[pl.ds(hi, step), :size].astype(bf16)

    def weight_gradient(left, right, stream, offset):
        size = right.shape[1]
        tile = 256
        for t in range(0, size, tile):
            acc[:, t : t + tile] = mm(left[...], right[:, t : t + tile], ((0,), (0,)))
        put(stream, offset, size)

    tail = part_refs[0][rows:, :].astype(f32)
    for part_ref in part_refs[1:]:
        tail = tail + part_ref[rows:, :].astype(f32)
    lines = tail[:owners] + tail[owners : 2 * owners]
    for owner in range(owners):
        for j in range(local):
            gg_all[owner * local + j : owner * local + j + 1, :] = lines[owner : owner + 1, j * rows : (j + 1) * rows]
    gates = gate_ref[...]
    grad_gates = gg_all[...]
    mean = jnp.sum(gates * grad_gates, 0, keepdims=True)
    glog = (gates * (grad_gates - mean)).astype(bf16)
    grad = part_refs[0][:rows, :].astype(f32)
    for part_ref in part_refs[1:]:
        grad = grad + part_ref[:rows, :].astype(f32)
    grad = grad + mm(glog, wr_ref[...], ((0,), (0,)))
    grouter = mm(glog, pack_ref[:rows, :])
    residual = res_ref[...]
    inverse = lax.rsqrt(jnp.mean(residual * residual, -1, keepdims=True) + EPS)
    ggain_two = jnp.sum(grad * residual * inverse, 0, keepdims=True)
    scaled = grad * g2_ref[...]
    gres = cot_ref[...].astype(f32) + inverse * scaled - residual * inverse**3 * jnp.mean(
        scaled * residual, -1, keepdims=True
    )
    branch = gres.astype(bf16)
    gmix[...] = mm(branch, wo_ref[...], ((1,), (1,))).astype(bf16)
    gin_ref[...] = gres
    gq[...] = branch
    one, two = (keep_one, send_one), (keep_two, send_two)
    weight_gradient(mixed_ref, gq, one, 0)
    rest = LANES - 1 - grouter.shape[0]
    acc[:, :LANES] = jnp.concatenate([grouter, ggain_two, jnp.zeros((rest, width), f32)], 0).T
    put(one, width, LANES)
    low = low_lanes(rows)
    allowed = allowed_keys(rows, len_ref[0])
    held = None
    for h in range(KEY_VALUE_HEADS):
        cols = slice(h * PAIR, (h + 1) * PAIR)
        queries = stack_heads(q_ref[:, cols], low)
        upstream = stack_heads(gmix[:, cols], low)
        scores = mm(queries, kk_ref[:, cols], ((1,), (1,))) * SCALE
        logs = jnp.concatenate([lse_ref[:, 2 * h : 2 * h + 1], lse_ref[:, 2 * h + 1 : 2 * h + 2]], 0)
        probs = jnp.exp(jnp.where(allowed, scores, -1e30) - logs)
        gprobs = mm(upstream, vv_ref[:, cols], ((1,), (1,)))
        inner = jnp.sum(gprobs * probs, -1, keepdims=True)
        gscores = (probs * (gprobs - inner)).astype(bf16)
        gqueries = mm(gscores, kk_ref[:, cols]) * SCALE
        gq[:, cols] = jnp.where(low, gqueries[:rows], gqueries[rows:]).astype(bf16)
        gkey = mm(gscores, queries, ((0,), (0,))) * SCALE
        gvalue = mm(probs.astype(bf16), upstream, ((0,), (0,)))
        gkey = gkey + pltpu.roll(gkey, HEAD_DIMENSION, 1)
        gvalue = gvalue + pltpu.roll(gvalue, HEAD_DIMENSION, 1)
        if h % 2 == 0:
            held = (gkey, gvalue)
        else:
            both = slice((h // 2) * PAIR, (h // 2 + 1) * PAIR)
            gk[:, both] = jnp.where(low, held[0], gkey).astype(bf16)
            gv[:, both] = jnp.where(low, held[1], gvalue).astype(bf16)
    col = 0
    for right in (gq, gk, gv):
        weight_gradient(n1_ref, right, two, col)
        col += right.shape[1]
    grad = mm(gq[...], wq_ref[...], ((1,), (1,)))
    grad = grad + mm(gk[...], wk_ref[...], ((1,), (1,)))
    grad = grad + mm(gv[...], wv_ref[...], ((1,), (1,)))
    x = x_ref[...].astype(f32)
    inverse = lax.rsqrt(jnp.mean(x * x, -1, keepdims=True) + EPS)
    ggain_one = jnp.sum(grad * x * inverse, 0, keepdims=True)
    scaled = grad * g1_ref[...]
    gin_ref[...] = gin_ref[...] + inverse * scaled - x * inverse**3 * jnp.mean(
        scaled * x, -1, keepdims=True
    )
    acc[:, :LANES] = jnp.concatenate([ggain_one, jnp.zeros((LANES - 1, width), f32)], 0).T
    put(two, col, LANES)


def on_device(
    inputs, gain_one, query_matrix, key_matrix, value_matrix, w_attn_out, gain_two, w_router,
    expert_in, expert_out, lengths, routes, ranks, cotangent,
):
    seq, width = inputs.shape
    picks = routes.shape[1]
    experts = w_router.shape[1]
    local = expert_in.shape[0]
    half = expert_out.shape[1]
    owners = lax.axis_size("expert")
    groups = lax.axis_size("group")
    steps = groups.bit_length() - 2
    capacity = (5 * seq * picks + 4 * experts - 1) // (4 * experts)
    places = owners * capacity
    z = lax.axis_index("expert").astype(jnp.int32)
    g = lax.axis_index("group").astype(jnp.int32)
    ids = jnp.stack([z, g % 2, g // 2])

    def ring(x, d):
        return lax.ppermute(x, "expert", [(i, (i + d) % owners) for i in range(owners)])

    def swap_cores(x):
        return lax.ppermute(x, "group", [(i, i ^ 1) for i in range(groups)])

    def swap(x, stage):
        return lax.ppermute(
            x, "group", [(i, i ^ (1 << (steps - stage if i % 2 else 1 + stage))) for i in range(groups)]
        )

    def near(x):
        return [ring(x, 1), ring(x, -1)] if owners == 4 else [ring(x, d) for d in range(1, owners)]

    def far(x, got):
        if owners != 4:
            return [x, *got]
        before, after = got
        up = lax.ppermute(before, "expert", [(1, 2), (2, 3)])
        down = lax.ppermute(after, "expert", [(1, 0), (2, 1)])
        return [x, before, jnp.where(z >= 2, up, down), after]

    def halve(keep, recv, stage, name, deps=(), us=4):
        pieces, *rest = keep.shape
        half = pieces // 2
        tile = rest[0] // 2
        core, mine = g % 2, g // 2
        index = jnp.arange(half, dtype=jnp.int32)
        low = (mine >> stage) & 1
        high = (mine >> (steps - 1 - stage)) & 1
        stay = jnp.where(core == 0, 2 * index + low, index + high * half)
        go = jnp.where(core == 0, 2 * index + 1 - low, index + (1 - high) * half)
        block = (1, tile, rest[1])
        here = pl.BlockSpec(block, lambda i, t, which: (which[0, i], t, 0))
        there = pl.BlockSpec(block, lambda i, t, which: (which[1, i], t, 0))
        made = pl.BlockSpec(block, lambda i, t, which: (i, t, 0))
        return call(
            halve_kernel, [((half, *rest), bf16), ((half, *rest), bf16), TOKEN],
            jnp.stack([stay, go]), keep, recv, keep, recv,
            prefetch=1, grid=(half, 2), specs=[here, here, there, there], out_specs=[made, made, VMEM], deps=deps, vmem=16, us=us, name=name,
        )

    def behind(arrays, deps, name):
        shapes = [(a.shape, a.dtype) for a in arrays]
        return call(
            nothing_kernel, shapes, *arrays, specs=[ANY] * len(arrays), out_specs=[ANY] * len(arrays), deps=deps,
            alias={i: i for i in range(len(arrays))}, us=0, name=name,
        )

    cot_got = near(cotangent)
    gain_one = gain_one.reshape(1, width)
    gain_two = gain_two.reshape(1, width)
    router = w_router.T
    extra = -(-3 * experts * seq // width // 16) * 16

    n1, q, kk, vv, lse, mixed, residual, pack, gates = call(
        functools.partial(dense_forward, capacity),
        [((seq, width), bf16)] * 4
        + [((seq, LANES), f32), ((seq, width), bf16), ((seq, width), f32), ((seq + extra, width), bf16), ((experts, seq), f32)],
        lengths, inputs, gain_one, query_matrix, key_matrix, value_matrix, w_attn_out, gain_two, router, routes.T, ranks.T,
        smem=1, us=9, name="dense_forward",
    )
    (pack,) = behind([pack], tuple(cot_got), "tokens_go")
    packs = far(pack, near(pack))
    cot_got = behind(cot_got, (packs[owners // 2],), "cotangents_go")
    cots = far(cotangent, cot_got)
    piece = (width + half) // groups

    def rows_of(n):
        return pl.BlockSpec((1, places, n), lambda i: (i, 0, 0))

    def weights(first):
        return [
            pl.BlockSpec((1, width, 2 * half), lambda i: (first + i, 0, 0)),
            pl.BlockSpec((1, half, width), lambda i: (first + i, 0, 0)),
        ]

    sent, hidden, slope, silu, wret = call(
        functools.partial(expert_forward, local, capacity, owners),
        [
            ((local, places, width), bf16),
            ((local, places, half), bf16),
            ((local, places, half), bf16),
            ((local, places, half), bf16),
            ((local, places, width), bf16),
        ],
        ids, *packs, expert_in, expert_out,
        grid=(local,), specs=[SMEM] + [VMEM] * owners + weights(0),
        out_specs=[rows_of(width), rows_of(half), rows_of(half), rows_of(half), rows_of(width)],
        scratch=[pltpu.VMEM((places, 1), f32)], us=17, name="expert_forward",
    )

    tail = -(-2 * owners // 16) * 16

    def backward(first, count, split, deps=()):
        def of(n):
            return pl.BlockSpec((1, places, n), lambda i: (first + i, 0, 0))

        if split:
            sums = [((groups // 2, count * piece, width), bf16)] * 2
            sum_specs = [pl.BlockSpec((groups // 2, piece, width), lambda i: (0, i, 0))] * 2
        else:
            sums = [((groups, count * piece, width), bf16)]
            sum_specs = [pl.BlockSpec((groups, piece, width), lambda i: (0, i, 0))]
        return call(
            functools.partial(expert_backward, first, split, local, capacity, owners),
            sums + [((count, places, 2 * half), bf16), ((count, owners, seq), f32)],
            ids, *packs, *cots, sent, hidden, slope, silu, expert_in, expert_out,
            grid=(count,),
            specs=[SMEM] + [VMEM] * (2 * owners) + [of(width), of(half), of(half), of(half)] + weights(first),
            out_specs=sum_specs + [rows_of(2 * half), pl.BlockSpec((1, owners, seq), lambda i: (i, 0, 0))],
            scratch=[
                pltpu.VMEM((places, width), bf16),
                pltpu.VMEM((places, 1), f32),
                pltpu.VMEM((places, width), bf16),
            ],
            deps=deps, us=8 * count, name=f"expert_backward{first}",
        )

    def combine(rows, dots, deps, name, us=8):
        outs = [((seq + tail, width), bf16)] * owners if dots else [((owners, seq, width), bf16)]
        return call(
            functools.partial(combine_kernel, local, capacity, owners, (len(rows), len(dots))),
            outs, ids, *packs, *rows, *dots, grid=(owners,),
            specs=[SMEM] + [VMEM] * owners
            + [pl.BlockSpec((r.shape[0], capacity, width), lambda d: (0, d, 0)) for r in rows]
            + [VMEM] * len(dots),
            scratch=[pltpu.VMEM((owners, seq, LANES), jnp.int32)],
            deps=deps, us=us, name=name,
        )

    sums, *grads = backward(0, local, False)
    mine = lax.psum_scatter(sums, "group", scatter_dimension=0, tiled=False)
    parts = call(
        functools.partial(rows_kernel, local, capacity, owners),
        [((seq + tail, width), bf16)] * owners,
        ids, *packs, grads[0], expert_in, grads[1],
        grid=(local,), specs=[SMEM] + [VMEM] * owners + [rows_of(2 * half), weights(0)[0], VMEM],
        scratch=[pltpu.VMEM((local, places, width), bf16)], us=14, name="expert_rows",
    )
    if owners == 4:
        near_by = [
            lax.ppermute(parts[2], "expert", [(2, 1), (3, 2)]),
            lax.ppermute(parts[2], "expert", [(0, 1), (1, 2)]),
        ]
        joined = call(hop_kernel, [(parts[0].shape, bf16)] * 2, parts[1], parts[3], *near_by, us=2, name="hop")
        grad_parts = [parts[0], ring(joined[0], -1), ring(joined[1], 1)]
    else:
        joined = parts
        grad_parts = [parts[0]] + [ring(parts[d], -d) for d in range(1, owners)]
    (owned,) = combine([wret], [], (joined[0],), "combine_out")
    deps = (owned,)

    def to_owners(x):
        return lax.all_to_all(x, "expert", split_axis=0, concat_axis=0, tiled=True)

    sizes = ((width, LANES), (width, key_matrix.shape[1], value_matrix.shape[1], LANES))
    grad_inputs, keep_one, send_one, keep_two, send_two = call(
        functools.partial(dense_backward, len(grad_parts), owners, local),
        [((seq, width), f32)] + [((groups // 2, width // groups, sum(cols)), bf16) for cols in sizes for _ in range(2)],
        ids, lengths, *grad_parts, gates, inputs, cotangent, residual, n1, pack, q, kk, vv, lse, mixed,
        query_matrix, key_matrix, value_matrix, w_attn_out, router, gain_one, gain_two,
        smem=2, deps=deps, us=18, vmem=44, name="dense_backward",
        scratch=[
            pltpu.VMEM((experts, seq), f32),
            pltpu.VMEM((seq, width), bf16),
            pltpu.VMEM((seq, width), bf16),
            pltpu.VMEM((seq, key_matrix.shape[1]), bf16),
            pltpu.VMEM((seq, value_matrix.shape[1]), bf16),
            pltpu.VMEM((width, width), f32),
        ],
    )
    rows = width // groups
    block = rows // owners
    recv_one, recv_two = swap_cores(send_one), swap_cores(send_two)
    (owned,) = behind([owned], (send_one,), "returned_go")
    out_parts = to_owners(owned)
    keep_one, send_one, token = halve(keep_one, recv_one, 0, "one_halve0", (owned,))
    recv_one = swap(send_one, 0)
    keep_two, send_two, token = halve(keep_two, recv_two, 0, "two_halve0", (token,))
    recv_two = swap(send_two, 0)
    (mine,) = behind([mine], (recv_one, token), "gather_go")
    gathered = lax.all_gather(mine, "group", axis=0, tiled=False)
    token = mine
    def spread(keep, recv, name, deps):
        cols = keep.shape[2]
        return call(
            functools.partial(spread_kernel, owners), [((block, cols), bf16)] * owners + [TOKEN], ids, keep, recv,
            smem=1, deps=deps, vmem=16, us=2, name=name, scratch=[pltpu.VMEM((owners, block, cols), f32)],
        )

    def total(blocks, name, deps):
        (made,) = call(sum_kernel, [(blocks[0].shape, bf16)], *blocks, deps=deps, vmem=16, us=2, name=name)
        return [made] + [ring(made, d) for d in range(1, owners)]

    def finish(shares, cols, name, deps):
        return call(
            functools.partial(finish_kernel, owners), [((rows, c), f32) for c in cols],
            ids, *shares, smem=1, deps=deps, vmem=16, us=2, name=name,
            scratch=[pltpu.VMEM((owners, block, sum(cols)), f32)],
        )

    for stage in range(1, steps):
        keep_one, send_one, token = halve(keep_one, recv_one, stage, f"one_halve{stage}", (token,))
        recv_one = swap(send_one, stage)
    *blocks_one, token = spread(keep_one, recv_one, "one_spread", (token,))
    blocks_one = [blocks_one[0]] + [ring(blocks_one[d], d) for d in range(1, owners)]
    for stage in range(1, steps):
        keep_two, send_two, token = halve(keep_two, recv_two, stage, f"two_halve{stage}", (token,))
        recv_two = swap(send_two, stage)
    shares_one = total(blocks_one, "one_sum", (token,))
    *blocks_two, token = spread(keep_two, recv_two, "two_spread", (shares_one[0],))
    blocks_two = [blocks_two[0]] + [ring(blocks_two[d], d) for d in range(1, owners)]
    spec = pl.BlockSpec((seq // 4, width), lambda t: (t, 0))
    output, token = call(
        add_kernel, [((seq, width), f32), TOKEN], residual, out_parts, grid=(4,),
        specs=[spec, pl.BlockSpec((owners, seq // 4, width), lambda t: (0, t, 0))], out_specs=[spec, VMEM],
        deps=(token,), us=4, name="output",
    )
    shares_two = total(blocks_two, "two_sum", (token,))
    *one, small_one = finish(shares_one, sizes[0], "one_finish", (shares_two[0],))
    *two, small_two = finish(shares_two, sizes[1], "two_finish", (small_one,))
    token = small_two
    *full, _ = call(
        widen_kernel,
        [((local, width, 2 * half), f32), ((local, half, width), f32), TOKEN],
        gathered,
        grid=(groups,),
        specs=[pl.BlockSpec((1, local * piece, width), lambda i: (i, 0, 0))],
        out_specs=[
            pl.BlockSpec((local, width // groups, 2 * half), lambda i: (0, i, 0)),
            pl.BlockSpec((local, half // groups, width), lambda i: (0, i, 0)),
            VMEM,
        ],
        deps=(token,), us=12, name="widen",
    )
    return (
        output,
        grad_inputs,
        small_two[:, 0],
        *two,
        *one,
        small_one[:, experts],
        small_one[:, :experts],
        *full,
    )


def solution(mesh):
    tokens = P(("group", "expert"), None)
    experts = P("expert", None, None)
    shares = P("group", None)
    return jax.shard_map(
        on_device,
        mesh=mesh,
        in_specs=(
            tokens, P(), P(), P(), P(), P(), P(), P(), experts, experts,
            P(("group", "expert")), tokens, tokens, tokens,
        ),
        out_specs=(
            tokens, tokens, P("group"), shares, shares, shares, shares, P("group"), shares,
            experts, experts,
        ),
        check_vma=False,
    )
```

```python
import functools

import jax
import jax.numpy as jnp
from jax import lax
from jax.experimental import pallas as pl
from jax.experimental.pallas import tpu as pltpu
from jax.sharding import PartitionSpec as P

QUERY_HEADS = 16
KEY_VALUE_HEADS = 8
HEAD_DIMENSION = 64
PAIR = 2 * HEAD_DIMENSION
EPS = 1e-05
UNROUTED = 1 << 20
LANES = 128
SCALE = HEAD_DIMENSION ** (-0.5)

bf16 = jnp.bfloat16
f32 = jnp.float32
VMEM = pl.BlockSpec(memory_space=pltpu.VMEM)
SMEM = pl.BlockSpec(memory_space=pltpu.SMEM)
ANY = pl.BlockSpec(memory_space=pl.ANY)
HELD = pl.BlockSpec(memory_space=pltpu.HBM)
COST = 3600000
TOKEN = ((8, LANES), f32)


def mm(left, right, dims=((1,), (0,))):
    return lax.dot_general(left, right, (dims, ((), ())), preferred_element_type=f32)


def call(kernel, outs, *args, smem=0, deps=(), specs=None, out_specs=None, grid=None, prefetch=0, scratch=(), vmem=56, alias=None, us=4, name=None):
    outs = [(pltpu.HBM if vmem > 32 else jax.ShapeDtypeStruct)(s, d) for s, d in outs]
    taken = len(args)

    def body(*refs):
        kernel(*refs[:taken], *refs[taken + len(deps) :])

    in_specs = (specs or [SMEM] * smem + [VMEM] * (taken - smem)) + [HELD] * len(deps)
    out_specs = out_specs or [VMEM] * len(outs)
    if prefetch:
        placed = dict(
            grid_spec=pltpu.PrefetchScalarGridSpec(
                num_scalar_prefetch=prefetch, grid=grid, in_specs=in_specs, out_specs=out_specs, scratch_shapes=list(scratch)
            )
        )
    else:
        placed = dict(in_specs=in_specs, out_specs=out_specs, scratch_shapes=list(scratch))
        if grid:
            placed["grid"] = grid
    return pl.pallas_call(
        body,
        out_shape=outs,
        compiler_params=pltpu.CompilerParams(vmem_limit_bytes=vmem * 1024 * 1024),
        cost_estimate=pl.CostEstimate(flops=0, bytes_accessed=us * COST, transcendentals=0),
        input_output_aliases=alias or {},
        name=name,
        **placed,
    )(*args, *deps)


def low_lanes(rows):
    return lax.broadcasted_iota(jnp.int32, (rows, PAIR), 1) < HEAD_DIMENSION


def stack_heads(pair, low):
    pair = pair.astype(f32)
    return jnp.concatenate([jnp.where(low, pair, 0.0), jnp.where(low, 0.0, pair)], 0).astype(bf16)


def allowed_keys(rows, length):
    shape = (2 * rows, rows)
    query = lax.broadcasted_iota(jnp.int32, shape, 0)
    query = jnp.where(query >= rows, query - rows, query)
    key = lax.broadcasted_iota(jnp.int32, shape, 1)
    return (key <= query) & (key < length)


def pack_rows(field, blocks):
    per = field.shape[0] // blocks
    return jnp.concatenate([field[c * per : (c + 1) * per] for c in range(blocks)], 1)


def places_and_ranks(length, routes_ref, ranks_ref, experts, capacity):
    picks, rows = routes_ref.shape
    expert = lax.broadcasted_iota(jnp.int32, (LANES, rows), 0)
    table = jnp.full((LANES, rows), UNROUTED, jnp.int32)
    for k in range(picks):
        table = jnp.where(expert == routes_ref[k : k + 1, :], ranks_ref[k : k + 1, :], table)
    token = lax.broadcasted_iota(jnp.int32, (LANES, rows), 1)
    table = jnp.where(token < length, table, UNROUTED).astype(f32)
    columns = table.T
    places = []
    for e in range(experts):
        row = table[e : e + 1]
        before = jnp.sum(jnp.where(columns[:, e : e + 1] < row, 1.0, 0.0), 0, keepdims=True)
        places.append(jnp.where((row < UNROUTED) & (before < capacity), before, -1.0))
    return jnp.concatenate(places, 0), table[:experts] < UNROUTED


def dense_forward(
    capacity, len_ref, x_ref, g1_ref, wq_ref, wk_ref, wv_ref, wo_ref, g2_ref, wr_ref, routes_ref, ranks_ref,
    n1_ref, q_ref, kk_ref, vv_ref, lse_ref, mixed_ref, res_ref, pack_ref, gate_ref,
):
    rows = x_ref.shape[0]
    x = x_ref[...].astype(f32)
    inverse = lax.rsqrt(jnp.mean(x * x, -1, keepdims=True) + EPS)
    n1 = (x * inverse * g1_ref[...]).astype(bf16)
    n1_ref[...] = n1
    q_ref[...] = mm(n1, wq_ref[...]).astype(bf16)
    low = low_lanes(rows)
    for weight_ref, twice_ref in ((wk_ref, kk_ref), (wv_ref, vv_ref)):
        both = mm(n1, weight_ref[...])
        for j in range(KEY_VALUE_HEADS // 2):
            block = both[:, j * PAIR : (j + 1) * PAIR]
            rolled = pltpu.roll(block, HEAD_DIMENSION, 1)
            twice_ref[:, 2 * j * PAIR : (2 * j + 1) * PAIR] = jnp.where(low, block, rolled).astype(bf16)
            twice_ref[:, (2 * j + 1) * PAIR : (2 * j + 2) * PAIR] = jnp.where(low, rolled, block).astype(bf16)
    allowed = allowed_keys(rows, len_ref[0])
    lane = lax.broadcasted_iota(jnp.int32, (rows, LANES), 1)
    totals = jnp.zeros((rows, LANES), f32)
    for h in range(KEY_VALUE_HEADS):
        cols = slice(h * PAIR, (h + 1) * PAIR)
        scores = mm(stack_heads(q_ref[:, cols], low), kk_ref[:, cols], ((1,), (1,))) * SCALE
        scores = jnp.where(allowed, scores, -1e30)
        top = jnp.max(scores, -1, keepdims=True)
        raised = jnp.exp(scores - top)
        total = jnp.sum(raised, -1, keepdims=True)
        probs = (raised / total).astype(bf16)
        mixed = mm(probs, vv_ref[:, cols])
        mixed_ref[:, cols] = jnp.where(low, mixed[:rows], mixed[rows:]).astype(bf16)
        logs = top + jnp.log(total)
        totals = jnp.where(lane == 2 * h, logs[:rows], totals)
        totals = jnp.where(lane == 2 * h + 1, logs[rows:], totals)
    lse_ref[...] = totals
    residual = x + mm(mixed_ref[...], wo_ref[...])
    res_ref[...] = residual
    inverse = lax.rsqrt(jnp.mean(residual * residual, -1, keepdims=True) + EPS)
    n2 = (residual * inverse * g2_ref[...]).astype(bf16)
    pack_ref[:rows, :] = n2
    logits = mm(wr_ref[...], n2, ((1,), (1,)))
    places, routed = places_and_ranks(len_ref[0], routes_ref, ranks_ref, wr_ref.shape[0], capacity)
    top = jnp.max(jnp.where(routed, logits, -jnp.inf), 0, keepdims=True)
    raised = jnp.where(routed, jnp.exp(jnp.where(routed, logits - top, 0.0)), 0.0)
    total = jnp.sum(raised, 0, keepdims=True)
    gates = raised / jnp.where(total > 0.0, total, 1.0)
    gate_ref[...] = gates
    high = gates.astype(bf16).astype(f32)
    blocks = x_ref.shape[1] // rows
    fields = [pack_rows(field, blocks) for field in (places, high, gates - high)]
    fill = pack_ref.shape[0] - rows - sum(field.shape[0] for field in fields)
    if fill:
        fields.append(jnp.zeros((fill, x_ref.shape[1]), f32))
    pack_ref[rows:, :] = jnp.concatenate(fields, 0).astype(bf16)


def unpack(pack_ref, expert, experts, seq):
    extra, width = pack_ref.shape[0] - seq, pack_ref.shape[1]
    per = experts * seq // width
    at = expert // per
    row = expert - at * per
    block = pack_ref[seq:, pl.ds(pl.multiple_of(at * seq, seq), seq)].astype(f32)
    index = lax.broadcasted_iota(jnp.int32, (extra, seq), 0)
    place = jnp.sum(jnp.where(index == row, block, 0.0), 0, keepdims=True)
    gate = jnp.sum(
        jnp.where((index == per + row) | (index == 2 * per + row), block, 0.0), 0, keepdims=True
    )
    return place, gate


def expert_forward(local, capacity, owners, id_ref, *refs):
    tokens = refs[:owners]
    (win_ref, wout_ref, sent_ref, hidden_ref, slope_ref, silu_ref, wret_ref, weight) = refs[owners:]
    width, half = win_ref.shape[1], wout_ref.shape[1]
    seq = width // local
    expert = id_ref[0] * local + pl.program_id(0)
    place = lax.broadcasted_iota(jnp.int32, (capacity, seq), 0).astype(f32)
    for d in range(owners):
        span = slice(d * capacity, (d + 1) * capacity)
        row, gate = unpack(tokens[d], expert, owners * local, seq)
        hit = place == row
        one = jnp.where(hit, 1.0, 0.0).astype(bf16)
        sent_ref[0, span, :] = mm(one, tokens[d][:seq, :]).astype(bf16)
        weight[span, :] = jnp.sum(jnp.where(hit, gate, 0.0), 1, keepdims=True)
    tile = 256
    for t in range(0, half, tile):
        gate = mm(sent_ref[0], win_ref[0, :, t : t + tile])
        up = mm(sent_ref[0], win_ref[0, :, half + t : half + t + tile])
        sig = jax.nn.sigmoid(gate)
        act = gate * sig
        silu_ref[0, :, t : t + tile] = act.astype(bf16)
        slope_ref[0, :, t : t + tile] = (up * sig * (1.0 + gate * (1.0 - sig))).astype(bf16)
        hidden_ref[0, :, t : t + tile] = (act * up).astype(bf16)
    for t in range(0, width, tile):
        cols = slice(t, t + tile)
        returned = mm(hidden_ref[0], wout_ref[0, :, cols]).astype(bf16).astype(f32)
        wret_ref[0, :, cols] = (weight[...] * returned).astype(bf16)


def expert_backward(first, split, local, capacity, owners, id_ref, *refs):
    tokens, cots = refs[:owners], refs[owners : 2 * owners]
    rest = refs[2 * owners :]
    sent_ref, hidden_ref, slope_ref, silu_ref, win_ref, wout_ref = rest[:6]
    sums, (gpre_ref, gg_ref, crow, weight, gret) = rest[6:-5], rest[-5:]
    gpre = gpre_ref.at[0]
    width, half = win_ref.shape[1], wout_ref.shape[1]
    seq = cots[0].shape[0]
    expert = id_ref[0] * local + first + pl.program_id(0)
    place = lax.broadcasted_iota(jnp.int32, (capacity, seq), 0).astype(f32)
    places = []
    for d in range(owners):
        span = slice(d * capacity, (d + 1) * capacity)
        row, gate = unpack(tokens[d], expert, owners * local, seq)
        places.append(row)
        hit = place == row
        one = jnp.where(hit, 1.0, 0.0).astype(bf16)
        weight[span, :] = jnp.sum(jnp.where(hit, gate, 0.0), 1, keepdims=True)
        rows = mm(one, cots[d][...])
        crow[span, :] = rows.astype(bf16)
        gret[span, :] = (weight[span, :] * rows).astype(bf16)
    tile = 256
    dots = jnp.zeros((owners * capacity, 1), f32)
    for t in range(0, half, tile):
        cols = slice(t, t + tile)
        ghid = mm(crow[...], wout_ref[0, cols, :], ((1,), (1,)))
        dots = dots + jnp.sum(ghid * hidden_ref[0, :, cols].astype(f32), 1, keepdims=True)
        ghid = ghid * weight[...]
        gpre[:, cols] = (ghid * slope_ref[0, :, cols].astype(f32)).astype(bf16)
        gpre[:, half + t : half + t + tile] = (ghid * silu_ref[0, :, cols].astype(f32)).astype(bf16)
    for d in range(owners):
        part = dots[d * capacity : (d + 1) * capacity]
        gg_ref[0, d : d + 1, :] = jnp.sum(jnp.where(place == places[d], part, 0.0), 0, keepdims=True)
    pieces = sums[0].shape[0] * len(sums)
    base = 0
    for left, right in ((sent_ref, gpre), (hidden_ref, gret)):
        size = left.shape[2]
        step = size // pieces
        for t in range(0, width, tile):
            made = mm(left[0], right[:, t : t + tile], ((0,), (0,)))
            for q in range(pieces // len(sums)):
                if split:
                    low = made[2 * q * step : (2 * q + 1) * step]
                    high = made[(2 * q + 1) * step : (2 * q + 2) * step]
                    mine = id_ref[1] == 0
                    sums[0][q, base : base + step, t : t + tile] = jnp.where(mine, low, high).astype(bf16)
                    sums[1][q, base : base + step, t : t + tile] = jnp.where(mine, high, low).astype(bf16)
                else:
                    sums[0][q, base : base + step, t : t + tile] = made[q * step : (q + 1) * step].astype(bf16)
        base += step


def combine_kernel(local, capacity, owners, counts, id_ref, *refs):
    tokens = refs[:owners]
    rest = refs[owners:]
    rows_in = [(r, i) for r in rest[: counts[0]] for i in range(r.shape[0])]
    dots = [(r, i) for r in rest[counts[0] : counts[0] + counts[1]] for i in range(r.shape[0])]
    parts, columns = rest[sum(counts) : -1], rest[-1]
    width = parts[0].shape[-1]
    seq = width // local
    d = pl.program_id(0)

    @pl.when(d == 0)
    def _():
        first = id_ref[0] * local
        for t in range(owners):
            table = [unpack(tokens[t], first + j, owners * local, seq)[0] for j in range(local)]
            table.append(jnp.zeros((LANES - local, seq), f32))
            columns[t] = jnp.concatenate(table, 0).T.astype(jnp.int32)

    lane = lax.broadcasted_iota(jnp.int32, (seq, local * capacity), 1)
    hit = None
    for j in range(local):
        col = columns[d, :, j : j + 1]
        same = lane == jnp.where(col < 0, -1, col + j * capacity)
        hit = same if hit is None else hit | same
    one = jnp.where(hit, 1.0, 0.0).astype(bf16)
    stacked = jnp.concatenate([r[i] for r, i in rows_in], 0)
    made = mm(one, stacked).astype(bf16)
    if dots:
        line = jnp.concatenate([r[i, pl.ds(d, 1), :] for r, i in dots], 1)
        high = line.astype(bf16).astype(f32)
        index = lax.broadcasted_iota(jnp.int32, (parts[0].shape[0] - seq, width), 0)
        mine = jnp.where(index == id_ref[0], high, 0.0)
        mine = jnp.where(index == owners + id_ref[0], line - high, mine)
    if len(parts) == 1:
        parts[0][lax.rem(id_ref[0] + owners - d, owners)] = made
    for t in range(len(parts) if dots else 0):

        @pl.when(d == t)
        def _():
            parts[t][:seq, :] = made
            parts[t][seq:, :] = mine.astype(bf16)


def rows_kernel(local, capacity, owners, id_ref, *refs):
    tokens, (gpre_ref, win_ref, dots_ref), parts, rows = (
        refs[:owners], refs[owners : owners + 3], refs[owners + 3 : -1], refs[-1]
    )
    width = win_ref.shape[1]
    seq = width // local
    step = pl.program_id(0)
    for t in range(0, width, 256):
        rows[step, :, t : t + 256] = mm(gpre_ref[0], win_ref[0, t : t + 256, :], ((1,), (1,))).astype(bf16)

    @pl.when(step == local - 1)
    def _():
        first = id_ref[0] * local
        lane = lax.broadcasted_iota(jnp.int32, (seq, local * capacity), 1)
        index = lax.broadcasted_iota(jnp.int32, (parts[0].shape[0] - seq, width), 0)
        for d in range(owners):
            table = [unpack(tokens[d], first + j, owners * local, seq)[0] for j in range(local)]
            table.append(jnp.zeros((LANES - local, seq), f32))
            columns = jnp.concatenate(table, 0).T.astype(jnp.int32)
            hit = None
            for j in range(local):
                col = columns[:, j : j + 1]
                same = lane == jnp.where(col < 0, -1, col + j * capacity)
                hit = same if hit is None else hit | same
            one = jnp.where(hit, 1.0, 0.0).astype(bf16)
            span = slice(d * capacity, (d + 1) * capacity)
            stacked = jnp.concatenate([rows[j, span, :] for j in range(local)], 0)
            parts[d][:seq, :] = mm(one, stacked).astype(bf16)
            line = jnp.concatenate([dots_ref[j, d : d + 1, :] for j in range(local)], 1)
            high = line.astype(bf16).astype(f32)
            mine = jnp.where(index == id_ref[0], high, 0.0)
            mine = jnp.where(index == owners + id_ref[0], line - high, mine)
            parts[d][seq:, :] = mine.astype(bf16)


def hop_kernel(*refs):
    pairs = len(refs) // 3
    for i in range(pairs):
        total = refs[i][...].astype(f32) + refs[pairs + i][...].astype(f32)
        refs[2 * pairs + i][...] = total.astype(bf16)


def halve_kernel(id_ref, keep_ref, recv_ref, keep_go_ref, recv_go_ref, own_ref, send_ref, token_ref):
    token_ref[...] = jnp.zeros_like(token_ref)
    own_ref[...] = (keep_ref[...].astype(f32) + recv_ref[...].astype(f32)).astype(own_ref.dtype)
    send_ref[...] = (keep_go_ref[...].astype(f32) + recv_go_ref[...].astype(f32)).astype(bf16)


def nothing_kernel(*refs):
    pass


def add_kernel(base_ref, parts_ref, out_ref, token_ref):
    total = base_ref[...]
    for i in range(parts_ref.shape[0]):
        total = total + parts_ref[i].astype(f32)
    out_ref[...] = total
    token_ref[...] = jnp.zeros_like(token_ref)


def spread_kernel(owners, id_ref, keep_ref, recv_ref, *refs):
    outs, token_ref, total = refs[:owners], refs[owners], refs[owners + 1]
    token_ref[...] = jnp.zeros_like(token_ref)
    block = outs[0].shape[0]
    for i in range(owners):
        span = slice(i * block, (i + 1) * block)
        total[i] = keep_ref[0, span, :].astype(f32) + recv_ref[0, span, :].astype(f32)
    for d in range(owners):
        outs[d][...] = total[lax.rem(id_ref[0] + d, owners)].astype(bf16)


def sum_kernel(*refs):
    total = refs[0][...].astype(f32)
    for ref in refs[1:-1]:
        total = total + ref[...].astype(f32)
    refs[-1][...] = total.astype(refs[-1].dtype)


def widen_kernel(in_ref, *refs):
    first_ref, second_ref, token_ref = refs[-3:]
    token_ref[...] = jnp.zeros_like(token_ref)
    count, rows, _ = first_ref.shape
    size = in_ref.shape[1] // count
    for j in range(count):
        first_ref[j] = in_ref[0, j * size : j * size + rows, :].astype(f32)
        second_ref[j] = in_ref[0, j * size + rows : (j + 1) * size, :].astype(f32)


def finish_kernel(owners, id_ref, *refs):
    blocks, outs, ordered = refs[:owners], refs[owners:-1], refs[-1]
    size = blocks[0].shape[0]
    for d in range(owners):
        ordered[lax.rem(id_ref[0] + owners - d, owners)] = blocks[d][...].astype(f32)
    for i in range(owners):
        col = 0
        for out in outs:
            cols = out.shape[1]
            out[i * size : (i + 1) * size, :] = ordered[i, :, col : col + cols]
            col += cols


def dense_backward(parts, owners, local, id_ref, len_ref, *refs):
    part_refs, refs = refs[:parts], refs[parts:]
    (gate_ref, x_ref, cot_ref, res_ref, n1_ref, pack_ref, q_ref, kk_ref, vv_ref, lse_ref, mixed_ref,
     wq_ref, wk_ref, wv_ref, wo_ref, wr_ref, g1_ref, g2_ref,
     gin_ref, keep_one, send_one, keep_two, send_two, gg_all, gmix, gq, gk, gv, acc) = refs
    rows, width = x_ref.shape
    core = id_ref[1]
    pieces = 2 * keep_one.shape[0]
    step = width // pieces

    def put(stream, offset, size):
        keep_ref, send_ref = stream
        for q in range(pieces // 2):
            lo = pl.multiple_of((2 * q + core) * step, step)
            hi = pl.multiple_of((2 * q + 1 - core) * step, step)
            keep_ref[q, :, offset : offset + size] = acc[pl.ds(lo, step), :size].astype(bf16)
            send_ref[q, :, offset : offset + size] = acc[pl.ds(hi, step), :size].astype(bf16)

    def weight_gradient(left, right, stream, offset):
        size = right.shape[1]
        tile = 256
        for t in range(0, size, tile):
            acc[:, t : t + tile] = mm(left[...], right[:, t : t + tile], ((0,), (0,)))
        put(stream, offset, size)

    tail = part_refs[0][rows:, :].astype(f32)
    for part_ref in part_refs[1:]:
        tail = tail + part_ref[rows:, :].astype(f32)
    lines = tail[:owners] + tail[owners : 2 * owners]
    for owner in range(owners):
        for j in range(local):
            gg_all[owner * local + j : owner * local + j + 1, :] = lines[owner : owner + 1, j * rows : (j + 1) * rows]
    gates = gate_ref[...]
    grad_gates = gg_all[...]
    mean = jnp.sum(gates * grad_gates, 0, keepdims=True)
    glog = (gates * (grad_gates - mean)).astype(bf16)
    grad = part_refs[0][:rows, :].astype(f32)
    for part_ref in part_refs[1:]:
        grad = grad + part_ref[:rows, :].astype(f32)
    grad = grad + mm(glog, wr_ref[...], ((0,), (0,)))
    grouter = mm(glog, pack_ref[:rows, :])
    residual = res_ref[...]
    inverse = lax.rsqrt(jnp.mean(residual * residual, -1, keepdims=True) + EPS)
    ggain_two = jnp.sum(grad * residual * inverse, 0, keepdims=True)
    scaled = grad * g2_ref[...]
    gres = cot_ref[...].astype(f32) + inverse * scaled - residual * inverse**3 * jnp.mean(
        scaled * residual, -1, keepdims=True
    )
    branch = gres.astype(bf16)
    gmix[...] = mm(branch, wo_ref[...], ((1,), (1,))).astype(bf16)
    gin_ref[...] = gres
    gq[...] = branch
    one, two = (keep_one, send_one), (keep_two, send_two)
    weight_gradient(mixed_ref, gq, one, 0)
    rest = LANES - 1 - grouter.shape[0]
    acc[:, :LANES] = jnp.concatenate([grouter, ggain_two, jnp.zeros((rest, width), f32)], 0).T
    put(one, width, LANES)
    low = low_lanes(rows)
    allowed = allowed_keys(rows, len_ref[0])
    held = None
    for h in range(KEY_VALUE_HEADS):
        cols = slice(h * PAIR, (h + 1) * PAIR)
        queries = stack_heads(q_ref[:, cols], low)
        upstream = stack_heads(gmix[:, cols], low)
        scores = mm(queries, kk_ref[:, cols], ((1,), (1,))) * SCALE
        logs = jnp.concatenate([lse_ref[:, 2 * h : 2 * h + 1], lse_ref[:, 2 * h + 1 : 2 * h + 2]], 0)
        probs = jnp.exp(jnp.where(allowed, scores, -1e30) - logs)
        gprobs = mm(upstream, vv_ref[:, cols], ((1,), (1,)))
        inner = jnp.sum(gprobs * probs, -1, keepdims=True)
        gscores = (probs * (gprobs - inner)).astype(bf16)
        gqueries = mm(gscores, kk_ref[:, cols]) * SCALE
        gq[:, cols] = jnp.where(low, gqueries[:rows], gqueries[rows:]).astype(bf16)
        gkey = mm(gscores, queries, ((0,), (0,))) * SCALE
        gvalue = mm(probs.astype(bf16), upstream, ((0,), (0,)))
        gkey = gkey + pltpu.roll(gkey, HEAD_DIMENSION, 1)
        gvalue = gvalue + pltpu.roll(gvalue, HEAD_DIMENSION, 1)
        if h % 2 == 0:
            held = (gkey, gvalue)
        else:
            both = slice((h // 2) * PAIR, (h // 2 + 1) * PAIR)
            gk[:, both] = jnp.where(low, held[0], gkey).astype(bf16)
            gv[:, both] = jnp.where(low, held[1], gvalue).astype(bf16)
    col = 0
    for right in (gq, gk, gv):
        weight_gradient(n1_ref, right, two, col)
        col += right.shape[1]
    grad = mm(gq[...], wq_ref[...], ((1,), (1,)))
    grad = grad + mm(gk[...], wk_ref[...], ((1,), (1,)))
    grad = grad + mm(gv[...], wv_ref[...], ((1,), (1,)))
    x = x_ref[...].astype(f32)
    inverse = lax.rsqrt(jnp.mean(x * x, -1, keepdims=True) + EPS)
    ggain_one = jnp.sum(grad * x * inverse, 0, keepdims=True)
    scaled = grad * g1_ref[...]
    gin_ref[...] = gin_ref[...] + inverse * scaled - x * inverse**3 * jnp.mean(
        scaled * x, -1, keepdims=True
    )
    acc[:, :LANES] = jnp.concatenate([ggain_one, jnp.zeros((LANES - 1, width), f32)], 0).T
    put(two, col, LANES)


def on_device(
    inputs, gain_one, query_matrix, key_matrix, value_matrix, w_attn_out, gain_two, w_router,
    expert_in, expert_out, lengths, routes, ranks, cotangent,
):
    seq, width = inputs.shape
    picks = routes.shape[1]
    experts = w_router.shape[1]
    local = expert_in.shape[0]
    half = expert_out.shape[1]
    owners = lax.axis_size("expert")
    groups = lax.axis_size("group")
    steps = groups.bit_length() - 2
    capacity = (5 * seq * picks + 4 * experts - 1) // (4 * experts)
    places = owners * capacity
    z = lax.axis_index("expert").astype(jnp.int32)
    g = lax.axis_index("group").astype(jnp.int32)
    ids = jnp.stack([z, g % 2, g // 2])

    def ring(x, d):
        return lax.ppermute(x, "expert", [(i, (i + d) % owners) for i in range(owners)])

    def swap_cores(x):
        return lax.ppermute(x, "group", [(i, i ^ 1) for i in range(groups)])

    def swap(x, stage):
        return lax.ppermute(
            x, "group", [(i, i ^ (1 << (steps - stage if i % 2 else 1 + stage))) for i in range(groups)]
        )

    def near(x):
        return [ring(x, 1), ring(x, -1)] if owners == 4 else [ring(x, d) for d in range(1, owners)]

    def far(x, got):
        if owners != 4:
            return [x, *got]
        before, after = got
        up = lax.ppermute(before, "expert", [(1, 2), (2, 3)])
        down = lax.ppermute(after, "expert", [(1, 0), (2, 1)])
        return [x, before, jnp.where(z >= 2, up, down), after]

    def halve(keep, recv, stage, name, deps=(), us=4):
        pieces, *rest = keep.shape
        half = pieces // 2
        tile = rest[0] // 2
        core, mine = g % 2, g // 2
        index = jnp.arange(half, dtype=jnp.int32)
        low = (mine >> stage) & 1
        high = (mine >> (steps - 1 - stage)) & 1
        stay = jnp.where(core == 0, 2 * index + low, index + high * half)
        go = jnp.where(core == 0, 2 * index + 1 - low, index + (1 - high) * half)
        block = (1, tile, rest[1])
        here = pl.BlockSpec(block, lambda i, t, which: (which[0, i], t, 0))
        there = pl.BlockSpec(block, lambda i, t, which: (which[1, i], t, 0))
        made = pl.BlockSpec(block, lambda i, t, which: (i, t, 0))
        return call(
            halve_kernel, [((half, *rest), bf16), ((half, *rest), bf16), TOKEN],
            jnp.stack([stay, go]), keep, recv, keep, recv,
            prefetch=1, grid=(half, 2), specs=[here, here, there, there], out_specs=[made, made, VMEM], deps=deps, vmem=16, us=us, name=name,
        )

    def behind(arrays, deps, name):
        shapes = [(a.shape, a.dtype) for a in arrays]
        return call(
            nothing_kernel, shapes, *arrays, specs=[ANY] * len(arrays), out_specs=[ANY] * len(arrays), deps=deps,
            alias={i: i for i in range(len(arrays))}, us=0, name=name,
        )

    cot_got = near(cotangent)
    gain_one = gain_one.reshape(1, width)
    gain_two = gain_two.reshape(1, width)
    router = w_router.T
    extra = -(-3 * experts * seq // width // 16) * 16

    n1, q, kk, vv, lse, mixed, residual, pack, gates = call(
        functools.partial(dense_forward, capacity),
        [((seq, width), bf16)] * 4
        + [((seq, LANES), f32), ((seq, width), bf16), ((seq, width), f32), ((seq + extra, width), bf16), ((experts, seq), f32)],
        lengths, inputs, gain_one, query_matrix, key_matrix, value_matrix, w_attn_out, gain_two, router, routes.T, ranks.T,
        smem=1, us=9, name="dense_forward",
    )
    (pack,) = behind([pack], tuple(cot_got), "tokens_go")
    packs = far(pack, near(pack))
    cot_got = behind(cot_got, (packs[owners // 2],), "cotangents_go")
    cots = far(cotangent, cot_got)
    piece = (width + half) // groups

    def rows_of(n):
        return pl.BlockSpec((1, places, n), lambda i: (i, 0, 0))

    def weights(first):
        return [
            pl.BlockSpec((1, width, 2 * half), lambda i: (first + i, 0, 0)),
            pl.BlockSpec((1, half, width), lambda i: (first + i, 0, 0)),
        ]

    sent, hidden, slope, silu, wret = call(
        functools.partial(expert_forward, local, capacity, owners),
        [
            ((local, places, width), bf16),
            ((local, places, half), bf16),
            ((local, places, half), bf16),
            ((local, places, half), bf16),
            ((local, places, width), bf16),
        ],
        ids, *packs, expert_in, expert_out,
        grid=(local,), specs=[SMEM] + [VMEM] * owners + weights(0),
        out_specs=[rows_of(width), rows_of(half), rows_of(half), rows_of(half), rows_of(width)],
        scratch=[pltpu.VMEM((places, 1), f32)], us=17, name="expert_forward",
    )

    tail = -(-2 * owners // 16) * 16

    def backward(first, count, split, deps=()):
        def of(n):
            return pl.BlockSpec((1, places, n), lambda i: (first + i, 0, 0))

        if split:
            sums = [((groups // 2, count * piece, width), bf16)] * 2
            sum_specs = [pl.BlockSpec((groups // 2, piece, width), lambda i: (0, i, 0))] * 2
        else:
            sums = [((groups, count * piece, width), bf16)]
            sum_specs = [pl.BlockSpec((groups, piece, width), lambda i: (0, i, 0))]
        return call(
            functools.partial(expert_backward, first, split, local, capacity, owners),
            sums + [((count, places, 2 * half), bf16), ((count, owners, seq), f32)],
            ids, *packs, *cots, sent, hidden, slope, silu, expert_in, expert_out,
            grid=(count,),
            specs=[SMEM] + [VMEM] * (2 * owners) + [of(width), of(half), of(half), of(half)] + weights(first),
            out_specs=sum_specs + [rows_of(2 * half), pl.BlockSpec((1, owners, seq), lambda i: (i, 0, 0))],
            scratch=[
                pltpu.VMEM((places, width), bf16),
                pltpu.VMEM((places, 1), f32),
                pltpu.VMEM((places, width), bf16),
            ],
            deps=deps, us=8 * count, name=f"expert_backward{first}",
        )

    def combine(rows, dots, deps, name, us=8):
        outs = [((seq + tail, width), bf16)] * owners if dots else [((owners, seq, width), bf16)]
        return call(
            functools.partial(combine_kernel, local, capacity, owners, (len(rows), len(dots))),
            outs, ids, *packs, *rows, *dots, grid=(owners,),
            specs=[SMEM] + [VMEM] * owners
            + [pl.BlockSpec((r.shape[0], capacity, width), lambda d: (0, d, 0)) for r in rows]
            + [VMEM] * len(dots),
            scratch=[pltpu.VMEM((owners, seq, LANES), jnp.int32)],
            deps=deps, us=us, name=name,
        )

    sums, *grads = backward(0, local, False)
    mine = lax.psum_scatter(sums, "group", scatter_dimension=0, tiled=False)
    parts = call(
        functools.partial(rows_kernel, local, capacity, owners),
        [((seq + tail, width), bf16)] * owners,
        ids, *packs, grads[0], expert_in, grads[1],
        grid=(local,), specs=[SMEM] + [VMEM] * owners + [rows_of(2 * half), weights(0)[0], VMEM],
        scratch=[pltpu.VMEM((local, places, width), bf16)], us=14, name="expert_rows",
    )
    if owners == 4:
        near_by = [
            lax.ppermute(parts[2], "expert", [(2, 1), (3, 2)]),
            lax.ppermute(parts[2], "expert", [(0, 1), (1, 2)]),
        ]
        joined = call(hop_kernel, [(parts[0].shape, bf16)] * 2, parts[1], parts[3], *near_by, us=2, name="hop")
        grad_parts = [parts[0], ring(joined[0], -1), ring(joined[1], 1)]
    else:
        joined = parts
        grad_parts = [parts[0]] + [ring(parts[d], -d) for d in range(1, owners)]
    (owned,) = combine([wret], [], (joined[0],), "combine_out")
    deps = (owned,)

    def to_owners(x):
        return lax.all_to_all(x, "expert", split_axis=0, concat_axis=0, tiled=True)

    sizes = ((width, LANES), (width, key_matrix.shape[1], value_matrix.shape[1], LANES))
    grad_inputs, keep_one, send_one, keep_two, send_two = call(
        functools.partial(dense_backward, len(grad_parts), owners, local),
        [((seq, width), f32)] + [((groups // 2, width // groups, sum(cols)), bf16) for cols in sizes for _ in range(2)],
        ids, lengths, *grad_parts, gates, inputs, cotangent, residual, n1, pack, q, kk, vv, lse, mixed,
        query_matrix, key_matrix, value_matrix, w_attn_out, router, gain_one, gain_two,
        smem=2, deps=deps, us=18, name="dense_backward",
        scratch=[
            pltpu.VMEM((experts, seq), f32),
            pltpu.VMEM((seq, width), bf16),
            pltpu.VMEM((seq, width), bf16),
            pltpu.VMEM((seq, key_matrix.shape[1]), bf16),
            pltpu.VMEM((seq, value_matrix.shape[1]), bf16),
            pltpu.VMEM((width, width), f32),
        ],
    )
    rows = width // groups
    block = rows // owners
    recv_one, recv_two = swap_cores(send_one), swap_cores(send_two)
    (owned,) = behind([owned], (send_one,), "returned_go")
    out_parts = to_owners(owned)
    keep_one, send_one, token = halve(keep_one, recv_one, 0, "one_halve0", (owned,))
    recv_one = swap(send_one, 0)
    keep_two, send_two, token = halve(keep_two, recv_two, 0, "two_halve0", (token,))
    recv_two = swap(send_two, 0)
    (mine,) = behind([mine], (recv_one, token), "gather_go")
    gathered = lax.all_gather(mine, "group", axis=0, tiled=False)
    token = mine
    def spread(keep, recv, name, deps):
        cols = keep.shape[2]
        return call(
            functools.partial(spread_kernel, owners), [((block, cols), bf16)] * owners + [TOKEN], ids, keep, recv,
            smem=1, deps=deps, vmem=16, us=2, name=name, scratch=[pltpu.VMEM((owners, block, cols), f32)],
        )

    def total(blocks, name, deps):
        (made,) = call(sum_kernel, [(blocks[0].shape, bf16)], *blocks, deps=deps, vmem=16, us=2, name=name)
        return [made] + [ring(made, d) for d in range(1, owners)]

    def finish(shares, cols, name, deps):
        return call(
            functools.partial(finish_kernel, owners), [((rows, c), f32) for c in cols],
            ids, *shares, smem=1, deps=deps, vmem=16, us=2, name=name,
            scratch=[pltpu.VMEM((owners, block, sum(cols)), f32)],
        )

    for stage in range(1, steps):
        keep_one, send_one, token = halve(keep_one, recv_one, stage, f"one_halve{stage}", (token,))
        recv_one = swap(send_one, stage)
    *blocks_one, token = spread(keep_one, recv_one, "one_spread", (token,))
    blocks_one = [blocks_one[0]] + [ring(blocks_one[d], d) for d in range(1, owners)]
    for stage in range(1, steps):
        keep_two, send_two, token = halve(keep_two, recv_two, stage, f"two_halve{stage}", (token,))
        recv_two = swap(send_two, stage)
    shares_one = total(blocks_one, "one_sum", (token,))
    *blocks_two, token = spread(keep_two, recv_two, "two_spread", (shares_one[0],))
    blocks_two = [blocks_two[0]] + [ring(blocks_two[d], d) for d in range(1, owners)]
    spec = pl.BlockSpec((seq // 4, width), lambda t: (t, 0))
    output, token = call(
        add_kernel, [((seq, width), f32), TOKEN], residual, out_parts, grid=(4,),
        specs=[spec, pl.BlockSpec((owners, seq // 4, width), lambda t: (0, t, 0))], out_specs=[spec, VMEM],
        deps=(token,), us=4, name="output",
    )
    shares_two = total(blocks_two, "two_sum", (token,))
    *one, small_one = finish(shares_one, sizes[0], "one_finish", (shares_two[0],))
    token = small_one
    *full, token = call(
        widen_kernel,
        [((local, width, 2 * half), f32), ((local, half, width), f32), TOKEN],
        gathered,
        grid=(groups,),
        specs=[pl.BlockSpec((1, local * piece, width), lambda i: (i, 0, 0))],
        out_specs=[
            pl.BlockSpec((local, width // groups, 2 * half), lambda i: (0, i, 0)),
            pl.BlockSpec((local, half // groups, width), lambda i: (0, i, 0)),
            VMEM,
        ],
        deps=(token,), us=12, name="widen",
    )
    *two, small_two = finish(shares_two, sizes[1], "two_finish", (token,))
    return (
        output,
        grad_inputs,
        small_two[:, 0],
        *two,
        *one,
        small_one[:, experts],
        small_one[:, :experts],
        *full,
    )


def solution(mesh):
    tokens = P(("group", "expert"), None)
    experts = P("expert", None, None)
    shares = P("group", None)
    return jax.shard_map(
        on_device,
        mesh=mesh,
        in_specs=(
            tokens, P(), P(), P(), P(), P(), P(), P(), experts, experts,
            P(("group", "expert")), tokens, tokens, tokens,
        ),
        out_specs=(
            tokens, tokens, P("group"), shares, shares, shares, shares, P("group"), shares,
            experts, experts,
        ),
        check_vma=False,
    )
```
